32 devices in a mesh: dp: 16 (over z, y, core), tp: 2 (over x).
Axes of the slice: x: 2, y: 2, z: 4, core: 2. Of those that a mesh axis runs over, the one named last changes fastest.
Arguments:
- tokens: bfloat16 [32768, 512], P(('dp', 'tp')), may hold values from -1.6953125 to 1.6953125
- long_docs: int32 [16], P('dp'), may hold values from 0 to 1, as said below
- w_qkv: bfloat16 [3, 512, 512], P(None, None, 'tp'), may hold values from -0.25 to 0.25
- bias_qv: bfloat16 [2, 512], P(None, 'tp'), may hold values from -0.796875 to 0.796875
- w_out: bfloat16 [512, 512], P('tp'), may hold values from -2 to 2
- bias_out: bfloat16 [512], replicated, may hold values from -0.796875 to 0.796875
- w_up: bfloat16 [512, 2048], P(None, 'tp'), may hold values from -0.25 to 0.25
- bias_up: bfloat16 [2048], P('tp'), may hold values from -0.796875 to 0.796875
- w_down: bfloat16 [2048, 512], P('tp'), may hold values from -0.125 to 0.125
- bias_down: bfloat16 [512], replicated, may hold values from -0.796875 to 0.796875
- alphas: float32 [2], replicated, may hold values from 0.5 to 1.5
- cotangent: bfloat16 [32768, 512], P(('dp', 'tp')), may hold values from -1.6953125 to 1.6953125
Outputs:
- out: bfloat16 [32768, 512], P(('dp', 'tp'))
- grad_tokens: bfloat16 [32768, 512], P(('dp', 'tp'))
- grad_w_qkv: float32 [3, 512, 512], P(None, None, 'tp')
- grad_bias_qv: float32 [2, 512], P(None, 'tp')
- grad_w_out: float32 [512, 512], P('tp')
- grad_bias_out: float32 [512], replicated
- grad_w_up: float32 [512, 2048], P(None, 'tp')
- grad_bias_up: float32 [2048], P('tp')
- grad_w_down: float32 [2048, 512], P('tp')
- grad_bias_down: float32 [512], replicated
- grad_alphas: float32 [2], replicated
The draws below stay inside these ranges and needn't reach their ends.
Inputs may be any that keep to these rules, and one draw needn't show every extreme that they name: Pack g holds long_docs[g] sequences of 2048 tokens first, then short ones of 1024; some pack has none and some has 1.
All inputs are finite; a program needn't handle non-finite values.
Results may differ from the reference program's by a relative error of at most 0.014.
Values may be sent and summed in bfloat16 or wider, within the bound.
No kernel may reach another device: no remote copies, remote signals or barrier semaphores. Data moves between devices by JAX's collectives and lax.ppermute only.
A program may use at most 192 MiB of HBM per device.

```python
import jax
import jax.numpy as jnp
from jax import lax

D = 512
HEADS = 8
HEAD_DIM = 64
FF = 2048
SHORT = 1024
SLOTS = 2
TOKENS = 32768
N_DP = 16


def draw_long_docs(key, part):
    key = jax.random.fold_in(key, 7)
    count_key, order_key = jax.random.split(key)
    counts = jax.random.randint(count_key, (N_DP,), 0, SLOTS // 2 + 1)
    order = jax.random.permutation(order_key, N_DP)
    counts = counts.at[order[0]].set(SLOTS // 2)
    counts = counts.at[order[1]].set(0)
    return counts.astype(jnp.int32)


def block_scale(rng, extent, cuts, least, top_value):
    def one(dim, blocks):
        draws = jax.random.uniform(jax.random.fold_in(jax.random.fold_in(rng, 6), dim), (blocks,), jnp.float32, least / len(cuts), top_value / len(cuts))
        return jnp.repeat(jnp.exp(draws), extent[dim] // blocks).reshape((-1,) + (1,) * (len(extent) - dim - 1))

    factor_of = one(*cuts[0])
    for cut in cuts[1:]:
        factor_of = factor_of * one(*cut)
    return factor_of


def gaussian(own_key, shape, spread, reach, cuts=(), held_as=jnp.bfloat16):
    entries = spread * jax.random.normal(own_key, shape, jnp.float32)
    if cuts:
        entries = entries * block_scale(own_key, shape, cuts, -0.22, 0.18)
    return jnp.clip(entries, -reach, reach).astype(held_as)


def setup_inputs(seed: int = 0) -> dict:
    splits = jax.random.split(jax.random.key(seed), 13)
    tokens = jnp.clip(jax.random.uniform(splits[0], (TOKENS, D), jnp.float32, -1.6953125, 1.6953125) * block_scale(splits[0], (TOKENS, D), ((0, 32),), -0.4, 0.0), -1.6953125, 1.6953125).astype(jnp.bfloat16)
    long_docs = draw_long_docs(jax.random.fold_in(splits[12], 71), 0)
    w_qkv = gaussian(splits[2], (3, D, D), D ** -0.5, 0.25, ((2, 2),))
    bias_qv = jnp.clip(jax.random.uniform(splits[3], (2, D), jnp.float32, -0.796875, 0.796875) * block_scale(splits[3], (2, D), ((1, 2),), -0.4, 0.0), -0.796875, 0.796875).astype(jnp.bfloat16)
    w_out = gaussian(splits[4], (D, D), (D // 64) ** -0.5, 2.0, ((0, 2),))
    bias_out = jnp.clip(jax.random.uniform(splits[5], (D,), jnp.float32, -0.796875, 0.796875), -0.796875, 0.796875).astype(jnp.bfloat16)
    w_up = gaussian(splits[6], (D, FF), D ** -0.5, 0.25, ((1, 2),))
    bias_up = jnp.clip(jax.random.uniform(splits[7], (FF,), jnp.float32, -0.796875, 0.796875) * block_scale(splits[7], (FF,), ((0, 2),), -0.4, 0.0), -0.796875, 0.796875).astype(jnp.bfloat16)
    w_down = gaussian(splits[8], (FF, D), FF ** -0.5, 0.125, ((0, 2),))
    bias_down = jnp.clip(jax.random.uniform(splits[9], (D,), jnp.float32, -0.796875, 0.796875), -0.796875, 0.796875).astype(jnp.bfloat16)
    alphas = jnp.clip(jax.random.uniform(splits[10], (2,), jnp.float32, 0.5, 1.5), 0.5, 1.5)
    cotangent = jnp.clip(jax.random.uniform(splits[11], (TOKENS, D), jnp.float32, -1.6953125, 1.6953125) * block_scale(splits[11], (TOKENS, D), ((0, 32),), -0.4, 0.0), -1.6953125, 1.6953125).astype(jnp.bfloat16)
    return dict(tokens=tokens, long_docs=long_docs, w_qkv=w_qkv, bias_qv=bias_qv, w_out=w_out, bias_out=bias_out, w_up=w_up, bias_up=bias_up, w_down=w_down, bias_down=bias_down, alphas=alphas, cotangent=cotangent)


@jax.custom_vjp
def low(v):
    return lax.optimization_barrier(v.astype(jnp.bfloat16)).astype(jnp.float32)

@jax.custom_vjp
def low_back(v):
    return v

def low_keep(v):
    return (low(v), None)

def low_pass(kept, grad):
    return (grad,)

def back_keep(v):
    return (v, None)

def back_low(kept, grad):
    return (low(grad),)
low.defvjp(low_keep, low_pass)
low_back.defvjp(back_keep, back_low)

def doc_numbers(total, longs):
    places = jnp.arange(total, dtype=jnp.int32)
    border = 2 * SHORT * longs
    return jnp.where(places < border, places // (2 * SHORT), longs + (places - border) // SHORT)

def pack_layer(inputs, w_qkv, bias_qv, w_out, bias_out, w_up, bias_up, w_down, bias_down, alphas, longs):
    highest = lax.Precision.HIGHEST
    total = inputs.shape[0]
    projected = jnp.einsum('td,cdf->ctf', inputs, w_qkv, precision=highest)
    query_all = low_back(low(projected[0] + bias_qv[0])).reshape(total, HEADS, HEAD_DIM)
    key_all = low_back(low(projected[1])).reshape(total, HEADS, HEAD_DIM)
    value_all = low_back(low(projected[2] + bias_qv[1])).reshape(total, HEADS, HEAD_DIM)
    docs = doc_numbers(total, longs)
    block = min(512, SHORT)
    window = 2 * SHORT // block
    span = window * block

    def one_block(index):
        query_start = (index * block).astype(jnp.int32)
        key_start = (jnp.maximum(index - window + 1, 0) * block).astype(jnp.int32)
        query_rows = lax.dynamic_slice_in_dim(query_all, query_start, block, 0)
        key_rows = lax.dynamic_slice_in_dim(key_all, key_start, span, 0)
        value_rows = lax.dynamic_slice_in_dim(value_all, key_start, span, 0)
        query_docs = lax.dynamic_slice_in_dim(docs, query_start, block, 0)
        key_docs = lax.dynamic_slice_in_dim(docs, key_start, span, 0)
        query_place = query_start + jnp.arange(block, dtype=jnp.int32)
        key_place = key_start + jnp.arange(span, dtype=jnp.int32)
        allowed = (key_docs[None, :] == query_docs[:, None]) & (key_place[None, :] <= query_place[:, None])
        logits = low_back(jnp.einsum('qhe,khe->hqk', query_rows, key_rows, precision=highest) * HEAD_DIM ** (-0.5))
        logits = jnp.where(allowed[None], logits, -1e+30)
        peak = lax.optimization_barrier(jnp.max(logits, axis=-1, keepdims=True))
        expo = jnp.exp(logits - peak)
        probs = expo / lax.optimization_barrier(jnp.sum(expo, axis=-1, keepdims=True))
        return jnp.einsum('hqk,khe->qhe', low(probs), value_rows, precision=highest)
    blocks_out = lax.map(jax.checkpoint(one_block), jnp.arange(total // block, dtype=jnp.int32))
    mixed = low_back(low(blocks_out.reshape(total, D)))
    branch = low_back(jnp.dot(mixed, w_out, precision=highest))
    resid = inputs + alphas[0] * (branch + bias_out)
    pre_act = low_back(jnp.dot(low(resid), w_up, precision=highest) + bias_up)
    act = low(jax.nn.gelu(pre_act))
    ffn = low_back(jnp.dot(act, w_down, precision=highest))
    return resid + alphas[1] * (ffn + bias_down)

def reference(tokens, long_docs, w_qkv, bias_qv, w_out, bias_out, w_up, bias_up, w_down, bias_down, alphas, cotangent):
    params = tuple((p.astype(jnp.float32) for p in (w_qkv, bias_qv, w_out, bias_out, w_up, bias_up, w_down, bias_down, alphas)))
    group = SLOTS * SHORT
    packs = tokens.astype(jnp.float32).reshape(N_DP, group, D)
    cot_packs = cotangent.astype(jnp.float32).reshape(N_DP, group, D)

    def per_pack(carry, item):
        inputs, cot_rows, longs = item

        def layer(values, *weights):
            return pack_layer(values, *weights, longs)
        result, pull = jax.vjp(layer, inputs, *params)
        grads = pull(cot_rows)
        carry = tuple((acc + grad for acc, grad in zip(carry, grads[1:])))
        return (carry, (result.astype(jnp.bfloat16), grads[0].astype(jnp.bfloat16)))
    start = tuple((jnp.zeros_like(p) for p in params))
    sums, (outputs, grad_inputs) = lax.scan(per_pack, start, (packs, cot_packs, long_docs))
    return (outputs.reshape(N_DP * group, D), grad_inputs.reshape(N_DP * group, D), sums[0], sums[1], sums[2], sums[3], sums[4], sums[5], sums[6], sums[7], sums[8])
```

```python
import functools

import jax
import jax.numpy as jnp
from jax import lax
from jax.experimental import pallas as pl
from jax.experimental.pallas import tpu as pltpu
from jax.sharding import PartitionSpec as P

HEAD_DIM = 64
SHORT = 1024
LOG2E = 1.4426950408889634
F32 = jnp.float32
BF16 = jnp.bfloat16
NT = (((1,), (1,)), ((), ()))
TN = (((0,), (0,)), ((), ()))
AXES = ("dp", "tp")
GRANT = 60 << 20
BIG = 1e30


def dot(left, right, dims=None):
    if dims is None:
        return jnp.dot(left, right, preferred_element_type=F32)
    return lax.dot_general(left, right, dims, preferred_element_type=F32)


def in_vmem():
    return pl.BlockSpec(memory_space=pltpu.VMEM)


def in_smem():
    return pl.BlockSpec(memory_space=pltpu.SMEM)


def lower_half(which, rows):
    zeros = jnp.zeros_like(rows)
    return jnp.where(
        which == 0, jnp.concatenate([rows, zeros], 0), jnp.concatenate([zeros, rows], 0)
    )


def attend_kernel(
    flags, mine_ref, other_ref, w_ref, bcol_ref, brow_ref,
    q_t_ref, k_t_ref, k_ref, v_ref, keep_ref, send_ref, lse_ref,
    v_t, mixed, scores, *, block,
):
    core, longs = flags[0], flags[2]
    half = mine_ref.shape[0]
    total = 2 * half
    width = w_ref.shape[2]
    pairs = width // 128
    heads = width // HEAD_DIM
    wq_t, wk_t, wv_t = (w_ref[i].T for i in range(3))

    def project(rows_ref, which):
        at = pl.ds(pl.multiple_of(which * half, half), half)
        rows = rows_ref[...]
        q_t_ref[:, at] = (dot(wq_t, rows, NT) + bcol_ref[0]).astype(BF16)
        k_t_ref[:, at] = dot(wk_t, rows, NT).astype(BF16)
        v_t[:, at] = (dot(wv_t, rows, NT) + bcol_ref[1]).astype(BF16)
        for pair in range(pairs):
            cols = slice(pair * 128, pair * 128 + 128)
            k_ref[pair, at, :] = dot(rows, w_ref[1, :, cols]).astype(BF16)
            v_ref[pair, at, :] = (dot(rows, w_ref[2, :, cols]) + brow_ref[0:1, cols]).astype(BF16)

    project(mine_ref, core)
    project(other_ref, 1 - core)
    row = lax.broadcasted_iota(jnp.int32, (block, block), 0)
    col = lax.broadcasted_iota(jnp.int32, (block, block), 1)
    scale = HEAD_DIM ** (-0.5) * LOG2E

    def one_head(head, _):
        at = pl.ds(pl.multiple_of(head * HEAD_DIM, HEAD_DIM), HEAD_DIM)
        pair, which = head // 2, head % 2
        for q0 in range(0, total, block):
            queries = lower_half(which, q_t_ref[at, q0 : q0 + block])
            peak = jnp.full((8, block), -BIG, F32)
            for k0 in range(0, q0 + block, block):
                s = dot(k_ref[pair, k0 : k0 + block, :], queries)
                if k0 == q0:
                    s = jnp.where(row <= col, s, -BIG)
                scores[k0 : k0 + block, :] = s
                top = jnp.max(s.reshape(block // 8, 8, block), 0)
                if q0 >= SHORT > k0:
                    top = jnp.where(longs > 0, top, -BIG)
                peak = jnp.maximum(peak, top)
            peak = jnp.max(peak, 0, keepdims=True) * scale
            acc = jnp.zeros((HEAD_DIM, block), F32)
            norm = jnp.zeros((8, block), F32)
            for k0 in range(0, q0 + block, block):
                base = peak
                if q0 >= SHORT > k0:
                    base = jnp.where(longs > 0, peak, BIG)
                e = jnp.exp2(scores[k0 : k0 + block, :] * scale - base)
                norm = norm + jnp.sum(e.reshape(block // 8, 8, block), 0)
                acc = acc + dot(v_t[at, k0 : k0 + block], e.astype(BF16))
            norm = jnp.sum(norm, 0, keepdims=True)
            mixed[q0 // half, at, q0 % half : q0 % half + block] = (acc / norm).astype(BF16)
            lse_ref[head, :, q0 : q0 + block] = jnp.broadcast_to(
                peak + jnp.log2(norm), (8, block)
            )
        return 0

    lax.fori_loop(0, heads, one_head, 0)
    keep_ref[...] = mixed[core]
    send_ref[...] = mixed[1 - core]


def attend(flags, mine, other, w, bcol, brow):
    half = mine.shape[0]
    total, width = 2 * half, w.shape[2]
    shape = jax.ShapeDtypeStruct
    block = 512
    return pl.pallas_call(
        functools.partial(attend_kernel, block=block),
        out_shape=(
            shape((width, total), BF16),
            shape((width, total), BF16),
            shape((width // 128, total, 128), BF16),
            shape((width // 128, total, 128), BF16),
            shape((width, half), BF16),
            shape((width, half), BF16),
            shape((width // HEAD_DIM, 8, total), F32),
        ),
        in_specs=[in_smem()] + [in_vmem()] * 5,
        out_specs=(in_vmem(),) * 7,
        scratch_shapes=[
            pltpu.VMEM((width, total), BF16),
            pltpu.VMEM((2, width, half), BF16),
            pltpu.VMEM((total, block), F32),
        ],
        compiler_params=pltpu.CompilerParams(vmem_limit_bytes=GRANT),
        cost_estimate=pl.CostEstimate(
            flops=20_000_000_000, bytes_accessed=10_000_000, transcendentals=0
        ),
    )(flags, mine, other, w, bcol, brow)


def feed_kernel(
    flags, alphas, tok_ref, cot_ref, keep_ref, recv_ref, up_ref, down_ref, wout_ref, near_ref,
    far_ref, bup_ref, bout_ref, bdown_ref,
    out_ref, dresid_ref, dkeep_ref, dsend_ref, gkeep_ref, gsend_ref, small_ref,
    mixed, dmixed, attn, resid, ffn, act, dpre, *, piece,
):
    core, place = flags[0], flags[1]
    same = flags[3]
    rows, width = tok_ref.shape
    unit = up_ref.shape[1] // 2
    part = wout_ref.shape[0] // 2
    a_attn, a_ffn = alphas[0], alphas[1]
    mixed[1 - same] = keep_ref[...]
    mixed[same] = recv_ref[...]

    def own_sub(j):
        return core if j == 0 else 1 - core

    def wout_part(h, j):
        if h == 0:
            return wout_ref[pl.ds(pl.multiple_of(own_sub(j) * part, part), part), :]
        return (near_ref, far_ref)[j][2 * unit : 2 * unit + part, :]

    def mixed_part(h, j):
        return mixed[h, pl.ds(pl.multiple_of(own_sub(j) * part, part), part), :]

    total = dot(mixed_part(0, 0), wout_part(0, 0), TN)
    for h, j in ((0, 1), (1, 0), (1, 1)):
        total = total + dot(mixed_part(h, j), wout_part(h, j), TN)
    attn[...] = total + bout_ref[...]
    resid[...] = tok_ref[...].astype(F32) + a_attn * attn[...]
    low = resid[...].astype(BF16)
    low_t = low.T
    dffn = (cot_ref[...].astype(F32) * a_ffn).astype(BF16)
    dffn_t = dffn.T
    dresid_ref[...] = cot_ref[...].astype(F32)
    ffn[...] = jnp.broadcast_to(bdown_ref[...], ffn.shape)
    for h in range(2):
        for j in range(2):
            sub = pl.ds(pl.multiple_of(own_sub(j) * unit, unit), unit)
            if h == 0:
                up, down = up_ref[:, sub], down_ref[sub, :]
            else:
                source = (near_ref, far_ref)[j]
                up, down = source[:unit, :], source[unit : 2 * unit, :]
            bias = bup_ref[h, :, sub]
            bias_grad = jnp.zeros((8, unit), F32)
            for r0 in range(0, rows, piece):
                at = slice(r0, r0 + piece)
                u = dot(low[at], up) + bias
                square = u * u
                t = jnp.tanh(u * (0.7978845608028654 + 0.035677408136300125 * square))
                s = 0.5 + 0.5 * t
                slope = s + (0.5 * u) * (1.0 - t * t) * (
                    0.7978845608028654 + 0.10703222440890037 * square
                )
                act[at, :] = (u * s).astype(BF16)
                d = dot(dffn[at], down, NT) * slope
                d_low = d.astype(BF16)
                dpre[at, :] = d_low
                bias_grad = bias_grad + jnp.sum(
                    d_low.astype(F32).reshape(piece // 8, 8, unit), 0
                )
                ffn[at, :] += dot(act[at, :], down)
                dresid_ref[at, :] += dot(d_low, up, NT)
            target = (gkeep_ref, gsend_ref)[j]
            target[h, :unit, :] = dot(low_t, dpre[...]).astype(BF16)
            target[h, unit : 2 * unit, :] = dot(dffn_t, act[...]).T.astype(BF16)
            half_index = place if h == 0 else 1 - place
            small_ref[pl.ds(4 + 2 * half_index + own_sub(j), 1), :] = jnp.sum(
                bias_grad, 0, keepdims=True
            )
    g = cot_ref[...].astype(F32)
    out_ref[...] = (resid[...] + a_ffn * ffn[...]).astype(BF16)
    small_ref[0:1, :] = a_ffn * jnp.sum(g, 0, keepdims=True)
    dresid = dresid_ref[...]
    small_ref[1:2, :] = a_attn * jnp.sum(dresid, 0, keepdims=True)
    small_ref[2:3, :] = jnp.sum(dresid * attn[...], 0, keepdims=True)
    small_ref[3:4, :] = jnp.sum(g * ffn[...], 0, keepdims=True)
    dattn = (a_attn * dresid).astype(BF16)
    for h in range(2):
        for j in range(2):
            (gkeep_ref, gsend_ref)[j][h, 2 * unit : 2 * unit + part, :] = dot(
                mixed_part(h, j), dattn
            ).astype(BF16)
            dmixed[h, pl.ds(pl.multiple_of(own_sub(j) * part, part), part), :] = dot(
                wout_part(h, j), dattn, NT
            ).astype(BF16)
    dkeep_ref[...] = dmixed[1 - same]
    dsend_ref[...] = dmixed[same]


def feed(flags, alphas, tok, cot, keep, recv, up, down, wout, near, far, bup, bout, bdown):
    rows, width = tok.shape
    unit = up.shape[1] // 2
    half_width = keep.shape[0]
    shape = jax.ShapeDtypeStruct
    return pl.pallas_call(
        functools.partial(feed_kernel, piece=256),
        out_shape=(
            shape((rows, width), BF16),
            shape((rows, width), F32),
            shape((half_width, rows), BF16),
            shape((half_width, rows), BF16),
            shape((2,) + near.shape, BF16),
            shape((2,) + near.shape, BF16),
            shape((8, width), F32),
        ),
        in_specs=[in_smem()] * 2 + [in_vmem()] * 12,
        out_specs=(in_vmem(),) * 7,
        scratch_shapes=[
            pltpu.VMEM((2, half_width, rows), BF16),
            pltpu.VMEM((2, half_width, rows), BF16),
            pltpu.VMEM((rows, width), F32),
            pltpu.VMEM((rows, width), F32),
            pltpu.VMEM((rows, width), F32),
            pltpu.VMEM((rows, unit), BF16),
            pltpu.VMEM((rows, unit), BF16),
        ],
        compiler_params=pltpu.CompilerParams(vmem_limit_bytes=GRANT),
        cost_estimate=pl.CostEstimate(
            flops=20_000_000_000, bytes_accessed=20_000_000, transcendentals=0
        ),
    )(flags, alphas, tok, cot, keep, recv, up, down, wout, near, far, bup, bout, bdown)


def attend_back_kernel(
    flags, mine_ref, other_ref, w_ref, q_t_ref, k_t_ref, k_ref, v_ref, keep_ref, send_ref,
    dkeep_ref, drecv_ref, lse_ref, dresid_ref,
    grad_ref, bias_ref, own_ref, away_ref,
    rows_all, mixed, dmixed, grads, dk_sum, dv_sum, *, block,
):
    core, longs = flags[0], flags[2]
    half, width_all = mine_ref.shape
    total = 2 * half
    width = w_ref.shape[2]
    heads = width // HEAD_DIM
    rows_all[core] = mine_ref[...]
    rows_all[1 - core] = other_ref[...]
    mixed[core] = keep_ref[...]
    mixed[1 - core] = send_ref[...]
    dmixed[core] = dkeep_ref[...]
    dmixed[1 - core] = drecv_ref[...]
    row = lax.broadcasted_iota(jnp.int32, (block, block), 0)
    col = lax.broadcasted_iota(jnp.int32, (block, block), 1)
    factor = HEAD_DIM ** (-0.5)
    scale = factor * LOG2E

    def one_head(head, _):
        at = pl.ds(pl.multiple_of(head * HEAD_DIM, HEAD_DIM), HEAD_DIM)
        pair, which = head // 2, head % 2
        dk_sum[...] = jnp.zeros_like(dk_sum)
        dv_sum[...] = jnp.zeros_like(dv_sum)
        for q0 in range(0, total, block):
            here = slice(q0 % half, q0 % half + block)
            q = q_t_ref[at, q0 : q0 + block]
            do = dmixed[q0 // half, at, here]
            queries, upstream = lower_half(which, q), lower_half(which, do)
            lse = lse_ref[head, 0:1, q0 : q0 + block]
            mean = jnp.sum(
                do.astype(F32) * mixed[q0 // half, at, here].astype(F32), 0, keepdims=True
            )
            acc = jnp.zeros((HEAD_DIM, block), F32)
            for k0 in range(0, q0 + block, block):
                keys = slice(k0, k0 + block)
                base = lse
                if q0 >= SHORT > k0:
                    base = jnp.where(longs > 0, lse, BIG)
                s = dot(k_ref[pair, keys, :], queries)
                dp = dot(v_ref[pair, keys, :], upstream)
                p = jnp.exp2(s * scale - base)
                if k0 == q0:
                    p = jnp.where(row <= col, p, 0.0)
                ds = (p * (dp - mean)).astype(BF16)
                acc = acc + dot(k_t_ref[at, keys], ds)
                dk_sum[:, keys] += dot(q, ds, NT)
                dv_sum[:, keys] += dot(do, p.astype(BF16), NT)
            grads[0, at, q0 : q0 + block] = (acc * factor).astype(BF16)
        grads[1, at, :] = (dk_sum[...] * factor).astype(BF16)
        grads[2, at, :] = dv_sum[...].astype(BF16)
        return 0

    lax.fori_loop(0, heads, one_head, 0)
    for i in range(3):
        grad_ref[i * width : (i + 1) * width, :] = (
            dot(grads[i, :, :half], rows_all[0]) + dot(grads[i, :, half:], rows_all[1])
        ).astype(BF16)
    ones = jnp.ones((8, total), BF16)
    bias_ref[...] = jnp.concatenate(
        [dot(ones, grads[0], NT)[0:4], dot(ones, grads[2], NT)[0:4]], 0
    )

    def back(which):
        at = pl.ds(pl.multiple_of(which * half, half), half)
        result = dot(w_ref[0], grads[0, :, at])
        for i in (1, 2):
            result = result + dot(w_ref[i], grads[i, :, at])
        return result.T

    away_ref[...] = back(1 - core).astype(BF16)
    own_ref[...] = dresid_ref[...] + back(core)


def attend_back(flags, mine, other, w, q_t, k_t, k, v, keep, send, dkeep, drecv, lse, dresid):
    half, width_all = mine.shape
    total, width = 2 * half, w.shape[2]
    shape = jax.ShapeDtypeStruct
    block = 512
    return pl.pallas_call(
        functools.partial(attend_back_kernel, block=block),
        out_shape=(
            shape((3 * width, width_all), BF16),
            shape((8, width), F32),
            shape((half, width_all), F32),
            shape((half, width_all), BF16),
        ),
        in_specs=[in_smem()] + [in_vmem()] * 13,
        out_specs=(in_vmem(),) * 4,
        scratch_shapes=[
            pltpu.VMEM((2, half, width_all), BF16),
            pltpu.VMEM((2, width, half), BF16),
            pltpu.VMEM((2, width, half), BF16),
            pltpu.VMEM((3, width, total), BF16),
            pltpu.VMEM((HEAD_DIM, total), F32),
            pltpu.VMEM((HEAD_DIM, total), F32),
        ],
        compiler_params=pltpu.CompilerParams(vmem_limit_bytes=GRANT),
        cost_estimate=pl.CostEstimate(
            flops=40_000_000_000, bytes_accessed=20_000_000, transcendentals=0
        ),
    )(flags, mine, other, w, q_t, k_t, k, v, keep, send, dkeep, drecv, lse, dresid)


def add_low(left, right):
    return (left.astype(F32) + right.astype(F32)).astype(left.dtype)


def paired_local(
    tokens, long_docs, w_qkv, bias_qv, w_out, bias_out, w_up, bias_up, w_down, bias_down, alphas,
    cotangent, *, n_dp,
):
    devices = 2 * n_dp
    place = lax.axis_index("tp")
    row_index = lax.axis_index("dp")
    core = row_index % 2
    same = (core == place).astype(jnp.int32)
    is_same = core == place

    def swapped(i):
        return (i & ~3) | ((i & 1) << 1) | ((i >> 1) & 1)

    def trade(value):
        return lax.ppermute(value, AXES, [(i, swapped(i)) for i in range(devices)])

    def cross(value, bit):
        return lax.ppermute(value, AXES, [(i, i ^ bit) for i in range(devices)])

    PLACE, CORE = 1, 2
    outer = []
    bit = 4
    while bit < devices:
        outer.append((bit, (row_index // (bit // 2)) % 2))
        bit *= 2

    half_qkv = w_qkv.shape[2]
    unit = w_up.shape[1] // 2
    part = w_out.shape[0] // 2
    mine = trade(tokens)
    w_role = trade(w_qkv)
    biases = jnp.concatenate([bias_qv.reshape(-1), bias_up]).reshape(-1, 128)
    other_biases = cross(biases, PLACE)
    other = cross(mine, CORE)
    longs = jnp.where(is_same, long_docs, cross(long_docs, CORE))[0]
    flags = jnp.stack([core, place, longs, same]).astype(jnp.int32)
    flat, other_flat = biases.reshape(-1), other_biases.reshape(-1)
    bias_role = (
        jnp.where(is_same, flat[: 2 * half_qkv], other_flat[: 2 * half_qkv])
        .reshape(2, half_qkv)
        .astype(F32)
    )
    bup = jnp.stack([flat[2 * half_qkv :], other_flat[2 * half_qkv :]])[:, None, :].astype(F32)
    q_t, k_t, k, v, keep, send, lse = attend(
        flags, mine, other, w_role, bias_role[:, :, None], bias_role[1:2]
    )
    packed = jnp.concatenate(
        [
            lax.dynamic_slice_in_dim(w_up, core * unit, unit, 1),
            lax.dynamic_slice_in_dim(w_down, core * unit, unit, 0),
            lax.dynamic_slice_in_dim(w_out, core * part, part, 0),
        ],
        0,
    )
    near = cross(packed, PLACE)
    far = cross(near, CORE)
    cot = trade(cotangent)
    recv = cross(send, CORE)
    out, dresid, dkeep, dsend, gkeep, gsend, small = feed(
        flags, alphas, mine, cot, keep, recv, w_up, w_down, w_out, near, far, bup,
        bias_out.astype(F32)[None], bias_down.astype(F32)[None],
    )
    drecv = cross(dsend, CORE)
    grad_qkv, grad_bias, own, away = attend_back(
        flags, mine, other, w_role, q_t, k_t, k, v, keep, send, dkeep, drecv, lse, dresid
    )
    grad_tokens = trade((own + cross(away, CORE).astype(F32)).astype(BF16))
    out = trade(out)

    def spread(value):
        for bit, side in outer:
            size = value.shape[0] // 2
            give = lax.dynamic_slice_in_dim(value, (1 - side) * size, size, 0)
            stay = lax.dynamic_slice_in_dim(value, side * size, size, 0)
            value = add_low(stay, cross(give, bit))
        for bit, side in reversed(outer):
            came = cross(value, bit)
            value = jnp.where(
                side == 0, jnp.concatenate([value, came]), jnp.concatenate([came, value])
            )
        return value

    def both(value):
        came = cross(value, CORE)
        return jnp.where(core == 0, value, came), jnp.where(core == 0, came, value)

    for bit in [CORE, PLACE] + [b for b, _ in outer]:
        small = small + cross(small, bit)
    kept = add_low(gkeep, cross(gsend, CORE))
    kept = add_low(kept[0], cross(kept[1], PLACE))
    first, second = both(spread(kept))
    grad_up = jnp.concatenate([first[:unit], second[:unit]], 1).astype(F32)
    grad_down = jnp.concatenate([first[unit : 2 * unit], second[unit : 2 * unit]], 0).astype(F32)
    grad_out = jnp.concatenate([first[2 * unit :], second[2 * unit :]], 0).astype(F32)
    grad_bias_up = lax.dynamic_slice_in_dim(small[4:], 2 * place, 2, 0).reshape(-1)
    grad_alphas = jnp.stack([jnp.sum(small[2]), jnp.sum(small[3])])

    for bit in [PLACE] + [b for b, _ in outer]:
        grad_bias = grad_bias + cross(grad_bias, bit)
    grad_bias = jnp.where(is_same, grad_bias, cross(grad_bias, CORE))
    heads_sum = add_low(grad_qkv, cross(grad_qkv, PLACE))
    size = heads_sum.shape[0] // 2
    give = lax.dynamic_slice_in_dim(heads_sum, (1 - core) * size, size, 0)
    stay = lax.dynamic_slice_in_dim(heads_sum, core * size, size, 0)
    shared = jnp.where(is_same, stay, cross(give, CORE))
    first, second = both(spread(shared))
    grad_w_qkv = (
        jnp.concatenate([first, second], 0)
        .reshape(3, half_qkv, -1)
        .transpose(0, 2, 1)
        .astype(F32)
    )
    grad_bias_qv = jnp.stack([grad_bias[0], grad_bias[4]])
    return (
        out, grad_tokens, grad_w_qkv, grad_bias_qv, grad_out, small[1], grad_up, grad_bias_up,
        grad_down, small[0], grad_alphas,
    )


def doc_numbers(total, longs):
    places = jnp.arange(total, dtype=jnp.int32)
    border = 2 * SHORT * longs
    return jnp.where(places < border, places // (2 * SHORT), longs + (places - border) // SHORT)


def contract_rows(left, right):
    return lax.dot_general(
        left, right, (((0,), (0,)), ((), ())), preferred_element_type=jnp.float32
    )


def contract_cols(left, right):
    return lax.dot_general(
        left, right, (((1,), (1,)), ((), ())), preferred_element_type=jnp.float32
    )


def gelu_grad(pre_act, upstream):
    _, pull = jax.vjp(jax.nn.gelu, pre_act)
    return pull(upstream)[0]


def local(
    tokens,
    long_docs,
    w_qkv,
    bias_qv,
    w_out,
    bias_out,
    w_up,
    bias_up,
    w_down,
    bias_down,
    alphas,
    cotangent,
):
    gathered = lax.all_gather(tokens, "tp", axis=0, tiled=True)
    total = gathered.shape[0]
    local_width = w_qkv.shape[2]
    local_heads = local_width // HEAD_DIM
    block = min(512, SHORT)
    window = 2 * SHORT // block
    span = window * block
    blocks_count = total // block
    docs = doc_numbers(total, long_docs[0])
    alpha_attn = alphas[0]
    alpha_ffn = alphas[1]
    scale_value = HEAD_DIM ** (-0.5)
    projected = jnp.einsum("td,cdf->ctf", gathered, w_qkv, preferred_element_type=jnp.float32)
    bias_float = bias_qv.astype(jnp.float32)
    query_all = (
        (projected[0] + bias_float[0]).astype(jnp.bfloat16).reshape(total, local_heads, HEAD_DIM)
    )
    key_all = projected[1].astype(jnp.bfloat16).reshape(total, local_heads, HEAD_DIM)
    value_all = (
        (projected[2] + bias_float[1]).astype(jnp.bfloat16).reshape(total, local_heads, HEAD_DIM)
    )

    def block_pieces(index):
        query_start = index * block
        key_start = jnp.maximum(index - window + 1, 0) * block
        query_rows = lax.dynamic_slice_in_dim(query_all, query_start, block, 0)
        query_docs = lax.dynamic_slice_in_dim(docs, query_start, block, 0)
        query_place = query_start + jnp.arange(block, dtype=jnp.int32)
        key_place = key_start + jnp.arange(span, dtype=jnp.int32)
        allowed = (docs[None, :] == query_docs[:, None]) & (
            key_place[None, :] <= query_place[:, None]
        )
        logits = (
            jnp.einsum("qhe,khe->hqk", query_rows, key_all, preferred_element_type=jnp.float32)
            * scale_value
        )
        logits = jnp.where(allowed[None], logits, -1e30)
        return (query_start, key_start, query_rows, key_all, value_all, logits)

    def forward_block(index):
        _, _, _, _, value_rows, logits = block_pieces(index)
        peak = jnp.max(logits, axis=-1, keepdims=True)
        expo = jnp.exp(logits - peak)
        summed = jnp.sum(expo, axis=-1, keepdims=True)
        probs = (expo / summed).astype(jnp.bfloat16)
        mixed_block = jnp.einsum(
            "hqk,khe->qhe", probs, value_rows, preferred_element_type=jnp.float32
        )
        return (mixed_block.astype(jnp.bfloat16), (peak + jnp.log(summed))[..., 0])

    mixed_blocks, log_totals = lax.map(forward_block, jnp.arange(blocks_count, dtype=jnp.int32))
    mixed = mixed_blocks.reshape(total, local_width)
    attn_full = lax.psum_scatter(
        jnp.dot(mixed, w_out, preferred_element_type=jnp.float32),
        "tp",
        scatter_dimension=0,
        tiled=True,
    ) + bias_out.astype(jnp.float32)
    resid = tokens.astype(jnp.float32) + alpha_attn * attn_full
    resid_low = resid.astype(jnp.bfloat16)
    cot_float = cotangent.astype(jnp.float32)
    ffn_grad_low = (alpha_ffn * cot_float).astype(jnp.bfloat16)
    resid_all = lax.all_gather(resid_low, "tp", axis=0, tiled=True)
    pre_act = jnp.dot(resid_all, w_up, preferred_element_type=jnp.float32) + bias_up.astype(
        jnp.float32
    )
    act_low = jax.nn.gelu(pre_act).astype(jnp.bfloat16)
    ffn_out = lax.psum_scatter(
        jnp.dot(act_low, w_down, preferred_element_type=jnp.float32),
        "tp",
        scatter_dimension=0,
        tiled=True,
    )
    ffn_grad_all = lax.all_gather(ffn_grad_low, "tp", axis=0, tiled=True)
    grad_w_down = contract_rows(act_low, ffn_grad_all)
    grad_pre = gelu_grad(pre_act, contract_cols(ffn_grad_all, w_down)).astype(jnp.bfloat16)
    grad_w_up = contract_rows(resid_all, grad_pre)
    grad_bias_up = jnp.sum(grad_pre.astype(jnp.float32), axis=0)
    grad_resid_ffn = lax.psum_scatter(
        contract_cols(grad_pre, w_up), "tp", scatter_dimension=0, tiled=True
    )
    ffn_full = ffn_out + bias_down.astype(jnp.float32)
    out = (resid + alpha_ffn * ffn_full).astype(jnp.bfloat16)
    grad_alpha_ffn = jnp.sum(cot_float * ffn_full)
    grad_bias_down = alpha_ffn * jnp.sum(cot_float, axis=0)
    grad_resid = cot_float + grad_resid_ffn
    grad_alpha_attn = jnp.sum(grad_resid * attn_full)
    grad_bias_out = alpha_attn * jnp.sum(grad_resid, axis=0)
    attn_grad_low = (alpha_attn * grad_resid).astype(jnp.bfloat16)
    attn_grad_all = lax.all_gather(attn_grad_low, "tp", axis=0, tiled=True)
    grad_w_out = contract_rows(mixed, attn_grad_all)
    grad_mixed = (
        contract_cols(attn_grad_all, w_out)
        .astype(jnp.bfloat16)
        .reshape(total, local_heads, HEAD_DIM)
    )

    def backward_block(carry, index):
        grad_keys, grad_values = carry
        query_start, key_start, query_rows, key_rows, value_rows, logits = block_pieces(index)
        block_totals = lax.dynamic_index_in_dim(log_totals, index, 0, keepdims=False)
        probs = jnp.exp(logits - block_totals[:, :, None])
        upstream = lax.dynamic_slice_in_dim(grad_mixed, query_start, block, 0)
        grad_probs = jnp.einsum(
            "qhe,khe->hqk", upstream, value_rows, preferred_element_type=jnp.float32
        )
        row_terms = jnp.sum(probs * grad_probs, axis=-1, keepdims=True)
        grad_logits = (probs * (grad_probs - row_terms)).astype(jnp.bfloat16)
        grad_query_block = (
            jnp.einsum("hqk,khe->qhe", grad_logits, key_rows, preferred_element_type=jnp.float32)
            * scale_value
        )
        key_part = (
            jnp.einsum("hqk,qhe->khe", grad_logits, query_rows, preferred_element_type=jnp.float32)
            * scale_value
        )
        value_part = jnp.einsum(
            "hqk,qhe->khe", probs.astype(jnp.bfloat16), upstream, preferred_element_type=jnp.float32
        )
        grad_keys = grad_keys + key_part
        grad_values = grad_values + value_part
        return ((grad_keys, grad_values), grad_query_block)

    zero_grads = jnp.zeros((total, local_heads, HEAD_DIM), jnp.float32)
    (grad_keys, grad_values), grad_query_blocks = lax.scan(
        backward_block, (zero_grads, zero_grads), jnp.arange(blocks_count, dtype=jnp.int32)
    )
    grad_proj = jnp.stack(
        [
            grad_query_blocks.reshape(total, local_width),
            grad_keys.reshape(total, local_width),
            grad_values.reshape(total, local_width),
        ]
    ).astype(jnp.bfloat16)
    grad_w_qkv = jnp.einsum("td,ctf->cdf", gathered, grad_proj, preferred_element_type=jnp.float32)
    grad_bias_qv = jnp.stack(
        [
            jnp.sum(grad_proj[0].astype(jnp.float32), axis=0),
            jnp.sum(grad_proj[2].astype(jnp.float32), axis=0),
        ]
    )
    grad_in_attn = lax.psum_scatter(
        jnp.einsum("ctf,cdf->td", grad_proj, w_qkv, preferred_element_type=jnp.float32),
        "tp",
        scatter_dimension=0,
        tiled=True,
    )
    grad_tokens = (grad_resid + grad_in_attn).astype(jnp.bfloat16)
    summed = lax.psum(
        (grad_w_qkv, grad_bias_qv, grad_w_out, grad_w_up, grad_bias_up, grad_w_down), "dp"
    )
    small = lax.psum(
        (grad_bias_out, grad_bias_down, jnp.stack([grad_alpha_attn, grad_alpha_ffn])), ("dp", "tp")
    )
    return (
        out,
        grad_tokens,
        summed[0],
        summed[1],
        summed[2],
        small[0],
        summed[3],
        summed[4],
        summed[5],
        small[1],
        small[2],
    )


def solution(mesh):
    step = local
    if mesh.shape["tp"] == 2 and mesh.shape["dp"] & (mesh.shape["dp"] - 1) == 0:
        step = functools.partial(paired_local, n_dp=mesh.shape["dp"])
    return jax.shard_map(
        step,
        mesh=mesh,
        in_specs=(
            P(("dp", "tp"), None),
            P("dp"),
            P(None, None, "tp"),
            P(None, "tp"),
            P("tp", None),
            P(),
            P(None, "tp"),
            P("tp"),
            P("tp", None),
            P(),
            P(),
            P(("dp", "tp"), None),
        ),
        out_specs=(
            P(("dp", "tp"), None),
            P(("dp", "tp"), None),
            P(None, None, "tp"),
            P(None, "tp"),
            P("tp", None),
            P(),
            P(None, "tp"),
            P("tp"),
            P("tp", None),
            P(),
            P(),
        ),
        check_vma=False,
    )
```

```python
import functools

import jax
import jax.numpy as jnp
from jax import lax
from jax.experimental import pallas as pl
from jax.experimental.pallas import tpu as pltpu
from jax.sharding import PartitionSpec as P

HEAD_DIM = 64
SHORT = 1024
LOG2E = 1.4426950408889634
F32 = jnp.float32
BF16 = jnp.bfloat16
NT = (((1,), (1,)), ((), ()))
TN = (((0,), (0,)), ((), ()))
AXES = ("dp", "tp")
GRANT = 60 << 20
BIG = 1e30
PIECES = 8


def dot(left, right, dims=None):
    if dims is None:
        return jnp.dot(left, right, preferred_element_type=F32)
    return lax.dot_general(left, right, dims, preferred_element_type=F32)


def in_vmem():
    return pl.BlockSpec(memory_space=pltpu.VMEM)


def in_smem():
    return pl.BlockSpec(memory_space=pltpu.SMEM)


def lower_half(which, rows):
    zeros = jnp.zeros_like(rows)
    return jnp.where(
        which == 0, jnp.concatenate([rows, zeros], 0), jnp.concatenate([zeros, rows], 0)
    )


def unpacked(pack_ref, which, width):
    rows = pack_ref.shape[1] // 2
    at = slice(which * rows, which * rows + rows)
    return pack_ref[at, :width], pack_ref[at, width : 2 * width]


def attend_kernel(
    flags, mine_ref, other_ref, own_pack_ref, came_pack_ref,
    q_t_ref, k_t_ref, k_ref, v_ref, keep_ref, send_ref, lse_ref,
    v_t, mixed, scores, pack_ref, *, block,
):
    core, longs = flags[0], flags[2]
    pack_ref[...] = jnp.where(flags[3] > 0, own_pack_ref[...], came_pack_ref[...])
    half = mine_ref.shape[0]
    total = 2 * half
    width = pack_ref.shape[1] // 2
    deep = pack_ref.shape[1] // 2
    pairs = width // 128
    heads = width // HEAD_DIM
    turned = [jnp.concatenate([p.T for p in unpacked(pack_ref, i, width)], 1) for i in range(3)]
    bias = pack_ref[3 * deep : 3 * deep + 16, :].astype(F32)[0:8]
    column = bias.T[:, 0:1]

    def project(rows_ref, which):
        at = pl.ds(pl.multiple_of(which * half, half), half)
        rows = rows_ref[...]
        q_t_ref[:, at] = (dot(turned[0], rows, NT) + column[:width]).astype(BF16)
        k_t_ref[:, at] = dot(turned[1], rows, NT).astype(BF16)
        v_t[:, at] = (dot(turned[2], rows, NT) + column[width:]).astype(BF16)
        for i, target in ((1, k_ref), (2, v_ref)):
            upper, lower = unpacked(pack_ref, i, width)
            for pair in range(pairs):
                cols = slice(pair * 128, pair * 128 + 128)
                part = dot(rows[:, :deep], upper[:, cols]) + dot(rows[:, deep:], lower[:, cols])
                if i == 2:
                    part = part + bias[0:1, width + pair * 128 : width + pair * 128 + 128]
                target[pair, at, :] = part.astype(BF16)

    project(mine_ref, core)
    project(other_ref, 1 - core)
    row = lax.broadcasted_iota(jnp.int32, (block, block), 0)
    col = lax.broadcasted_iota(jnp.int32, (block, block), 1)
    scale = HEAD_DIM ** (-0.5) * LOG2E

    def one_head(head, _):
        at = pl.ds(pl.multiple_of(head * HEAD_DIM, HEAD_DIM), HEAD_DIM)
        pair, which = head // 2, head % 2
        for q0 in range(0, total, block):
            queries = lower_half(which, q_t_ref[at, q0 : q0 + block])
            peak = jnp.full((8, block), -BIG, F32)
            for k0 in range(0, q0 + block, block):
                s = dot(k_ref[pair, k0 : k0 + block, :], queries)
                if k0 == q0:
                    s = jnp.where(row <= col, s, -BIG)
                scores[k0 : k0 + block, :] = s
                top = jnp.max(s.reshape(block // 8, 8, block), 0)
                if q0 >= SHORT > k0:
                    top = jnp.where(longs > 0, top, -BIG)
                peak = jnp.maximum(peak, top)
            peak = jnp.max(peak, 0, keepdims=True) * scale
            acc = jnp.zeros((HEAD_DIM, block), F32)
            norm = jnp.zeros((8, block), F32)
            for k0 in range(0, q0 + block, block):
                base = peak
                if q0 >= SHORT > k0:
                    base = jnp.where(longs > 0, peak, BIG)
                e = jnp.exp2(scores[k0 : k0 + block, :] * scale - base)
                norm = norm + jnp.sum(e.reshape(block // 8, 8, block), 0)
                acc = acc + dot(v_t[at, k0 : k0 + block], e.astype(BF16))
            norm = jnp.sum(norm, 0, keepdims=True)
            mixed[q0 // half, at, q0 % half : q0 % half + block] = (acc / norm).astype(BF16)
            lse_ref[head, :, q0 : q0 + block] = jnp.broadcast_to(
                peak + jnp.log2(norm), (8, block)
            )
        return 0

    lax.fori_loop(0, heads, one_head, 0)
    keep_ref[...] = mixed[core]
    send_ref[...] = mixed[1 - core]


def attend(flags, mine, other, own_pack, came_pack):
    half = mine.shape[0]
    total, width = 2 * half, own_pack.shape[1] // 2
    shape = jax.ShapeDtypeStruct
    block = 512
    return pl.pallas_call(
        functools.partial(attend_kernel, block=block),
        out_shape=(
            shape((width, total), BF16),
            shape((width, total), BF16),
            shape((width // 128, total, 128), BF16),
            shape((width // 128, total, 128), BF16),
            shape((width, half), BF16),
            shape((width, half), BF16),
            shape((width // HEAD_DIM, 8, total), F32),
        ),
        in_specs=[in_smem()] + [in_vmem()] * 4,
        out_specs=(in_vmem(),) * 7,
        scratch_shapes=[
            pltpu.VMEM((width, total), BF16),
            pltpu.VMEM((2, width, half), BF16),
            pltpu.VMEM((total, block), F32),
            pltpu.VMEM(own_pack.shape, BF16),
        ],
        compiler_params=pltpu.CompilerParams(vmem_limit_bytes=GRANT),
        cost_estimate=pl.CostEstimate(
            flops=0, bytes_accessed=0, transcendentals=0
        ),
    )(flags, mine, other, own_pack, came_pack)


def feed_kernel(
    flags, alphas, tok_ref, own_cot_ref, came_cot_ref, keep_ref, recv_ref, up_ref, down_ref,
    wout_ref, near_ref, far_ref, bias_ref, bup_ref,
    out_ref, dresid_ref, dkeep_ref, dsend_ref, gkeep_a_ref, gkeep_b_ref, gsend_a_ref, gsend_b_ref,
    mixed, dmixed, attn, resid, ffn, act, dpre, small, cot_ref, *, piece,
):
    core, same = flags[0], flags[3]
    rows, width = tok_ref.shape
    side, deep = flags[4], flags[5]
    main = gkeep_a_ref.shape[2] - 8
    unit = up_ref.shape[1] // 2
    part = wout_ref.shape[0] // 2
    a_attn, a_ffn = alphas[0], alphas[1]
    cot_ref[...] = jnp.where(same > 0, own_cot_ref[...], came_cot_ref[...])
    biases = bias_ref[...].astype(F32)
    own_bup = bup_ref[...].astype(F32)
    mixed[1 - same] = keep_ref[...]
    mixed[same] = recv_ref[...]

    def own_sub(j):
        return core if j == 0 else 1 - core

    def place_of(h, j, piece_at):
        y = 1 - side if (piece_at // 2) % 2 else side
        z = 1 - deep if piece_at % 2 else deep
        if piece_at < PIECES // 2:
            return (gkeep_a_ref, gsend_a_ref)[j].at[h, 2 * y + z]
        return (gkeep_b_ref, gsend_b_ref)[j].at[y, 2 * h + z]

    def put(h, j, start, value):
        value = value.astype(BF16)
        at = 0
        while at < value.shape[0]:
            piece_at, row = divmod(start + at, main)
            size = min(main - row, value.shape[0] - at)
            place_of(h, j, piece_at)[row : row + size, :] = value[at : at + size]
            at += size

    def wout_part(h, j):
        if h == 0:
            return wout_ref[pl.ds(pl.multiple_of(own_sub(j) * part, part), part), :]
        return (near_ref, far_ref)[j][2 * unit : 2 * unit + part, :]

    def mixed_part(h, j):
        return mixed[h, pl.ds(pl.multiple_of(own_sub(j) * part, part), part), :]

    total = dot(mixed_part(0, 0), wout_part(0, 0), TN)
    for h, j in ((0, 1), (1, 0), (1, 1)):
        total = total + dot(mixed_part(h, j), wout_part(h, j), TN)
    attn[...] = total + biases[1:2]
    resid[...] = tok_ref[...].astype(F32) + a_attn * attn[...]
    low = resid[...].astype(BF16)
    low_t = low.T
    dffn = (cot_ref[...].astype(F32) * a_ffn).astype(BF16)
    dffn_t = dffn.T
    dresid_ref[...] = cot_ref[...].astype(F32)
    ffn[...] = jnp.broadcast_to(biases[2:3], ffn.shape)
    for h in range(2):
        for j in range(2):
            sub = pl.ds(pl.multiple_of(own_sub(j) * unit, unit), unit)
            if h == 0:
                up, down = up_ref[:, sub], down_ref[sub, :]
            else:
                source = (near_ref, far_ref)[j]
                up, down = source[:unit, :], source[unit : 2 * unit, :]
            if h == 0:
                bias = jnp.where(own_sub(j) == 0, own_bup[1:2], own_bup[2:3])
            else:
                end = 2 * unit + part
                bias = source[end : end + 16, :].astype(F32)[0:1]
            bias_grad = jnp.zeros((8, unit), F32)
            for r0 in range(0, rows, piece):
                at = slice(r0, r0 + piece)
                u = dot(low[at], up) + bias
                square = u * u
                t = jnp.tanh(u * (0.7978845608028654 + 0.035677408136300125 * square))
                s = 0.5 + 0.5 * t
                slope = s + (0.5 * u) * (1.0 - t * t) * (
                    0.7978845608028654 + 0.10703222440890037 * square
                )
                act[at, :] = (u * s).astype(BF16)
                d = dot(dffn[at], down, NT) * slope
                d_low = d.astype(BF16)
                dpre[at, :] = d_low
                bias_grad = bias_grad + jnp.sum(
                    d_low.astype(F32).reshape(piece // 8, 8, unit), 0
                )
                ffn[at, :] += dot(act[at, :], down)
                dresid_ref[at, :] += dot(d_low, up, NT)
            put(h, j, 0, dot(low_t, dpre[...]))
            put(h, j, unit, dot(dffn_t, act[...]).T)
            small[2 * h + j, :] = jnp.sum(bias_grad, 0)
    g = cot_ref[...].astype(F32)
    out_ref[...] = (resid[...] + a_ffn * ffn[...]).astype(BF16)
    dresid = dresid_ref[...]
    bias_down = a_ffn * jnp.sum(g, 0, keepdims=True)
    bias_out = a_attn * jnp.sum(dresid, 0, keepdims=True)
    sums = [
        jnp.sum(jnp.sum(v, 0, keepdims=True), 1, keepdims=True)
        for v in (dresid * attn[...], g * ffn[...])
    ]
    lane = lax.broadcasted_iota(jnp.int32, (1, width), 1)
    both = jnp.where(lane == 0, sums[0], jnp.where(lane == 1, sums[1], 0.0))
    dattn = (a_attn * dresid).astype(BF16)
    for h in range(2):
        for j in range(2):
            put(h, j, 2 * unit, dot(mixed_part(h, j), dattn))
            dmixed[h, pl.ds(pl.multiple_of(own_sub(j) * part, part), part), :] = dot(
                wout_part(h, j), dattn, NT
            ).astype(BF16)
            exact = jnp.concatenate(
                [small[2 * h + j : 2 * h + j + 1, :], bias_down, bias_out, both], 0
            )
            high = exact.astype(BF16).astype(F32)
            for i in range(1, PIECES):
                place_of(h, j, i)[main:, :] = jnp.zeros((8, width), BF16)
            place_of(h, j, 0)[main:, :] = jnp.concatenate([high, exact - high], 0).astype(BF16)
    dkeep_ref[...] = dmixed[1 - same]
    dsend_ref[...] = dmixed[same]


def feed(
    flags, alphas, tok, own_cot, came_cot, keep, recv, up, down, wout, near, far, pack, packed
):
    rows, width = tok.shape
    unit = up.shape[1] // 2
    half_width = keep.shape[0]
    shape = jax.ShapeDtypeStruct

    def last_rows(x):
        return pl.BlockSpec((16, x.shape[1]), lambda i: (x.shape[0] // 16 - 1, 0))

    def whole(x):
        return pl.BlockSpec(x.shape, lambda i: (0,) * x.ndim)

    piece = shape((2, PIECES // 2, (2 * unit + half_width // 2) // PIECES + 8, width), BF16)
    outs = (
        shape((rows, width), BF16),
        shape((rows, width), F32),
        shape((half_width, rows), BF16),
        shape((half_width, rows), BF16),
        piece,
        piece,
        piece,
        piece,
    )
    values = (tok, own_cot, came_cot, keep, recv, up, down, wout, near, far)
    return pl.pallas_call(
        functools.partial(feed_kernel, piece=256),
        grid=(1,),
        out_shape=outs,
        in_specs=[in_smem()] * 2 + [whole(x) for x in values] + [last_rows(pack), last_rows(packed)],
        out_specs=tuple(whole(x) for x in outs),
        scratch_shapes=[
            pltpu.VMEM((2, half_width, rows), BF16),
            pltpu.VMEM((2, half_width, rows), BF16),
            pltpu.VMEM((rows, width), F32),
            pltpu.VMEM((rows, width), F32),
            pltpu.VMEM((rows, width), F32),
            pltpu.VMEM((rows, unit), BF16),
            pltpu.VMEM((rows, unit), BF16),
            pltpu.VMEM((8, unit), F32),
            pltpu.VMEM((rows, width), BF16),
        ],
        compiler_params=pltpu.CompilerParams(vmem_limit_bytes=GRANT),
        cost_estimate=pl.CostEstimate(
            flops=0, bytes_accessed=0, transcendentals=0
        ),
    )(flags, alphas, *values, pack, packed)


def attend_back_kernel(
    flags, mine_ref, other_ref, q_t_ref, k_t_ref, k_ref, v_ref, keep_ref, send_ref,
    dkeep_ref, drecv_ref, lse_ref,
    sums_ref, grads,
    mixed, dmixed, probs, dscores, *, block,
):
    core, longs = flags[0], flags[2]
    half = mine_ref.shape[0]
    total = 2 * half
    mixed[core] = keep_ref[...]
    mixed[1 - core] = send_ref[...]
    dmixed[core] = dkeep_ref[...]
    dmixed[1 - core] = drecv_ref[...]
    factor = HEAD_DIM ** (-0.5)
    scale = factor * LOG2E
    part = block // 2

    def one_head(which, _):
        at = pl.ds(pl.multiple_of(which * HEAD_DIM, HEAD_DIM), HEAD_DIM)
        for q0 in range(0, total, block):
            here = slice(q0 % half, q0 % half + block)
            do = dmixed[q0 // half, at, here]
            queries = lower_half(which, q_t_ref[at, q0 : q0 + block])
            upstream = lower_half(which, do)
            lse = lse_ref[which, 0:1, q0 : q0 + block]
            mean = jnp.sum(
                do.astype(F32) * mixed[q0 // half, at, here].astype(F32), 0, keepdims=True
            )
            pieces = [(k0, block, 0) for k0 in range(0, q0, block)]
            pieces += [(q0, part, 0), (q0 + part, part, part)]
            for k0, size, skip in pieces:
                keys, cols = slice(k0, k0 + size), slice(q0 + skip, q0 + block)
                base = lse
                if q0 >= SHORT > k0:
                    base = jnp.where(longs > 0, lse, BIG)
                s = dot(k_ref[0, keys, :], queries[:, skip:])
                dp = dot(v_ref[0, keys, :], upstream[:, skip:])
                p = jnp.exp2(s * scale - base[:, skip:])
                if k0 >= q0:
                    row = lax.broadcasted_iota(jnp.int32, p.shape, 0) + k0
                    col = lax.broadcasted_iota(jnp.int32, p.shape, 1) + (q0 + skip)
                    p = jnp.where(row <= col, p, 0.0)
                probs[keys, cols] = p.astype(BF16)
                dscores[keys, cols] = (p * (dp - mean[:, skip:])).astype(BF16)
                if skip:
                    probs[keys, q0 : q0 + skip] = jnp.zeros((size, skip), BF16)
                    dscores[keys, q0 : q0 + skip] = jnp.zeros((size, skip), BF16)
            end = q0 + block
            grads[0, at, q0:end] = (
                dot(k_t_ref[at, 0:end], dscores[0:end, q0:end]) * factor
            ).astype(BF16)
        for k0 in range(0, total, block):
            keys = slice(k0, k0 + block)
            grads[1, at, keys] = (
                dot(q_t_ref[at, k0:], dscores[keys, k0:], NT) * factor
            ).astype(BF16)
            first = k0 // half
            acc = dot(dmixed[first, at, k0 % half :], probs[keys, k0 : (first + 1) * half], NT)
            if first == 0:
                acc = acc + dot(dmixed[1, at, :], probs[keys, half:], NT)
            grads[2, at, keys] = acc.astype(BF16)
        return 0

    lax.fori_loop(0, 2, one_head, 0)
    near = pl.ds(pl.multiple_of(core * half, half), half)
    far = pl.ds(pl.multiple_of((1 - core) * half, half), half)
    main = sums_ref.shape[1] - 16
    deep = mine_ref.shape[1]
    for i in range(3):
        value = (
            dot(grads[i, :, near], mine_ref[...]) + dot(grads[i, :, far], other_ref[...])
        ).T.astype(BF16)
        at = 0
        while at < deep:
            piece, row = divmod(i * deep + at, main)
            size = min(main - row, deep - at)
            sums_ref[piece, row : row + size, :] = value[at : at + size]
            at += size
    ones = jnp.ones((8, total), BF16)
    rest = jnp.zeros((14, 2 * HEAD_DIM), F32)
    sums_ref[0, main:, :] = jnp.concatenate(
        [dot(ones, grads[0], NT)[0:1], dot(ones, grads[2], NT)[0:1], rest], 0
    ).astype(BF16)
    for piece in range(1, sums_ref.shape[0]):
        sums_ref[piece, main:, :] = jnp.zeros((16, 2 * HEAD_DIM), BF16)


def attend_back(pair, flags, mine, other, q_t, k_t, k, v, keep, send, dkeep, drecv, lse):
    half, width_all = mine.shape
    total = 2 * half
    shape = jax.ShapeDtypeStruct

    def whole(x):
        return pl.BlockSpec(x.shape, lambda i: (0,) * x.ndim)

    def rows_of(x):
        return pl.BlockSpec((2 * HEAD_DIM, x.shape[1]), lambda i: (pair, 0))

    def pair_of(x):
        return pl.BlockSpec((1,) + x.shape[1:], lambda i: (pair, 0, 0))

    outs = (
        shape((4, 3 * width_all // 4 + 16, 2 * HEAD_DIM), BF16),
        shape((3, 2 * HEAD_DIM, total), BF16),
    )
    return pl.pallas_call(
        functools.partial(attend_back_kernel, block=512),
        grid=(1,),
        out_shape=outs,
        in_specs=[in_smem(), whole(mine), whole(other), rows_of(q_t), rows_of(k_t), pair_of(k),
                  pair_of(v), rows_of(keep), rows_of(send), rows_of(dkeep), rows_of(drecv),
                  pl.BlockSpec((2, 8, total), lambda i: (pair, 0, 0))],
        out_specs=tuple(whole(x) for x in outs),
        scratch_shapes=[
            pltpu.VMEM((2, 2 * HEAD_DIM, half), BF16),
            pltpu.VMEM((2, 2 * HEAD_DIM, half), BF16),
            pltpu.VMEM((total, total), BF16),
            pltpu.VMEM((total, total), BF16),
        ],
        compiler_params=pltpu.CompilerParams(vmem_limit_bytes=GRANT),
        cost_estimate=pl.CostEstimate(
            flops=0, bytes_accessed=0, transcendentals=0
        ),
    )(flags, mine, other, q_t, k_t, k, v, keep, send, dkeep, drecv, lse)


def inputs_back_kernel(flags, own_pack_ref, came_pack_ref, dresid_ref, *refs):
    core = flags[0]
    *grads, own_ref, away_ref, pack_ref = refs
    pack_ref[...] = jnp.where(flags[3] > 0, own_pack_ref[...], came_pack_ref[...])
    half = own_ref.shape[0]
    width = pack_ref.shape[1] // 2

    def back(which):
        at = pl.ds(pl.multiple_of(which * half, half), half)
        result = []
        for part in range(2):
            total = 0.0
            for i in range(3):
                weights = unpacked(pack_ref, i, width)[part]
                stacked = jnp.concatenate([g[i, :, at] for g in grads], 0)
                total = total + dot(weights, stacked)
            result.append(total.T)
        return jnp.concatenate(result, 1)

    away_ref[...] = back(1 - core).astype(BF16)
    own_ref[...] = dresid_ref[...] + back(core)


def inputs_back(flags, own_pack, came_pack, dresid, grads):
    half, width_all = dresid.shape
    shape = jax.ShapeDtypeStruct
    return pl.pallas_call(
        inputs_back_kernel,
        out_shape=(shape((half, width_all), F32), shape((half, width_all), BF16)),
        in_specs=[in_smem()] + [in_vmem()] * (3 + len(grads)),
        out_specs=(in_vmem(),) * 2,
        scratch_shapes=[pltpu.VMEM(own_pack.shape, BF16)],
        compiler_params=pltpu.CompilerParams(vmem_limit_bytes=GRANT),
        cost_estimate=pl.CostEstimate(
            flops=0, bytes_accessed=0, transcendentals=0
        ),
    )(flags, own_pack, came_pack, dresid, *grads)


def unpack_heads_kernel(flags, mine_ref, came_ref, grad_ref, bias_ref):
    core, side = flags[0], flags[4]
    main = mine_ref.shape[2] - 16
    for far in range(2):
        source = came_ref if far else mine_ref
        for turn in range(2):
            piece = 2 * (1 - core if far else core) + (1 - side if turn else side)
            at = pl.ds(pl.multiple_of(piece * main, main), main)
            for pair in range(source.shape[1]):
                cols = slice(pair * 128, pair * 128 + 128)
                grad_ref[at, cols] = source[turn, pair, :main, :].astype(F32)

            @pl.when(piece == 0)
            def _():
                for pair in range(source.shape[1]):
                    cols = slice(pair * 128, pair * 128 + 128)
                    bias_ref[:, cols] = source[turn, pair, main:, :].astype(F32)[0:2]


def unpack_heads(flags, mine, came, width):
    shape = jax.ShapeDtypeStruct
    main = mine.shape[2] - 16
    return pl.pallas_call(
        unpack_heads_kernel,
        out_shape=(shape((4 * main, width), F32), shape((2, width), F32)),
        in_specs=[in_smem()] + [in_vmem()] * 2,
        out_specs=(in_vmem(),) * 2,
        compiler_params=pltpu.CompilerParams(vmem_limit_bytes=GRANT),
    )(flags, mine, came)


def unpack_feed_kernel(
    flags, mine_ref, came_ref, up_ref, down_ref, out_ref, bup_ref, bdown_ref, bout_ref,
    alphas_ref, rows_ref, small_ref, *, unit,
):
    core, side, deep = flags[0], flags[4], flags[5]
    main = mine_ref.shape[3] - 8
    for far in range(2):
        source = came_ref if far else mine_ref
        which = 1 - core if far else core
        for turn in range(2):
            for dip in range(2):
                for order in range(2):
                    piece = (
                        4 * order
                        + 2 * (1 - side if turn else side)
                        + (1 - deep if dip else deep)
                    )
                    at = pl.ds(pl.multiple_of(piece * main, 16), main)
                    rows_ref[which, at, :] = source[turn, dip, order, :main, :]
                    if order == 0:

                        @pl.when(piece == 0)
                        def _():
                            both = source[turn, dip, order, main:, :].astype(F32)
                            small_ref[which] = both[0:4] + both[4:8]

    width = small_ref.shape[2]
    for i in range(2):
        bup_ref[i * unit : (i + 1) * unit] = small_ref[i, 0, :]
    bdown_ref[...] = small_ref[0, 1, :]
    bout_ref[...] = small_ref[0, 2, :]
    last = small_ref[0, 3:4, :]
    lane = lax.broadcasted_iota(jnp.int32, (1, width), 1)
    for i in range(2):
        alphas_ref[i] = jnp.sum(jnp.where(lane == i, last, 0.0))
    for i in range(2):
        up_ref[:, i * unit : (i + 1) * unit] = rows_ref[i, :unit, :].astype(F32)
        down_ref[i * unit : (i + 1) * unit, :] = rows_ref[i, unit : 2 * unit, :].astype(F32)
        part = rows_ref.shape[1] - 2 * unit
        out_ref[i * part : (i + 1) * part, :] = rows_ref[i, 2 * unit :, :].astype(F32)


def unpack_feed(flags, mine, came, unit):
    shape = jax.ShapeDtypeStruct
    main, width = mine.shape[3] - 8, mine.shape[4]
    return pl.pallas_call(
        functools.partial(unpack_feed_kernel, unit=unit),
        out_shape=(
            shape((width, 2 * unit), F32),
            shape((2 * unit, width), F32),
            shape((2 * (PIECES * main - 2 * unit), width), F32),
            shape((2 * unit,), F32),
            shape((width,), F32),
            shape((width,), F32),
            shape((2,), F32),
        ),
        in_specs=[in_smem()] + [in_vmem()] * 2,
        out_specs=(in_vmem(),) * 6 + (in_smem(),),
        scratch_shapes=[
            pltpu.VMEM((2, PIECES * main, width), BF16),
            pltpu.VMEM((2, 4, width), F32),
        ],
        compiler_params=pltpu.CompilerParams(vmem_limit_bytes=GRANT),
    )(flags, mine, came)


def add_low(values):
    total = values[0].astype(F32)
    for value in values[1:]:
        total = total + value.astype(F32)
    return total.astype(BF16)


def take(value, *picks):
    block, index = [], []
    for axis in range(value.ndim - 2):
        what = picks[axis] if axis < len(picks) else None
        if what is None:
            what = (0, value.shape[axis])
        elif isinstance(what, int):
            what = (what, 1)
        block.append(what[1])
        index.append(what[0])
    return value, tuple(block) + value.shape[-2:], tuple(index) + (0, 0)


def sum_kernel(*refs, plan, n_in):
    ins, outs = refs[:n_in], refs[n_in:]

    def terms(total):
        exact = total[0:4] + total[4:8]
        high = exact.astype(BF16).astype(F32)
        return jnp.concatenate([high, exact - high], 0)

    for out, groups in zip(outs, plan):
        at = 0
        main = out.shape[-2] - 8
        for members, alike in groups:
            lead = 1
            for size in ins[members[0]].shape[:-2]:
                lead *= size
            for i in range(lead):
                total, rows = None, None
                for n, member in enumerate(members):
                    ref = ins[member]
                    index, rest = [], i
                    for size in reversed(ref.shape[:-2]):
                        index.insert(0, rest % size)
                        rest //= size
                    value = ref[tuple(index)].astype(F32)
                    top, low = value[:main], value[main:]
                    total = top if total is None else total + top
                    rows = low if rows is None else rows + low
                    if n + 1 == alike:
                        rows = terms(rows).astype(BF16).astype(F32)
                out[at, :main, :] = total.astype(BF16)
                out[at, main:, :] = terms(rows).astype(BF16)
                at += 1


def sum_pieces(*outs):
    blocks, plan, shapes = [], [], []
    for groups in outs:
        lead, steps = 0, []
        for members, alike in groups:
            steps.append((tuple(range(len(blocks), len(blocks) + len(members))), alike))
            blocks.extend(members)
            count = 1
            for size in members[0][1][:-2]:
                count *= size
            lead += count
        plan.append(tuple(steps))
        shapes.append(jax.ShapeDtypeStruct((lead,) + groups[0][0][0][1][-2:], BF16))
    return pl.pallas_call(
        functools.partial(sum_kernel, plan=tuple(plan), n_in=len(blocks)),
        grid=(1,),
        out_shape=tuple(shapes),
        in_specs=[pl.BlockSpec(block, lambda i, at=at: at) for _, block, at in blocks],
        out_specs=tuple(pl.BlockSpec(x.shape, lambda i: (0, 0, 0)) for x in shapes),
        compiler_params=pltpu.CompilerParams(vmem_limit_bytes=GRANT),
        cost_estimate=pl.CostEstimate(flops=0, bytes_accessed=0, transcendentals=0),
    )(*(value for value, _, _ in blocks))


def pick(value, side, axis):
    size = value.shape[axis] // 2
    return lax.dynamic_slice_in_dim(value, side * size, size, axis)


def paired_local(
    tokens, long_docs, w_qkv, bias_qv, w_out, bias_out, w_up, bias_up, w_down, bias_down, alphas,
    cotangent, *, n_dp,
):
    devices = 2 * n_dp
    place = lax.axis_index("tp")
    row_index = lax.axis_index("dp")
    core = row_index % 2
    same = (core == place).astype(jnp.int32)
    is_same = core == place

    def swapped(i):
        return (i & ~3) | ((i & 1) << 1) | ((i >> 1) & 1)

    def trade(value):
        pairs = [(i, swapped(i)) for i in range(devices) if i != swapped(i)]
        return lax.ppermute(value, AXES, pairs)

    def cross(value, bit):
        return lax.ppermute(value, AXES, [(i, i ^ bit) for i in range(devices)])

    def collect(value):
        return lax.ppermute(
            value, AXES, [(i, i ^ 1) for i in range(devices) if (i & 1) != (i >> 1) & 1]
        )

    PLACE, CORE, NEXT = 1, 2, 4
    side = (row_index // 2) % 2
    outer = []
    bit = 8
    while bit < devices:
        outer.append((bit, (row_index // (bit // 2)) % 2))
        bit *= 2

    width_all, half_qkv = w_qkv.shape[1:]
    unit = w_up.shape[1] // 2
    part = w_out.shape[0] // 2
    own_pack = jnp.concatenate(
        [
            jnp.concatenate(
                [w_qkv[:, : width_all // 2], w_qkv[:, width_all // 2 :]], 2
            ).reshape(-1, 2 * half_qkv),
            bias_qv.reshape(1, -1),
            bias_out[None],
            bias_down[None],
            jnp.zeros((13, width_all), BF16),
        ],
        0,
    )
    packed = jnp.concatenate(
        [
            lax.dynamic_slice_in_dim(w_up, core * unit, unit, 1),
            lax.dynamic_slice_in_dim(w_down, core * unit, unit, 0),
            lax.dynamic_slice_in_dim(w_out, core * part, part, 0),
            lax.dynamic_slice_in_dim(bias_up, core * unit, unit, 0)[None],
            bias_up.reshape(2, unit),
            jnp.zeros((13, unit), BF16),
        ],
        0,
    )
    came, came_pack = trade(tokens), trade(own_pack)
    came, came_pack, packed_tied, cotangent_tied = lax.optimization_barrier(
        (came, came_pack, packed, cotangent)
    )
    near = cross(packed_tied, PLACE)
    came_cot = trade(cotangent_tied)
    mine = jnp.where(is_same, tokens, came)
    longs = jnp.where(is_same, long_docs, cross(long_docs, CORE))[0]
    flags = jnp.stack([core, place, longs, same, side, outer[0][1]]).astype(jnp.int32)
    other = cross(mine, CORE)
    q_t, k_t, k, v, keep, send, lse = attend(flags, mine, other, own_pack, came_pack)
    near, came_cot, _ = lax.optimization_barrier((near, came_cot, send))
    far = cross(near, CORE)
    recv = cross(send, CORE)
    out, dresid, dkeep, dsend, keep_a, keep_b, send_a, send_b = feed(
        flags, alphas, mine, cotangent, came_cot, keep, recv, w_up, w_down, w_out, near, far,
        own_pack, packed,
    )
    drecv = cross(dsend, CORE)
    back_args = (flags, mine, other, q_t, k_t, k, v, keep, send, dkeep, drecv, lse)
    tie = lax.optimization_barrier

    other_a, other_b = cross(send_a, CORE), cross(send_b, CORE)
    give_a, give_b = sum_pieces(
        [([take(keep_a, 1), take(other_a, 1)], 0)], [([take(keep_b, 1), take(other_b, 1)], 0)]
    )
    back_args, give_a, give_b = tie((back_args, give_a, give_b))
    got_a, got_b = cross(give_a, PLACE), cross(give_b, NEXT)
    sums_0, grads_0 = attend_back(0, *back_args)
    total_a, give_b = sum_pieces(
        [([take(keep_a, 0), take(other_a, 0), take(got_a[None])], 2)],
        [([take(keep_b, 0, (1, 2)), take(other_b, 0, (1, 2)), take(got_b, (1, 2))], 0)],
    )
    give_a = total_a[2:]
    back_args, give_a, give_b, sums_0, out = tie((back_args, give_a, give_b, sums_0, out))
    got_a, got_b2 = cross(give_a, NEXT), cross(give_b, PLACE)
    got_0 = collect(sums_0)
    out_came = trade(out)
    sums_1, grads_1 = attend_back(1, *back_args)
    stay, give = sum_pieces(
        *(
            [
                ([take(total_a, i), take(got_a, i)], 0),
                ([take(keep_b, 0, i), take(other_b, 0, i), take(got_b, i), take(got_b2, i)], 0),
            ]
            for i in range(2)
        )
    )
    grads_0, give, sums_1, out_came = tie((grads_0, give, sums_1, out_came))
    got = cross(give, outer[0][0])
    got_1 = collect(sums_1)
    own, away = inputs_back(flags, own_pack, came_pack, dresid, (grads_0, grads_1))
    got, got_1, own, away = tie((got, got_1, own, away))

    (value,) = sum_pieces([([take(stay), take(got)], 0)])
    parts = [jnp.stack([sums_0, sums_1]), jnp.stack([got_0, got_1])]
    stay_q, give_q = (add_low([pick(p, i, 1) for p in parts]) for i in (core, 1 - core))
    heads = jnp.where(is_same, stay_q, cross(give_q, CORE))
    grad_tokens = (own + cross(away, CORE).astype(F32)).astype(BF16)
    value, give_q, grad_tokens = tie((value, pick(heads, 1 - side, 1), grad_tokens))
    low_bit, high_bit = outer[0][0], outer[1][0]
    halves = [value[:1], value[1:]]
    got_half = cross(halves[0], high_bit)
    got_q = cross(give_q, NEXT)
    tokens_came = trade(grad_tokens)
    heads = add_low([pick(heads, side, 1), got_q])[:, 0]
    got_half, heads = tie((got_half, heads))
    got_other = cross(halves[1], high_bit)
    heads = add_low([heads, cross(heads, low_bit)])
    (value,) = sum_pieces(
        [([take(halves[0]), take(got_half)], 0), ([take(halves[1]), take(got_other)], 0)]
    )
    value, heads = tie((value, heads))
    along, beside = cross(value, low_bit), cross(value, NEXT)
    heads = add_low([heads, cross(heads, high_bit)])
    along, beside, heads, tokens_came = tie((along, beside, heads, tokens_came))
    corner = cross(along, NEXT)
    heads_next = cross(heads, NEXT)
    corner, heads_next = tie((corner, heads_next))
    value = jnp.stack([jnp.stack([value, along]), jnp.stack([beside, corner])])
    heads = jnp.stack([heads, heads_next])
    value, heads = tie((value, heads))
    heads_came, value_came = cross(heads, CORE), cross(value, CORE)
    grad_w_qkv, grad_bias_qv = unpack_heads(flags, heads, heads_came, half_qkv)
    out = jnp.where(is_same, out, out_came)
    grad_tokens = jnp.where(is_same, grad_tokens, tokens_came)
    grad_w_qkv, value_came, out, grad_tokens = tie((grad_w_qkv, value_came, out, grad_tokens))
    grad_up, grad_down, grad_out, grad_bias_up, grad_bias_down, grad_bias_out, grad_alphas = (
        unpack_feed(flags, value, value_came, unit)
    )
    return (
        out, grad_tokens, grad_w_qkv.reshape(3, width_all, half_qkv), grad_bias_qv, grad_out,
        grad_bias_out, grad_up, grad_bias_up, grad_down, grad_bias_down, grad_alphas,
    )


def doc_numbers(total, longs):
    places = jnp.arange(total, dtype=jnp.int32)
    border = 2 * SHORT * longs
    return jnp.where(places < border, places // (2 * SHORT), longs + (places - border) // SHORT)


def contract_rows(left, right):
    return lax.dot_general(
        left, right, (((0,), (0,)), ((), ())), preferred_element_type=jnp.float32
    )


def contract_cols(left, right):
    return lax.dot_general(
        left, right, (((1,), (1,)), ((), ())), preferred_element_type=jnp.float32
    )


def gelu_grad(pre_act, upstream):
    _, pull = jax.vjp(jax.nn.gelu, pre_act)
    return pull(upstream)[0]


def local(
    tokens,
    long_docs,
    w_qkv,
    bias_qv,
    w_out,
    bias_out,
    w_up,
    bias_up,
    w_down,
    bias_down,
    alphas,
    cotangent,
):
    gathered = lax.all_gather(tokens, "tp", axis=0, tiled=True)
    total = gathered.shape[0]
    local_width = w_qkv.shape[2]
    local_heads = local_width // HEAD_DIM
    block = min(512, SHORT)
    window = 2 * SHORT // block
    span = window * block
    blocks_count = total // block
    docs = doc_numbers(total, long_docs[0])
    alpha_attn = alphas[0]
    alpha_ffn = alphas[1]
    scale_value = HEAD_DIM ** (-0.5)
    projected = jnp.einsum("td,cdf->ctf", gathered, w_qkv, preferred_element_type=jnp.float32)
    bias_float = bias_qv.astype(jnp.float32)
    query_all = (
        (projected[0] + bias_float[0]).astype(jnp.bfloat16).reshape(total, local_heads, HEAD_DIM)
    )
    key_all = projected[1].astype(jnp.bfloat16).reshape(total, local_heads, HEAD_DIM)
    value_all = (
        (projected[2] + bias_float[1]).astype(jnp.bfloat16).reshape(total, local_heads, HEAD_DIM)
    )

    def block_pieces(index):
        query_start = index * block
        key_start = jnp.maximum(index - window + 1, 0) * block
        query_rows = lax.dynamic_slice_in_dim(query_all, query_start, block, 0)
        query_docs = lax.dynamic_slice_in_dim(docs, query_start, block, 0)
        query_place = query_start + jnp.arange(block, dtype=jnp.int32)
        key_place = key_start + jnp.arange(span, dtype=jnp.int32)
        allowed = (docs[None, :] == query_docs[:, None]) & (
            key_place[None, :] <= query_place[:, None]
        )
        logits = (
            jnp.einsum("qhe,khe->hqk", query_rows, key_all, preferred_element_type=jnp.float32)
            * scale_value
        )
        logits = jnp.where(allowed[None], logits, -1e30)
        return (query_start, key_start, query_rows, key_all, value_all, logits)

    def forward_block(index):
        _, _, _, _, value_rows, logits = block_pieces(index)
        peak = jnp.max(logits, axis=-1, keepdims=True)
        expo = jnp.exp(logits - peak)
        summed = jnp.sum(expo, axis=-1, keepdims=True)
        probs = (expo / summed).astype(jnp.bfloat16)
        mixed_block = jnp.einsum(
            "hqk,khe->qhe", probs, value_rows, preferred_element_type=jnp.float32
        )
        return (mixed_block.astype(jnp.bfloat16), (peak + jnp.log(summed))[..., 0])

    mixed_blocks, log_totals = lax.map(forward_block, jnp.arange(blocks_count, dtype=jnp.int32))
    mixed = mixed_blocks.reshape(total, local_width)
    attn_full = lax.psum_scatter(
        jnp.dot(mixed, w_out, preferred_element_type=jnp.float32),
        "tp",
        scatter_dimension=0,
        tiled=True,
    ) + bias_out.astype(jnp.float32)
    resid = tokens.astype(jnp.float32) + alpha_attn * attn_full
    resid_low = resid.astype(jnp.bfloat16)
    cot_float = cotangent.astype(jnp.float32)
    ffn_grad_low = (alpha_ffn * cot_float).astype(jnp.bfloat16)
    resid_all = lax.all_gather(resid_low, "tp", axis=0, tiled=True)
    pre_act = jnp.dot(resid_all, w_up, preferred_element_type=jnp.float32) + bias_up.astype(
        jnp.float32
    )
    act_low = jax.nn.gelu(pre_act).astype(jnp.bfloat16)
    ffn_out = lax.psum_scatter(
        jnp.dot(act_low, w_down, preferred_element_type=jnp.float32),
        "tp",
        scatter_dimension=0,
        tiled=True,
    )
    ffn_grad_all = lax.all_gather(ffn_grad_low, "tp", axis=0, tiled=True)
    grad_w_down = contract_rows(act_low, ffn_grad_all)
    grad_pre = gelu_grad(pre_act, contract_cols(ffn_grad_all, w_down)).astype(jnp.bfloat16)
    grad_w_up = contract_rows(resid_all, grad_pre)
    grad_bias_up = jnp.sum(grad_pre.astype(jnp.float32), axis=0)
    grad_resid_ffn = lax.psum_scatter(
        contract_cols(grad_pre, w_up), "tp", scatter_dimension=0, tiled=True
    )
    ffn_full = ffn_out + bias_down.astype(jnp.float32)
    out = (resid + alpha_ffn * ffn_full).astype(jnp.bfloat16)
    grad_alpha_ffn = jnp.sum(cot_float * ffn_full)
    grad_bias_down = alpha_ffn * jnp.sum(cot_float, axis=0)
    grad_resid = cot_float + grad_resid_ffn
    grad_alpha_attn = jnp.sum(grad_resid * attn_full)
    grad_bias_out = alpha_attn * jnp.sum(grad_resid, axis=0)
    attn_grad_low = (alpha_attn * grad_resid).astype(jnp.bfloat16)
    attn_grad_all = lax.all_gather(attn_grad_low, "tp", axis=0, tiled=True)
    grad_w_out = contract_rows(mixed, attn_grad_all)
    grad_mixed = (
        contract_cols(attn_grad_all, w_out)
        .astype(jnp.bfloat16)
        .reshape(total, local_heads, HEAD_DIM)
    )

    def backward_block(carry, index):
        grad_keys, grad_values = carry
        query_start, key_start, query_rows, key_rows, value_rows, logits = block_pieces(index)
        block_totals = lax.dynamic_index_in_dim(log_totals, index, 0, keepdims=False)
        probs = jnp.exp(logits - block_totals[:, :, None])
        upstream = lax.dynamic_slice_in_dim(grad_mixed, query_start, block, 0)
        grad_probs = jnp.einsum(
            "qhe,khe->hqk", upstream, value_rows, preferred_element_type=jnp.float32
        )
        row_terms = jnp.sum(probs * grad_probs, axis=-1, keepdims=True)
        grad_logits = (probs * (grad_probs - row_terms)).astype(jnp.bfloat16)
        grad_query_block = (
            jnp.einsum("hqk,khe->qhe", grad_logits, key_rows, preferred_element_type=jnp.float32)
            * scale_value
        )
        key_part = (
            jnp.einsum("hqk,qhe->khe", grad_logits, query_rows, preferred_element_type=jnp.float32)
            * scale_value
        )
        value_part = jnp.einsum(
            "hqk,qhe->khe", probs.astype(jnp.bfloat16), upstream, preferred_element_type=jnp.float32
        )
        grad_keys = grad_keys + key_part
        grad_values = grad_values + value_part
        return ((grad_keys, grad_values), grad_query_block)

    zero_grads = jnp.zeros((total, local_heads, HEAD_DIM), jnp.float32)
    (grad_keys, grad_values), grad_query_blocks = lax.scan(
        backward_block, (zero_grads, zero_grads), jnp.arange(blocks_count, dtype=jnp.int32)
    )
    grad_proj = jnp.stack(
        [
            grad_query_blocks.reshape(total, local_width),
            grad_keys.reshape(total, local_width),
            grad_values.reshape(total, local_width),
        ]
    ).astype(jnp.bfloat16)
    grad_w_qkv = jnp.einsum("td,ctf->cdf", gathered, grad_proj, preferred_element_type=jnp.float32)
    grad_bias_qv = jnp.stack(
        [
            jnp.sum(grad_proj[0].astype(jnp.float32), axis=0),
            jnp.sum(grad_proj[2].astype(jnp.float32), axis=0),
        ]
    )
    grad_in_attn = lax.psum_scatter(
        jnp.einsum("ctf,cdf->td", grad_proj, w_qkv, preferred_element_type=jnp.float32),
        "tp",
        scatter_dimension=0,
        tiled=True,
    )
    grad_tokens = (grad_resid + grad_in_attn).astype(jnp.bfloat16)
    summed = lax.psum(
        (grad_w_qkv, grad_bias_qv, grad_w_out, grad_w_up, grad_bias_up, grad_w_down), "dp"
    )
    small = lax.psum(
        (grad_bias_out, grad_bias_down, jnp.stack([grad_alpha_attn, grad_alpha_ffn])), ("dp", "tp")
    )
    return (
        out,
        grad_tokens,
        summed[0],
        summed[1],
        summed[2],
        small[0],
        summed[3],
        summed[4],
        summed[5],
        small[1],
        small[2],
    )


def solution(mesh):
    step = local
    if mesh.shape["tp"] == 2 and mesh.shape["dp"] == 16:
        step = functools.partial(paired_local, n_dp=mesh.shape["dp"])
    return jax.shard_map(
        step,
        mesh=mesh,
        in_specs=(
            P(("dp", "tp"), None),
            P("dp"),
            P(None, None, "tp"),
            P(None, "tp"),
            P("tp", None),
            P(),
            P(None, "tp"),
            P("tp"),
            P("tp", None),
            P(),
            P(),
            P(("dp", "tp"), None),
        ),
        out_specs=(
            P(("dp", "tp"), None),
            P(("dp", "tp"), None),
            P(None, None, "tp"),
            P(None, "tp"),
            P("tp", None),
            P(),
            P(None, "tp"),
            P("tp"),
            P("tp", None),
            P(),
            P(),
        ),
        check_vma=False,
    )
```

```python
import functools

import jax
import jax.numpy as jnp
from jax import lax
from jax.experimental import pallas as pl
from jax.experimental.pallas import tpu as pltpu
from jax.sharding import PartitionSpec as P

HEAD_DIM = 64
SHORT = 1024
LOG2E = 1.4426950408889634
F32 = jnp.float32
BF16 = jnp.bfloat16
NT = (((1,), (1,)), ((), ()))
TN = (((0,), (0,)), ((), ()))
AXES = ("dp", "tp")
BIG = 1e30
PIECES = 8


def dot(left, right, dims=None):
    if dims is None:
        return jnp.dot(left, right, preferred_element_type=F32)
    return lax.dot_general(left, right, dims, preferred_element_type=F32)


def in_vmem():
    return pl.BlockSpec(memory_space=pltpu.VMEM)


def in_smem():
    return pl.BlockSpec(memory_space=pltpu.SMEM)


def in_place():
    return pl.BlockSpec(memory_space=pl.ANY)


def fill_pack(flags, pack_ref, own_ref, first_ref, second_ref):
    same, side = flags[3] > 0, flags[4] == 0
    size = first_ref.shape[0]
    first, second = first_ref[...], second_ref[...]
    pack_ref[:size] = jnp.where(same, own_ref[:size], jnp.where(side, first, second))
    pack_ref[size:] = jnp.where(same, own_ref[size:], jnp.where(side, second, first))


def lower_half(which, rows):
    zeros = jnp.zeros_like(rows)
    return jnp.where(
        which == 0, jnp.concatenate([rows, zeros], 0), jnp.concatenate([zeros, rows], 0)
    )


def unpacked(pack_ref, which, width):
    rows = pack_ref.shape[1] // 2
    at = slice(which * rows, which * rows + rows)
    return pack_ref[at, :width], pack_ref[at, width : 2 * width]


def attend_kernel(
    flags, mine_ref, other_ref, own_pack_ref, first_ref, second_ref, bias_ref, came_bias_ref,
    q_t_out, k_t_out, k_out, v_out, keep_ref, send_ref, lse_ref,
    v_t, mixed, scores, pack_ref, q_t_ref, k_t_ref, k_ref, v_ref, done, *, block,
):
    core, longs = flags[0], flags[2]
    fill_pack(flags, pack_ref, own_pack_ref, first_ref, second_ref)
    half = mine_ref.shape[0]
    total = 2 * half
    width = pack_ref.shape[1] // 2
    deep = pack_ref.shape[1] // 2
    pairs = width // 128
    heads = width // HEAD_DIM
    turned = [jnp.concatenate([p.T for p in unpacked(pack_ref, i, width)], 1) for i in range(3)]
    bias = jnp.where(flags[3] > 0, bias_ref[...], came_bias_ref[...]).astype(F32)[0:8]
    column = bias.T[:, 0:1]

    def project(rows_ref, which):
        at = pl.ds(pl.multiple_of(which * half, half), half)
        rows = rows_ref[...]
        q_t_ref[:, at] = (dot(turned[0], rows, NT) + column[:width]).astype(BF16)
        k_t_ref[:, at] = dot(turned[1], rows, NT).astype(BF16)
        v_t[:, at] = (dot(turned[2], rows, NT) + column[width:]).astype(BF16)
        for i, target in ((1, k_ref), (2, v_ref)):
            upper, lower = unpacked(pack_ref, i, width)
            for pair in range(pairs):
                cols = slice(pair * 128, pair * 128 + 128)
                part = dot(rows[:, :deep], upper[:, cols]) + dot(rows[:, deep:], lower[:, cols])
                if i == 2:
                    part = part + bias[0:1, width + pair * 128 : width + pair * 128 + 128]
                target[pair, at, :] = part.astype(BF16)

    project(mine_ref, core)
    project(other_ref, 1 - core)
    copies = [
        pltpu.make_async_copy(source, target, done.at[i])
        for i, (source, target) in enumerate(
            ((q_t_ref, q_t_out), (k_t_ref, k_t_out), (k_ref, k_out), (v_ref, v_out))
        )
    ]
    for copy in copies:
        copy.start()
    row = lax.broadcasted_iota(jnp.int32, (block, block), 0)
    col = lax.broadcasted_iota(jnp.int32, (block, block), 1)
    scale = HEAD_DIM ** (-0.5) * LOG2E

    def one_head(head, _):
        at = pl.ds(pl.multiple_of(head * HEAD_DIM, HEAD_DIM), HEAD_DIM)
        pair, which = head // 2, head % 2
        for q0 in range(0, total, block):
            queries = lower_half(which, q_t_ref[at, q0 : q0 + block])
            peak = jnp.full((8, block), -BIG, F32)
            for k0 in range(0, q0 + block, block):
                s = dot(k_ref[pair, k0 : k0 + block, :], queries)
                if k0 == q0:
                    s = jnp.where(row <= col, s, -BIG)
                scores[k0 : k0 + block, :] = s
                top = jnp.max(s.reshape(block // 8, 8, block), 0)
                if q0 >= SHORT > k0:
                    top = jnp.where(longs > 0, top, -BIG)
                peak = jnp.maximum(peak, top)
            peak = jnp.max(peak, 0, keepdims=True) * scale
            acc = jnp.zeros((HEAD_DIM, block), F32)
            norm = jnp.zeros((8, block), F32)
            for k0 in range(0, q0 + block, block):
                base = peak
                if q0 >= SHORT > k0:
                    base = jnp.where(longs > 0, peak, BIG)
                e = jnp.exp2(scores[k0 : k0 + block, :] * scale - base)
                norm = norm + jnp.sum(e.reshape(block // 8, 8, block), 0)
                acc = acc + dot(v_t[at, k0 : k0 + block], e.astype(BF16))
            norm = jnp.sum(norm, 0, keepdims=True)
            mixed[q0 // half, at, q0 % half : q0 % half + block] = (acc / norm).astype(BF16)
            lse_ref[head, :, q0 : q0 + block] = jnp.broadcast_to(
                peak + jnp.log2(norm), (8, block)
            )
        return 0

    lax.fori_loop(0, heads, one_head, 0)
    keep_ref[...] = mixed[core]
    send_ref[...] = mixed[1 - core]
    for copy in copies:
        copy.wait()


def attend(flags, mine, other, own_pack, first, second, bias, came_bias):
    half = mine.shape[0]
    total, width = 2 * half, own_pack.shape[1] // 2
    shape = jax.ShapeDtypeStruct
    block = 512
    return pl.pallas_call(
        functools.partial(attend_kernel, block=block),
        out_shape=(
            shape((width, total), BF16),
            shape((width, total), BF16),
            shape((width // 128, total, 128), BF16),
            shape((width // 128, total, 128), BF16),
            shape((width, half), BF16),
            shape((width, half), BF16),
            shape((width // HEAD_DIM, 8, total), F32),
        ),
        in_specs=[in_smem()] + [in_vmem()] * 7,
        out_specs=(in_place(),) * 4 + (in_vmem(),) * 3,
        scratch_shapes=[
            pltpu.VMEM((width, total), BF16),
            pltpu.VMEM((2, width, half), BF16),
            pltpu.VMEM((total, block), F32),
            pltpu.VMEM(own_pack.shape, BF16),
            pltpu.VMEM((width, total), BF16),
            pltpu.VMEM((width, total), BF16),
            pltpu.VMEM((width // 128, total, 128), BF16),
            pltpu.VMEM((width // 128, total, 128), BF16),
            pltpu.SemaphoreType.DMA((4,)),
        ],
        compiler_params=pltpu.CompilerParams(vmem_limit_bytes=18 << 20),
        cost_estimate=pl.CostEstimate(
            flops=0, bytes_accessed=0, transcendentals=0
        ),
    )(flags, mine, other, own_pack, first, second, bias, came_bias)


def feed_kernel(
    flags, alphas, tok_ref, own_cot_ref, came_cot_ref, keep_ref, recv_ref, wout_ref, bias_ref,
    bup_ref, up_in, down_in, near_up_in, far_up_in, near_down_in, far_down_in,
    out_ref, dresid_ref, dkeep_ref, dsend_ref, gkeep_a_ref, gkeep_b_ref, gsend_a_ref, gsend_b_ref,
    mixed, dmixed, attn, resid, ffn, act, dpre, small, cot_ref,
    up_ref, down_ref, near_up, far_up, near_down, far_down, done, *, piece,
):
    core, same = flags[0], flags[3]
    rows, width = tok_ref.shape
    copies = [
        pltpu.make_async_copy(source, target, done.at[i])
        for i, (source, target) in enumerate(
            (
                (near_down_in, near_down), (far_down_in, far_down), (up_in, up_ref),
                (down_in, down_ref), (near_up_in, near_up), (far_up_in, far_up),
            )
        )
    ]
    for copy in copies:
        copy.start()
    side, deep = flags[4], flags[5]
    main = gkeep_a_ref.shape[2] - 8
    unit = up_ref.shape[1] // 2
    part = wout_ref.shape[0] // 2
    a_attn, a_ffn = alphas[0], alphas[1]
    cot_ref[...] = jnp.where(same > 0, own_cot_ref[...], came_cot_ref[...])
    biases = bias_ref[...].astype(F32)
    own_bup = bup_ref[...].astype(F32)
    mixed[1 - same] = keep_ref[...]
    mixed[same] = recv_ref[...]

    def own_sub(j):
        return core if j == 0 else 1 - core

    def place_of(h, j, piece_at):
        y = 1 - side if (piece_at // 2) % 2 else side
        z = 1 - deep if piece_at % 2 else deep
        if piece_at < PIECES // 2:
            return (gkeep_a_ref, gsend_a_ref)[j].at[h, 2 * y + z]
        return (gkeep_b_ref, gsend_b_ref)[j].at[y, 2 * h + z]

    def put(h, j, start, value):
        value = value.astype(BF16)
        at = 0
        while at < value.shape[0]:
            piece_at, row = divmod(start + at, main)
            size = min(main - row, value.shape[0] - at)
            place_of(h, j, piece_at)[row : row + size, :] = value[at : at + size]
            at += size

    def wout_part(h, j):
        if h == 0:
            return wout_ref[pl.ds(pl.multiple_of(own_sub(j) * part, part), part), :]
        return (near_down, far_down)[j][unit : unit + part, :]

    def mixed_part(h, j):
        return mixed[h, pl.ds(pl.multiple_of(own_sub(j) * part, part), part), :]

    copies[0].wait()
    copies[1].wait()
    total = dot(mixed_part(0, 0), wout_part(0, 0), TN)
    for h, j in ((0, 1), (1, 0), (1, 1)):
        total = total + dot(mixed_part(h, j), wout_part(h, j), TN)
    attn[...] = total + biases[1:2]
    resid[...] = tok_ref[...].astype(F32) + a_attn * attn[...]
    low = resid[...].astype(BF16)
    low_t = low.T
    dffn = (cot_ref[...].astype(F32) * a_ffn).astype(BF16)
    dffn_t = dffn.T
    dresid_ref[...] = cot_ref[...].astype(F32)
    ffn[...] = jnp.broadcast_to(biases[2:3], ffn.shape)
    for h in range(2):
        copies[2 + 2 * h].wait()
        copies[3 + 2 * h].wait()
        for j in range(2):
            sub = pl.ds(pl.multiple_of(own_sub(j) * unit, unit), unit)
            if h == 0:
                up, down = up_ref[:, sub], down_ref[sub, :]
            else:
                source = (near_up, far_up)[j]
                up, down = source[:unit, :], (near_down, far_down)[j][:unit, :]
            if h == 0:
                bias = jnp.where(own_sub(j) == 0, own_bup[1:2], own_bup[2:3])
            else:
                bias = source[unit : unit + 16, :].astype(F32)[0:1]
            bias_grad = jnp.zeros((8, unit), F32)
            for r0 in range(0, rows, piece):
                at = slice(r0, r0 + piece)
                u = dot(low[at], up) + bias
                square = u * u
                t = jnp.tanh(u * (0.7978845608028654 + 0.035677408136300125 * square))
                s = 0.5 + 0.5 * t
                slope = s + (0.5 * u) * (1.0 - t * t) * (
                    0.7978845608028654 + 0.10703222440890037 * square
                )
                act[at, :] = (u * s).astype(BF16)
                d = dot(dffn[at], down, NT) * slope
                d_low = d.astype(BF16)
                dpre[at, :] = d_low
                bias_grad = bias_grad + jnp.sum(
                    d_low.astype(F32).reshape(piece // 8, 8, unit), 0
                )
                ffn[at, :] += dot(act[at, :], down)
                dresid_ref[at, :] += dot(d_low, up, NT)
            put(h, j, 0, dot(low_t, dpre[...]))
            put(h, j, unit, dot(dffn_t, act[...]).T)
            small[2 * h + j, :] = jnp.sum(bias_grad, 0)
    g = cot_ref[...].astype(F32)
    out_ref[...] = (resid[...] + a_ffn * ffn[...]).astype(BF16)
    dresid = dresid_ref[...]
    bias_down = a_ffn * jnp.sum(g, 0, keepdims=True)
    bias_out = a_attn * jnp.sum(dresid, 0, keepdims=True)
    sums = [
        jnp.sum(jnp.sum(v, 0, keepdims=True), 1, keepdims=True)
        for v in (dresid * attn[...], g * ffn[...])
    ]
    lane = lax.broadcasted_iota(jnp.int32, (1, width), 1)
    both = jnp.where(lane == 0, sums[0], jnp.where(lane == 1, sums[1], 0.0))
    dattn = (a_attn * dresid).astype(BF16)
    for h in range(2):
        for j in range(2):
            put(h, j, 2 * unit, dot(mixed_part(h, j), dattn))
            dmixed[h, pl.ds(pl.multiple_of(own_sub(j) * part, part), part), :] = dot(
                wout_part(h, j), dattn, NT
            ).astype(BF16)
            exact = jnp.concatenate(
                [small[2 * h + j : 2 * h + j + 1, :], bias_down, bias_out, both], 0
            )
            high = exact.astype(BF16).astype(F32)
            for i in range(1, PIECES):
                place_of(h, j, i)[main:, :] = jnp.zeros((8, width), BF16)
            place_of(h, j, 0)[main:, :] = jnp.concatenate([high, exact - high], 0).astype(BF16)
    dkeep_ref[...] = dmixed[1 - same]
    dsend_ref[...] = dmixed[same]


def feed(
    flags, alphas, tok, own_cot, came_cot, keep, recv, up, down, wout, near_up, far_up,
    near_down, far_down, bias, bias_up,
):
    rows, width = tok.shape
    unit = up.shape[1] // 2
    half_width = keep.shape[0]
    shape = jax.ShapeDtypeStruct

    piece = shape((2, PIECES // 2, (2 * unit + half_width // 2) // PIECES + 8, width), BF16)
    outs = (
        shape((rows, width), BF16),
        shape((rows, width), F32),
        shape((half_width, rows), BF16),
        shape((half_width, rows), BF16),
        piece,
        piece,
        piece,
        piece,
    )
    values = (tok, own_cot, came_cot, keep, recv, wout, bias, bias_up)
    later = (up, down, near_up, far_up, near_down, far_down)
    return pl.pallas_call(
        functools.partial(feed_kernel, piece=256),
        out_shape=outs,
        in_specs=[in_smem()] * 2
        + [in_vmem()] * len(values)
        + [in_place()] * len(later),
        out_specs=(in_vmem(),) * len(outs),
        scratch_shapes=[
            pltpu.VMEM((2, half_width, rows), BF16),
            pltpu.VMEM((2, half_width, rows), BF16),
            pltpu.VMEM((rows, width), F32),
            pltpu.VMEM((rows, width), F32),
            pltpu.VMEM((rows, width), F32),
            pltpu.VMEM((rows, unit), BF16),
            pltpu.VMEM((rows, unit), BF16),
            pltpu.VMEM((8, unit), F32),
            pltpu.VMEM((rows, width), BF16),
            *(pltpu.VMEM(x.shape, BF16) for x in later),
            pltpu.SemaphoreType.DMA((len(later),)),
        ],
        compiler_params=pltpu.CompilerParams(vmem_limit_bytes=28 << 20),
        cost_estimate=pl.CostEstimate(
            flops=0, bytes_accessed=0, transcendentals=0
        ),
    )(flags, alphas, *values, *later)


def attend_back_kernel(
    flags, mine_in, other_in, q_t_ref, k_t_ref, k_ref, v_ref, keep_ref, send_ref,
    dkeep_ref, drecv_ref, lse_ref, *refs, block, pair,
):
    if pair:
        before_ref, sums_all, *refs = refs
        sums_all[0] = before_ref[...]
        sums_ref = sums_all.at[1]
    else:
        sums_ref, *refs = refs
    grads, mixed, dmixed, probs, dscores, mine_ref, other_ref, done = refs
    core, longs = flags[0], flags[2]
    half = mine_ref.shape[0]
    total = 2 * half
    copies = [
        pltpu.make_async_copy(mine_in, mine_ref, done.at[0]),
        pltpu.make_async_copy(other_in, other_ref, done.at[1]),
    ]
    for copy in copies:
        copy.start()
    mixed[core] = keep_ref[...]
    mixed[1 - core] = send_ref[...]
    dmixed[core] = dkeep_ref[...]
    dmixed[1 - core] = drecv_ref[...]
    factor = HEAD_DIM ** (-0.5)
    scale = factor * LOG2E
    part = block // 2

    def one_head(which, _):
        at = pl.ds(pl.multiple_of(which * HEAD_DIM, HEAD_DIM), HEAD_DIM)
        for q0 in range(0, total, block):
            here = slice(q0 % half, q0 % half + block)
            do = dmixed[q0 // half, at, here]
            queries = lower_half(which, q_t_ref[at, q0 : q0 + block])
            upstream = lower_half(which, do)
            lse = lse_ref[which, 0:1, q0 : q0 + block]
            mean = jnp.sum(
                do.astype(F32) * mixed[q0 // half, at, here].astype(F32), 0, keepdims=True
            )
            pieces = [(k0, block, 0) for k0 in range(0, q0, block)]
            pieces += [(q0, part, 0), (q0 + part, part, part)]
            for k0, size, skip in pieces:
                keys, cols = slice(k0, k0 + size), slice(q0 + skip, q0 + block)
                base = lse
                if q0 >= SHORT > k0:
                    base = jnp.where(longs > 0, lse, BIG)
                s = dot(k_ref[0, keys, :], queries[:, skip:])
                dp = dot(v_ref[0, keys, :], upstream[:, skip:])
                p = jnp.exp2(s * scale - base[:, skip:])
                if k0 >= q0:
                    row = lax.broadcasted_iota(jnp.int32, p.shape, 0) + k0
                    col = lax.broadcasted_iota(jnp.int32, p.shape, 1) + (q0 + skip)
                    p = jnp.where(row <= col, p, 0.0)
                probs[keys, cols] = p.astype(BF16)
                dscores[keys, cols] = (p * (dp - mean[:, skip:])).astype(BF16)
                if skip:
                    probs[keys, q0 : q0 + skip] = jnp.zeros((size, skip), BF16)
                    dscores[keys, q0 : q0 + skip] = jnp.zeros((size, skip), BF16)
            end = q0 + block
            grads[0, at, q0:end] = (
                dot(k_t_ref[at, 0:end], dscores[0:end, q0:end]) * factor
            ).astype(BF16)
        for k0 in range(0, total, block):
            keys = slice(k0, k0 + block)
            grads[1, at, keys] = (
                dot(q_t_ref[at, k0:], dscores[keys, k0:], NT) * factor
            ).astype(BF16)
            first = k0 // half
            acc = dot(dmixed[first, at, k0 % half :], probs[keys, k0 : (first + 1) * half], NT)
            if first == 0:
                acc = acc + dot(dmixed[1, at, :], probs[keys, half:], NT)
            grads[2, at, keys] = acc.astype(BF16)
        return 0

    lax.fori_loop(0, 2, one_head, 0)
    for copy in copies:
        copy.wait()
    near = pl.ds(pl.multiple_of(core * half, half), half)
    far = pl.ds(pl.multiple_of((1 - core) * half, half), half)
    main = sums_ref.shape[1] - 16
    deep = mine_ref.shape[1]
    for i in range(3):
        value = (
            dot(grads[i, :, near], mine_ref[...]) + dot(grads[i, :, far], other_ref[...])
        ).T.astype(BF16)
        at = 0
        while at < deep:
            piece, row = divmod(i * deep + at, main)
            size = min(main - row, deep - at)
            sums_ref[piece, row : row + size, :] = value[at : at + size]
            at += size
    ones = jnp.ones((8, total), BF16)
    rest = jnp.zeros((14, 2 * HEAD_DIM), F32)
    sums_ref[0, main:, :] = jnp.concatenate(
        [dot(ones, grads[0], NT)[0:1], dot(ones, grads[2], NT)[0:1], rest], 0
    ).astype(BF16)
    for piece in range(1, sums_ref.shape[0]):
        sums_ref[piece, main:, :] = jnp.zeros((16, 2 * HEAD_DIM), BF16)


def attend_back(pair, before, flags, mine, other, q_t, k_t, k, v, keep, send, dkeep, drecv, lse):
    half, width_all = mine.shape
    total = 2 * half
    shape = jax.ShapeDtypeStruct

    def whole(x):
        return pl.BlockSpec(x.shape, lambda i: (0,) * x.ndim)

    def rows_of(x):
        return pl.BlockSpec((2 * HEAD_DIM, x.shape[1]), lambda i: (pair, 0))

    def pair_of(x):
        return pl.BlockSpec((1,) + x.shape[1:], lambda i: (pair, 0, 0))

    sums = (4, 3 * width_all // 4 + 16, 2 * HEAD_DIM)
    outs = (
        shape((2,) + sums if pair else sums, BF16),
        shape((3, 2 * HEAD_DIM, total), BF16),
    )
    return pl.pallas_call(
        functools.partial(attend_back_kernel, block=512, pair=pair),
        grid=(1,),
        out_shape=outs,
        in_specs=[in_smem(), in_place(), in_place(), rows_of(q_t), rows_of(k_t), pair_of(k),
                  pair_of(v), rows_of(keep), rows_of(send), rows_of(dkeep), rows_of(drecv),
                  pl.BlockSpec((2, 8, total), lambda i: (pair, 0, 0))]
        + [whole(x) for x in before],
        out_specs=tuple(whole(x) for x in outs),
        scratch_shapes=[
            pltpu.VMEM((2, 2 * HEAD_DIM, half), BF16),
            pltpu.VMEM((2, 2 * HEAD_DIM, half), BF16),
            pltpu.VMEM((total, total), BF16),
            pltpu.VMEM((total, total), BF16),
            pltpu.VMEM(mine.shape, BF16),
            pltpu.VMEM(mine.shape, BF16),
            pltpu.SemaphoreType.DMA((2,)),
        ],
        compiler_params=pltpu.CompilerParams(vmem_limit_bytes=24 << 20),
        cost_estimate=pl.CostEstimate(
            flops=0, bytes_accessed=0, transcendentals=0
        ),
    )(flags, mine, other, q_t, k_t, k, v, keep, send, dkeep, drecv, lse, *before)


def inputs_back_kernel(flags, own_pack_ref, first_ref, second_ref, dresid_in, *refs):
    core = flags[0]
    *grads, own_ref, away_ref, pack_ref, dresid_ref, done = refs
    copy = pltpu.make_async_copy(dresid_in, dresid_ref, done)
    copy.start()
    fill_pack(flags, pack_ref, own_pack_ref, first_ref, second_ref)
    half = own_ref.shape[0]
    width = pack_ref.shape[1] // 2

    def back(which):
        at = pl.ds(pl.multiple_of(which * half, half), half)
        result = []
        for part in range(2):
            total = 0.0
            for i in range(3):
                weights = unpacked(pack_ref, i, width)[part]
                stacked = jnp.concatenate([g[i, :, at] for g in grads], 0)
                total = total + dot(weights, stacked)
            result.append(total.T)
        return jnp.concatenate(result, 1)

    away_ref[...] = back(1 - core).astype(BF16)
    result = back(core)
    copy.wait()
    own_ref[...] = dresid_ref[...] + result


def inputs_back(flags, own_pack, first, second, dresid, grads):
    half, width_all = dresid.shape
    shape = jax.ShapeDtypeStruct
    return pl.pallas_call(
        inputs_back_kernel,
        out_shape=(shape((half, width_all), F32), shape((half, width_all), BF16)),
        in_specs=[in_smem()] + [in_vmem()] * 3 + [in_place()] + [in_vmem()] * len(grads),
        out_specs=(in_vmem(),) * 2,
        scratch_shapes=[
            pltpu.VMEM(own_pack.shape, BF16),
            pltpu.VMEM(dresid.shape, F32),
            pltpu.SemaphoreType.DMA,
        ],
        compiler_params=pltpu.CompilerParams(vmem_limit_bytes=12 << 20),
        cost_estimate=pl.CostEstimate(
            flops=0, bytes_accessed=0, transcendentals=0
        ),
    )(flags, own_pack, first, second, dresid, *grads)


def unpack_heads_kernel(flags, mine_ref, came_ref, grad_ref, bias_ref):
    core, side = flags[0], flags[4]
    main = mine_ref.shape[2] - 16
    for far in range(2):
        source = came_ref if far else mine_ref
        for turn in range(2):
            piece = 2 * (1 - core if far else core) + (1 - side if turn else side)
            at = pl.ds(pl.multiple_of(piece * main, main), main)
            for pair in range(source.shape[1]):
                cols = slice(pair * 128, pair * 128 + 128)
                grad_ref[at, cols] = source[turn, pair, :main, :].astype(F32)

            @pl.when(piece == 0)
            def _():
                for pair in range(source.shape[1]):
                    cols = slice(pair * 128, pair * 128 + 128)
                    bias_ref[:, cols] = source[turn, pair, main:, :].astype(F32)[0:2]


def unpack_heads(flags, mine, came, width):
    shape = jax.ShapeDtypeStruct
    main = mine.shape[2] - 16
    return pl.pallas_call(
        unpack_heads_kernel,
        out_shape=(shape((4 * main, width), F32), shape((2, width), F32)),
        in_specs=[in_smem()] + [in_vmem()] * 2,
        out_specs=(in_vmem(),) * 2,
        compiler_params=pltpu.CompilerParams(vmem_limit_bytes=5 << 20),
    )(flags, mine, came)


def unpack_feed_kernel(
    flags, mine_ref, came_ref, up_ref, down_ref, out_ref, bup_ref, bdown_ref, bout_ref,
    alphas_ref, rows_ref, small_ref, *, unit,
):
    core, side, deep = flags[0], flags[4], flags[5]
    main = mine_ref.shape[3] - 8
    for far in range(2):
        source = came_ref if far else mine_ref
        which = 1 - core if far else core
        for turn in range(2):
            for dip in range(2):
                for order in range(2):
                    piece = (
                        4 * order
                        + 2 * (1 - side if turn else side)
                        + (1 - deep if dip else deep)
                    )
                    at = pl.ds(pl.multiple_of(piece * main, 16), main)
                    rows_ref[which, at, :] = source[turn, dip, order, :main, :]
                    if order == 0:

                        @pl.when(piece == 0)
                        def _():
                            both = source[turn, dip, order, main:, :].astype(F32)
                            small_ref[which] = both[0:4] + both[4:8]

    width = small_ref.shape[2]
    for i in range(2):
        bup_ref[i * unit : (i + 1) * unit] = small_ref[i, 0, :]
    bdown_ref[...] = small_ref[0, 1, :]
    bout_ref[...] = small_ref[0, 2, :]
    last = small_ref[0, 3:4, :]
    lane = lax.broadcasted_iota(jnp.int32, (1, width), 1)
    for i in range(2):
        alphas_ref[i] = jnp.sum(jnp.where(lane == i, last, 0.0))
    for i in range(2):
        up_ref[:, i * unit : (i + 1) * unit] = rows_ref[i, :unit, :].astype(F32)
        down_ref[i * unit : (i + 1) * unit, :] = rows_ref[i, unit : 2 * unit, :].astype(F32)
        part = rows_ref.shape[1] - 2 * unit
        out_ref[i * part : (i + 1) * part, :] = rows_ref[i, 2 * unit :, :].astype(F32)


def unpack_feed(flags, mine, came, unit):
    shape = jax.ShapeDtypeStruct
    main, width = mine.shape[3] - 8, mine.shape[4]
    return pl.pallas_call(
        functools.partial(unpack_feed_kernel, unit=unit),
        out_shape=(
            shape((width, 2 * unit), F32),
            shape((2 * unit, width), F32),
            shape((2 * (PIECES * main - 2 * unit), width), F32),
            shape((2 * unit,), F32),
            shape((width,), F32),
            shape((width,), F32),
            shape((2,), F32),
        ),
        in_specs=[in_smem()] + [in_vmem()] * 2,
        out_specs=(in_vmem(),) * 6 + (in_smem(),),
        scratch_shapes=[
            pltpu.VMEM((2, PIECES * main, width), BF16),
            pltpu.VMEM((2, 4, width), F32),
        ],
        compiler_params=pltpu.CompilerParams(vmem_limit_bytes=10 << 20),
    )(flags, mine, came)


def add_low(values):
    total = values[0].astype(F32)
    for value in values[1:]:
        total = total + value.astype(F32)
    return total.astype(BF16)


def take(value, *picks):
    block, index = [], []
    for axis in range(value.ndim - 2):
        what = picks[axis] if axis < len(picks) else None
        if what is None:
            what = (0, value.shape[axis])
        elif isinstance(what, int):
            what = (what, 1)
        block.append(what[1])
        index.append(what[0])
    return value, tuple(block) + value.shape[-2:], tuple(index) + (0, 0)


def sum_kernel(*refs, plan, n_in):
    ins, outs = refs[:n_in], refs[n_in:]

    def terms(total):
        exact = total[0:4] + total[4:8]
        high = exact.astype(BF16).astype(F32)
        return jnp.concatenate([high, exact - high], 0)

    for out, groups in zip(outs, plan):
        at = 0
        main = out.shape[-2] - 8
        for members, alike in groups:
            lead = 1
            for size in ins[members[0]].shape[:-2]:
                lead *= size
            for i in range(lead):
                total, rows = None, None
                for n, member in enumerate(members):
                    ref = ins[member]
                    index, rest = [], i
                    for size in reversed(ref.shape[:-2]):
                        index.insert(0, rest % size)
                        rest //= size
                    value = ref[tuple(index)].astype(F32)
                    top, low = value[:main], value[main:]
                    total = top if total is None else total + top
                    rows = low if rows is None else rows + low
                    if n + 1 == alike:
                        rows = terms(rows).astype(BF16).astype(F32)
                out[at, :main, :] = total.astype(BF16)
                out[at, main:, :] = terms(rows).astype(BF16)
                at += 1


def sum_pieces(*outs):
    blocks, plan, shapes = [], [], []
    for groups in outs:
        lead, steps = 0, []
        for members, alike in groups:
            steps.append((tuple(range(len(blocks), len(blocks) + len(members))), alike))
            blocks.extend(members)
            count = 1
            for size in members[0][1][:-2]:
                count *= size
            lead += count
        plan.append(tuple(steps))
        shapes.append(jax.ShapeDtypeStruct((lead,) + groups[0][0][0][1][-2:], BF16))
    return pl.pallas_call(
        functools.partial(sum_kernel, plan=tuple(plan), n_in=len(blocks)),
        grid=(1,),
        out_shape=tuple(shapes),
        in_specs=[pl.BlockSpec(block, lambda i, at=at: at) for _, block, at in blocks],
        out_specs=tuple(pl.BlockSpec(x.shape, lambda i: (0, 0, 0)) for x in shapes),
        compiler_params=pltpu.CompilerParams(vmem_limit_bytes=5 << 20),
        cost_estimate=pl.CostEstimate(flops=0, bytes_accessed=0, transcendentals=0),
    )(*(value for value, _, _ in blocks))


def pick(value, side, axis):
    size = value.shape[axis] // 2
    return lax.dynamic_slice_in_dim(value, side * size, size, axis)


def paired_local(
    tokens, long_docs, w_qkv, bias_qv, w_out, bias_out, w_up, bias_up, w_down, bias_down, alphas,
    cotangent, *, n_dp,
):
    devices = 2 * n_dp
    place = lax.axis_index("tp")
    row_index = lax.axis_index("dp")
    core = row_index % 2
    same = (core == place).astype(jnp.int32)
    is_same = core == place

    def swapped(i):
        return (i & ~3) | ((i & 1) << 1) | ((i >> 1) & 1)

    def trade(value):
        pairs = [(i, swapped(i)) for i in range(devices) if i != swapped(i)]
        return lax.ppermute(value, AXES, pairs)

    def cross(value, bit):
        return lax.ppermute(value, AXES, [(i, i ^ bit) for i in range(devices)])

    def collect(value):
        return lax.ppermute(
            value, AXES, [(i, i ^ 1) for i in range(devices) if (i & 1) != (i >> 1) & 1]
        )

    PLACE, CORE, NEXT = 1, 2, 4
    side = (row_index // 2) % 2
    outer = []
    bit = 8
    while bit < devices:
        outer.append((bit, (row_index // (bit // 2)) % 2))
        bit *= 2

    width_all, half_qkv = w_qkv.shape[1:]
    unit = w_up.shape[1] // 2
    part = w_out.shape[0] // 2
    tie = lax.optimization_barrier
    longs = jnp.where(is_same, long_docs, cross(long_docs, CORE))[0]
    flags = jnp.stack([core, place, longs, same, side, outer[0][1]]).astype(jnp.int32)
    small = tie(
        jnp.concatenate(
            [bias_qv.reshape(1, -1), bias_out[None], bias_down[None],
             jnp.zeros((13, width_all), BF16)], 0,
        )
    )
    own_pack = jnp.concatenate(
        [w_qkv[:, : width_all // 2], w_qkv[:, width_all // 2 :]], 2
    ).reshape(-1, 2 * half_qkv)
    small_up = tie(
        jnp.concatenate(
            [lax.dynamic_slice_in_dim(bias_up, core * unit, unit, 0)[None],
             bias_up.reshape(2, unit), jnp.zeros((13, unit), BF16)], 0,
        )
    )
    packed_up = jnp.concatenate(
        [lax.dynamic_slice_in_dim(w_up, core * unit, unit, 1), small_up], 0
    )
    packed_down = jnp.concatenate(
        [
            lax.dynamic_slice_in_dim(w_down, core * unit, unit, 0),
            lax.dynamic_slice_in_dim(w_out, core * part, part, 0),
        ],
        0,
    )
    came, first, came_small = trade(tokens), trade(pick(own_pack, side, 0)), trade(small)
    came, first, came_small, packed_up, packed_down, cotangent_tied, flags = tie(
        (came, first, came_small, packed_up, packed_down, cotangent, flags)
    )
    second = lax.ppermute(
        first, AXES, [(i, i ^ NEXT) for i in range(devices) if (i & 1) != (i >> 1) & 1]
    )
    near_up, near_down = cross(packed_up, PLACE), cross(packed_down, PLACE)
    came_cot = trade(cotangent_tied)
    mine = jnp.where(is_same, tokens, came)
    other = cross(mine, CORE)
    q_t, k_t, k, v, keep, send, lse = attend(
        flags, mine, other, own_pack, first, second, small, came_small
    )
    near_up, near_down, send = tie((near_up, near_down, send))
    far_up, far_down = cross(near_up, CORE), cross(near_down, CORE)
    recv = cross(send, CORE)
    out, dresid, dkeep, dsend, keep_a, keep_b, send_a, send_b = feed(
        flags, alphas, mine, cotangent, came_cot, keep, recv, w_up, w_down, w_out, near_up, far_up,
        near_down, far_down, small, small_up,
    )
    drecv = cross(dsend, CORE)
    back_args = (flags, mine, other, q_t, k_t, k, v, keep, send, dkeep, drecv, lse)

    other_a, other_b = cross(send_a, CORE), cross(send_b, CORE)
    give_a, give_b = sum_pieces(
        [([take(keep_a, 1), take(other_a, 1)], 0)], [([take(keep_b, 1), take(other_b, 1)], 0)]
    )
    back_args, give_a, give_b = tie((back_args, give_a, give_b))
    got_a, got_b = cross(give_a, PLACE), cross(give_b, NEXT)
    sums_0, grads_0 = attend_back(0, (), *back_args)
    stay_a, give_a, give_b = sum_pieces(
        *(
            [
                ([take(keep_a, 0, (i, 2)), take(other_a, 0, (i, 2)), take(got_a, (i, 2))], 2)
            ]
            for i in range(2)
        ),
        [([take(keep_b, 0, (1, 2)), take(other_b, 0, (1, 2)), take(got_b, (1, 2))], 0)],
    )
    back_args, give_a, give_b, sums_0 = tie((back_args, give_a, give_b, sums_0))
    got_a, got_b2 = cross(give_a, NEXT), cross(give_b, PLACE)
    sums, grads_1 = attend_back(1, (sums_0,), *back_args)
    stay, give = sum_pieces(
        *(
            [
                ([take(stay_a, i), take(got_a, i)], 0),
                ([take(keep_b, 0, i), take(other_b, 0, i), take(got_b, i), take(got_b2, i)], 0),
            ]
            for i in range(2)
        )
    )
    grads_0, give, sums = tie((grads_0, give, sums))
    got = cross(give, outer[0][0])
    got_sums = collect(sums)
    own, away = inputs_back(flags, own_pack, first, second, dresid, (grads_0, grads_1))
    got, got_sums, own, away = tie((got, got_sums, own, away))

    (value,) = sum_pieces([([take(stay), take(got)], 0)])
    stay_q, give_q = (
        add_low([pick(p, i, 1) for p in (sums, got_sums)]) for i in (core, 1 - core)
    )
    heads = jnp.where(is_same, stay_q, cross(give_q, CORE))
    grad_tokens = (own + cross(away, CORE).astype(F32)).astype(BF16)
    value, give_q, grad_tokens = tie((value, pick(heads, 1 - side, 1), grad_tokens))
    low_bit, high_bit = outer[0][0], outer[1][0]
    halves = [value[:1], value[1:]]
    got_half = cross(halves[0], high_bit)
    got_q = cross(give_q, NEXT)
    tokens_came = trade(grad_tokens)
    heads = add_low([pick(heads, side, 1), got_q])[:, 0]
    got_half, heads, out = tie((got_half, heads, out))
    out_came = trade(out)
    got_other = cross(halves[1], high_bit)
    heads = add_low([heads, cross(heads, low_bit)])
    (value,) = sum_pieces(
        [([take(halves[0]), take(got_half)], 0), ([take(halves[1]), take(got_other)], 0)]
    )
    value, heads = tie((value, heads))
    along, beside = cross(value, low_bit), cross(value, NEXT)
    heads = add_low([heads, cross(heads, high_bit)])
    along, beside, heads, tokens_came, out_came = tie(
        (along, beside, heads, tokens_came, out_came)
    )
    corner = cross(along, NEXT)
    heads_next = cross(heads, NEXT)
    out = jnp.where(is_same, out, out_came)
    grad_tokens = jnp.where(is_same, grad_tokens, tokens_came)
    corner, heads_next, out, grad_tokens = tie((corner, heads_next, out, grad_tokens))
    value = jnp.stack([jnp.stack([value, along]), jnp.stack([beside, corner])])
    heads = jnp.stack([heads, heads_next])
    value, heads = tie((value, heads))
    heads_came, value_came = cross(heads, CORE), cross(value, CORE)
    grad_w_qkv, grad_bias_qv = unpack_heads(flags, heads, heads_came, half_qkv)
    grad_w_qkv, value_came = tie((grad_w_qkv, value_came))
    grad_up, grad_down, grad_out, grad_bias_up, grad_bias_down, grad_bias_out, grad_alphas = (
        unpack_feed(flags, value, value_came, unit)
    )
    return (
        out, grad_tokens, grad_w_qkv.reshape(3, width_all, half_qkv), grad_bias_qv, grad_out,
        grad_bias_out, grad_up, grad_bias_up, grad_down, grad_bias_down, grad_alphas,
    )


def doc_numbers(total, longs):
    places = jnp.arange(total, dtype=jnp.int32)
    border = 2 * SHORT * longs
    return jnp.where(places < border, places // (2 * SHORT), longs + (places - border) // SHORT)


def contract_rows(left, right):
    return lax.dot_general(
        left, right, (((0,), (0,)), ((), ())), preferred_element_type=jnp.float32
    )


def contract_cols(left, right):
    return lax.dot_general(
        left, right, (((1,), (1,)), ((), ())), preferred_element_type=jnp.float32
    )


def gelu_grad(pre_act, upstream):
    _, pull = jax.vjp(jax.nn.gelu, pre_act)
    return pull(upstream)[0]


def local(
    tokens,
    long_docs,
    w_qkv,
    bias_qv,
    w_out,
    bias_out,
    w_up,
    bias_up,
    w_down,
    bias_down,
    alphas,
    cotangent,
):
    gathered = lax.all_gather(tokens, "tp", axis=0, tiled=True)
    total = gathered.shape[0]
    local_width = w_qkv.shape[2]
    local_heads = local_width // HEAD_DIM
    block = min(512, SHORT)
    window = 2 * SHORT // block
    span = window * block
    blocks_count = total // block
    docs = doc_numbers(total, long_docs[0])
    alpha_attn = alphas[0]
    alpha_ffn = alphas[1]
    scale_value = HEAD_DIM ** (-0.5)
    projected = jnp.einsum("td,cdf->ctf", gathered, w_qkv, preferred_element_type=jnp.float32)
    bias_float = bias_qv.astype(jnp.float32)
    query_all = (
        (projected[0] + bias_float[0]).astype(jnp.bfloat16).reshape(total, local_heads, HEAD_DIM)
    )
    key_all = projected[1].astype(jnp.bfloat16).reshape(total, local_heads, HEAD_DIM)
    value_all = (
        (projected[2] + bias_float[1]).astype(jnp.bfloat16).reshape(total, local_heads, HEAD_DIM)
    )

    def block_pieces(index):
        query_start = index * block
        key_start = jnp.maximum(index - window + 1, 0) * block
        query_rows = lax.dynamic_slice_in_dim(query_all, query_start, block, 0)
        query_docs = lax.dynamic_slice_in_dim(docs, query_start, block, 0)
        query_place = query_start + jnp.arange(block, dtype=jnp.int32)
        key_place = key_start + jnp.arange(span, dtype=jnp.int32)
        allowed = (docs[None, :] == query_docs[:, None]) & (
            key_place[None, :] <= query_place[:, None]
        )
        logits = (
            jnp.einsum("qhe,khe->hqk", query_rows, key_all, preferred_element_type=jnp.float32)
            * scale_value
        )
        logits = jnp.where(allowed[None], logits, -1e30)
        return (query_start, key_start, query_rows, key_all, value_all, logits)

    def forward_block(index):
        _, _, _, _, value_rows, logits = block_pieces(index)
        peak = jnp.max(logits, axis=-1, keepdims=True)
        expo = jnp.exp(logits - peak)
        summed = jnp.sum(expo, axis=-1, keepdims=True)
        probs = (expo / summed).astype(jnp.bfloat16)
        mixed_block = jnp.einsum(
            "hqk,khe->qhe", probs, value_rows, preferred_element_type=jnp.float32
        )
        return (mixed_block.astype(jnp.bfloat16), (peak + jnp.log(summed))[..., 0])

    mixed_blocks, log_totals = lax.map(forward_block, jnp.arange(blocks_count, dtype=jnp.int32))
    mixed = mixed_blocks.reshape(total, local_width)
    attn_full = lax.psum_scatter(
        jnp.dot(mixed, w_out, preferred_element_type=jnp.float32),
        "tp",
        scatter_dimension=0,
        tiled=True,
    ) + bias_out.astype(jnp.float32)
    resid = tokens.astype(jnp.float32) + alpha_attn * attn_full
    resid_low = resid.astype(jnp.bfloat16)
    cot_float = cotangent.astype(jnp.float32)
    ffn_grad_low = (alpha_ffn * cot_float).astype(jnp.bfloat16)
    resid_all = lax.all_gather(resid_low, "tp", axis=0, tiled=True)
    pre_act = jnp.dot(resid_all, w_up, preferred_element_type=jnp.float32) + bias_up.astype(
        jnp.float32
    )
    act_low = jax.nn.gelu(pre_act).astype(jnp.bfloat16)
    ffn_out = lax.psum_scatter(
        jnp.dot(act_low, w_down, preferred_element_type=jnp.float32),
        "tp",
        scatter_dimension=0,
        tiled=True,
    )
    ffn_grad_all = lax.all_gather(ffn_grad_low, "tp", axis=0, tiled=True)
    grad_w_down = contract_rows(act_low, ffn_grad_all)
    grad_pre = gelu_grad(pre_act, contract_cols(ffn_grad_all, w_down)).astype(jnp.bfloat16)
    grad_w_up = contract_rows(resid_all, grad_pre)
    grad_bias_up = jnp.sum(grad_pre.astype(jnp.float32), axis=0)
    grad_resid_ffn = lax.psum_scatter(
        contract_cols(grad_pre, w_up), "tp", scatter_dimension=0, tiled=True
    )
    ffn_full = ffn_out + bias_down.astype(jnp.float32)
    out = (resid + alpha_ffn * ffn_full).astype(jnp.bfloat16)
    grad_alpha_ffn = jnp.sum(cot_float * ffn_full)
    grad_bias_down = alpha_ffn * jnp.sum(cot_float, axis=0)
    grad_resid = cot_float + grad_resid_ffn
    grad_alpha_attn = jnp.sum(grad_resid * attn_full)
    grad_bias_out = alpha_attn * jnp.sum(grad_resid, axis=0)
    attn_grad_low = (alpha_attn * grad_resid).astype(jnp.bfloat16)
    attn_grad_all = lax.all_gather(attn_grad_low, "tp", axis=0, tiled=True)
    grad_w_out = contract_rows(mixed, attn_grad_all)
    grad_mixed = (
        contract_cols(attn_grad_all, w_out)
        .astype(jnp.bfloat16)
        .reshape(total, local_heads, HEAD_DIM)
    )

    def backward_block(carry, index):
        grad_keys, grad_values = carry
        query_start, key_start, query_rows, key_rows, value_rows, logits = block_pieces(index)
        block_totals = lax.dynamic_index_in_dim(log_totals, index, 0, keepdims=False)
        probs = jnp.exp(logits - block_totals[:, :, None])
        upstream = lax.dynamic_slice_in_dim(grad_mixed, query_start, block, 0)
        grad_probs = jnp.einsum(
            "qhe,khe->hqk", upstream, value_rows, preferred_element_type=jnp.float32
        )
        row_terms = jnp.sum(probs * grad_probs, axis=-1, keepdims=True)
        grad_logits = (probs * (grad_probs - row_terms)).astype(jnp.bfloat16)
        grad_query_block = (
            jnp.einsum("hqk,khe->qhe", grad_logits, key_rows, preferred_element_type=jnp.float32)
            * scale_value
        )
        key_part = (
            jnp.einsum("hqk,qhe->khe", grad_logits, query_rows, preferred_element_type=jnp.float32)
            * scale_value
        )
        value_part = jnp.einsum(
            "hqk,qhe->khe", probs.astype(jnp.bfloat16), upstream, preferred_element_type=jnp.float32
        )
        grad_keys = grad_keys + key_part
        grad_values = grad_values + value_part
        return ((grad_keys, grad_values), grad_query_block)

    zero_grads = jnp.zeros((total, local_heads, HEAD_DIM), jnp.float32)
    (grad_keys, grad_values), grad_query_blocks = lax.scan(
        backward_block, (zero_grads, zero_grads), jnp.arange(blocks_count, dtype=jnp.int32)
    )
    grad_proj = jnp.stack(
        [
            grad_query_blocks.reshape(total, local_width),
            grad_keys.reshape(total, local_width),
            grad_values.reshape(total, local_width),
        ]
    ).astype(jnp.bfloat16)
    grad_w_qkv = jnp.einsum("td,ctf->cdf", gathered, grad_proj, preferred_element_type=jnp.float32)
    grad_bias_qv = jnp.stack(
        [
            jnp.sum(grad_proj[0].astype(jnp.float32), axis=0),
            jnp.sum(grad_proj[2].astype(jnp.float32), axis=0),
        ]
    )
    grad_in_attn = lax.psum_scatter(
        jnp.einsum("ctf,cdf->td", grad_proj, w_qkv, preferred_element_type=jnp.float32),
        "tp",
        scatter_dimension=0,
        tiled=True,
    )
    grad_tokens = (grad_resid + grad_in_attn).astype(jnp.bfloat16)
    summed = lax.psum(
        (grad_w_qkv, grad_bias_qv, grad_w_out, grad_w_up, grad_bias_up, grad_w_down), "dp"
    )
    small = lax.psum(
        (grad_bias_out, grad_bias_down, jnp.stack([grad_alpha_attn, grad_alpha_ffn])), ("dp", "tp")
    )
    return (
        out,
        grad_tokens,
        summed[0],
        summed[1],
        summed[2],
        small[0],
        summed[3],
        summed[4],
        summed[5],
        small[1],
        small[2],
    )


def solution(mesh):
    step = local
    if mesh.shape["tp"] == 2 and mesh.shape["dp"] == 16:
        step = functools.partial(paired_local, n_dp=mesh.shape["dp"])
    return jax.shard_map(
        step,
        mesh=mesh,
        in_specs=(
            P(("dp", "tp"), None),
            P("dp"),
            P(None, None, "tp"),
            P(None, "tp"),
            P("tp", None),
            P(),
            P(None, "tp"),
            P("tp"),
            P("tp", None),
            P(),
            P(),
            P(("dp", "tp"), None),
        ),
        out_specs=(
            P(("dp", "tp"), None),
            P(("dp", "tp"), None),
            P(None, None, "tp"),
            P(None, "tp"),
            P("tp", None),
            P(),
            P(None, "tp"),
            P("tp"),
            P("tp", None),
            P(),
            P(),
        ),
        check_vma=False,
    )
```

```python
import functools

import jax
import jax.numpy as jnp
from jax import lax
from jax.experimental import pallas as pl
from jax.experimental.pallas import tpu as pltpu
from jax.sharding import PartitionSpec as P

HEAD_DIM = 64
SHORT = 1024
LOG2E = 1.4426950408889634
F32 = jnp.float32
BF16 = jnp.bfloat16
NT = (((1,), (1,)), ((), ()))
TN = (((0,), (0,)), ((), ()))
AXES = ("dp", "tp")
BIG = 1e30
PIECES = 8


def dot(left, right, dims=None):
    if dims is None:
        return jnp.dot(left, right, preferred_element_type=F32)
    return lax.dot_general(left, right, dims, preferred_element_type=F32)


def in_vmem():
    return pl.BlockSpec(memory_space=pltpu.VMEM)


def in_smem():
    return pl.BlockSpec(memory_space=pltpu.SMEM)


def in_place():
    return pl.BlockSpec(memory_space=pl.ANY)


def fill_pack(flags, pack_ref, own_ref, first_ref, second_ref):
    same, side = flags[3] > 0, flags[4] == 0
    size = first_ref.shape[0]
    first, second = first_ref[...], second_ref[...]
    pack_ref[:size] = jnp.where(same, own_ref[:size], jnp.where(side, first, second))
    pack_ref[size:] = jnp.where(same, own_ref[size:], jnp.where(side, second, first))


def lower_half(which, rows):
    zeros = jnp.zeros_like(rows)
    return jnp.where(
        which == 0, jnp.concatenate([rows, zeros], 0), jnp.concatenate([zeros, rows], 0)
    )


def unpacked(pack_ref, which, width):
    rows = pack_ref.shape[1] // 2
    at = slice(which * rows, which * rows + rows)
    return pack_ref[at, :width], pack_ref[at, width : 2 * width]


def attend_kernel(
    flags, mine_ref, other_ref, own_pack_ref, first_ref, second_ref, bias_ref, came_bias_ref,
    q_t_out, k_t_out, k_out, v_out, keep_ref, send_ref, lse_ref,
    v_t, mixed, scores, pack_ref, q_t_ref, k_t_ref, k_ref, v_ref, done, *, block,
):
    core, longs = flags[0], flags[2]
    fill_pack(flags, pack_ref, own_pack_ref, first_ref, second_ref)
    half = mine_ref.shape[0]
    total = 2 * half
    width = pack_ref.shape[1] // 2
    deep = pack_ref.shape[1] // 2
    pairs = width // 128
    heads = width // HEAD_DIM
    turned = [jnp.concatenate([p.T for p in unpacked(pack_ref, i, width)], 1) for i in range(3)]
    bias = jnp.where(flags[3] > 0, bias_ref[...], came_bias_ref[...]).astype(F32)[0:8]
    column = bias.T[:, 0:1]

    def project(rows_ref, which):
        at = pl.ds(pl.multiple_of(which * half, half), half)
        rows = rows_ref[...]
        q_t_ref[:, at] = (dot(turned[0], rows, NT) + column[:width]).astype(BF16)
        k_t_ref[:, at] = dot(turned[1], rows, NT).astype(BF16)
        v_t[:, at] = (dot(turned[2], rows, NT) + column[width:]).astype(BF16)
        for i, target in ((1, k_ref), (2, v_ref)):
            upper, lower = unpacked(pack_ref, i, width)
            for pair in range(pairs):
                cols = slice(pair * 128, pair * 128 + 128)
                part = dot(rows[:, :deep], upper[:, cols]) + dot(rows[:, deep:], lower[:, cols])
                if i == 2:
                    part = part + bias[0:1, width + pair * 128 : width + pair * 128 + 128]
                target[pair, at, :] = part.astype(BF16)

    project(mine_ref, core)
    project(other_ref, 1 - core)
    copies = [
        pltpu.make_async_copy(source, target, done.at[i])
        for i, (source, target) in enumerate(
            ((q_t_ref, q_t_out), (k_t_ref, k_t_out), (k_ref, k_out), (v_ref, v_out))
        )
    ]
    for copy in copies:
        copy.start()
    row = lax.broadcasted_iota(jnp.int32, (block, block), 0)
    col = lax.broadcasted_iota(jnp.int32, (block, block), 1)
    scale = HEAD_DIM ** (-0.5) * LOG2E

    def one_head(head, _):
        at = pl.ds(pl.multiple_of(head * HEAD_DIM, HEAD_DIM), HEAD_DIM)
        pair, which = head // 2, head % 2
        for q0 in range(0, total, block):
            queries = lower_half(which, q_t_ref[at, q0 : q0 + block])
            peak = jnp.full((8, block), -BIG, F32)
            for k0 in range(0, q0 + block, block):
                s = dot(k_ref[pair, k0 : k0 + block, :], queries)
                if k0 == q0:
                    s = jnp.where(row <= col, s, -BIG)
                scores[k0 : k0 + block, :] = s
                top = jnp.max(s.reshape(block // 8, 8, block), 0)
                if q0 >= SHORT > k0:
                    top = jnp.where(longs > 0, top, -BIG)
                peak = jnp.maximum(peak, top)
            peak = jnp.max(peak, 0, keepdims=True) * scale
            acc = jnp.zeros((HEAD_DIM, block), F32)
            norm = jnp.zeros((8, block), F32)
            for k0 in range(0, q0 + block, block):
                base = peak
                if q0 >= SHORT > k0:
                    base = jnp.where(longs > 0, peak, BIG)
                e = jnp.exp2(scores[k0 : k0 + block, :] * scale - base)
                norm = norm + jnp.sum(e.reshape(block // 8, 8, block), 0)
                acc = acc + dot(v_t[at, k0 : k0 + block], e.astype(BF16))
            norm = jnp.sum(norm, 0, keepdims=True)
            mixed[q0 // half, at, q0 % half : q0 % half + block] = (acc / norm).astype(BF16)
            lse_ref[head, :, q0 : q0 + block] = jnp.broadcast_to(
                peak + jnp.log2(norm), (8, block)
            )
        return 0

    lax.fori_loop(0, heads, one_head, 0)
    keep_ref[...] = mixed[core]
    send_ref[...] = mixed[1 - core]
    for copy in copies:
        copy.wait()


def attend(flags, mine, other, own_pack, first, second, bias, came_bias):
    half = mine.shape[0]
    total, width = 2 * half, own_pack.shape[1] // 2
    shape = jax.ShapeDtypeStruct
    block = 512
    return pl.pallas_call(
        functools.partial(attend_kernel, block=block),
        out_shape=(
            shape((width, total), BF16),
            shape((width, total), BF16),
            shape((width // 128, total, 128), BF16),
            shape((width // 128, total, 128), BF16),
            shape((width, half), BF16),
            shape((width, half), BF16),
            shape((width // HEAD_DIM, 8, total), F32),
        ),
        in_specs=[in_smem()] + [in_vmem()] * 7,
        out_specs=(in_place(),) * 4 + (in_vmem(),) * 3,
        scratch_shapes=[
            pltpu.VMEM((width, total), BF16),
            pltpu.VMEM((2, width, half), BF16),
            pltpu.VMEM((total, block), F32),
            pltpu.VMEM(own_pack.shape, BF16),
            pltpu.VMEM((width, total), BF16),
            pltpu.VMEM((width, total), BF16),
            pltpu.VMEM((width // 128, total, 128), BF16),
            pltpu.VMEM((width // 128, total, 128), BF16),
            pltpu.SemaphoreType.DMA((4,)),
        ],
        compiler_params=pltpu.CompilerParams(vmem_limit_bytes=16 << 20),
        cost_estimate=pl.CostEstimate(
            flops=0, bytes_accessed=0, transcendentals=0
        ),
    )(flags, mine, other, own_pack, first, second, bias, came_bias)


def feed_kernel(
    flags, alphas, tok_ref, own_cot_ref, came_cot_ref, keep_ref, recv_ref, wout_ref, bias_ref,
    bup_ref, up_ref, down_ref, near_up, far_up, near_down, far_down,
    out_ref, dresid_ref, dkeep_ref, dsend_ref, gkeep_a_ref, gkeep_b_ref, gsend_a_ref, gsend_b_ref,
    mixed, dmixed, attn, resid, ffn, act, dpre, small, cot_ref,
    *, piece,
):
    core, same = flags[0], flags[3]
    rows, width = tok_ref.shape
    side, deep = flags[4], flags[5]
    main = gkeep_a_ref.shape[2] - 8
    unit = up_ref.shape[1] // 2
    part = wout_ref.shape[0] // 2
    a_attn, a_ffn = alphas[0], alphas[1]
    cot_ref[...] = jnp.where(same > 0, own_cot_ref[...], came_cot_ref[...])
    biases = bias_ref[...].astype(F32)
    own_bup = bup_ref[...].astype(F32)
    mixed[1 - same] = keep_ref[...]
    mixed[same] = recv_ref[...]

    def own_sub(j):
        return core if j == 0 else 1 - core

    def place_of(h, j, piece_at):
        y = 1 - side if (piece_at // 2) % 2 else side
        z = 1 - deep if piece_at % 2 else deep
        if piece_at < PIECES // 2:
            return (gkeep_a_ref, gsend_a_ref)[j].at[h, 2 * y + z]
        return (gkeep_b_ref, gsend_b_ref)[j].at[y, 2 * h + z]

    def put(h, j, start, value):
        value = value.astype(BF16)
        at = 0
        while at < value.shape[0]:
            piece_at, row = divmod(start + at, main)
            size = min(main - row, value.shape[0] - at)
            place_of(h, j, piece_at)[row : row + size, :] = value[at : at + size]
            at += size

    def wout_part(h, j):
        if h == 0:
            return wout_ref[pl.ds(pl.multiple_of(own_sub(j) * part, part), part), :]
        return (near_down, far_down)[j][unit : unit + part, :]

    def mixed_part(h, j):
        return mixed[h, pl.ds(pl.multiple_of(own_sub(j) * part, part), part), :]

    total = dot(mixed_part(0, 0), wout_part(0, 0), TN)
    for h, j in ((0, 1), (1, 0), (1, 1)):
        total = total + dot(mixed_part(h, j), wout_part(h, j), TN)
    attn[...] = total + biases[1:2]
    resid[...] = tok_ref[...].astype(F32) + a_attn * attn[...]
    low = resid[...].astype(BF16)
    low_t = low.T
    dffn = (cot_ref[...].astype(F32) * a_ffn).astype(BF16)
    dffn_t = dffn.T
    dresid_ref[...] = cot_ref[...].astype(F32)
    ffn[...] = jnp.broadcast_to(biases[2:3], ffn.shape)
    for h in range(2):
        for j in range(2):
            sub = pl.ds(pl.multiple_of(own_sub(j) * unit, unit), unit)
            if h == 0:
                up, down = up_ref[:, sub], down_ref[sub, :]
            else:
                source = (near_up, far_up)[j]
                up, down = source[:unit, :], (near_down, far_down)[j][:unit, :]
            if h == 0:
                bias = jnp.where(own_sub(j) == 0, own_bup[1:2], own_bup[2:3])
            else:
                bias = source[unit : unit + 16, :].astype(F32)[0:1]
            bias_grad = jnp.zeros((8, unit), F32)
            for r0 in range(0, rows, piece):
                at = slice(r0, r0 + piece)
                u = dot(low[at], up) + bias
                square = u * u
                t = jnp.tanh(u * (0.7978845608028654 + 0.035677408136300125 * square))
                s = 0.5 + 0.5 * t
                slope = s + (0.5 * u) * (1.0 - t * t) * (
                    0.7978845608028654 + 0.10703222440890037 * square
                )
                act[at, :] = (u * s).astype(BF16)
                d = dot(dffn[at], down, NT) * slope
                d_low = d.astype(BF16)
                dpre[at, :] = d_low
                bias_grad = bias_grad + jnp.sum(
                    d_low.astype(F32).reshape(piece // 8, 8, unit), 0
                )
                ffn[at, :] += dot(act[at, :], down)
                dresid_ref[at, :] += dot(d_low, up, NT)
            put(h, j, 0, dot(low_t, dpre[...]))
            put(h, j, unit, dot(dffn_t, act[...]).T)
            small[2 * h + j, :] = jnp.sum(bias_grad, 0)
    g = cot_ref[...].astype(F32)
    out_ref[...] = (resid[...] + a_ffn * ffn[...]).astype(BF16)
    dresid = dresid_ref[...]
    bias_down = a_ffn * jnp.sum(g, 0, keepdims=True)
    bias_out = a_attn * jnp.sum(dresid, 0, keepdims=True)
    sums = [
        jnp.sum(jnp.sum(v, 0, keepdims=True), 1, keepdims=True)
        for v in (dresid * attn[...], g * ffn[...])
    ]
    lane = lax.broadcasted_iota(jnp.int32, (1, width), 1)
    both = jnp.where(lane == 0, sums[0], jnp.where(lane == 1, sums[1], 0.0))
    dattn = (a_attn * dresid).astype(BF16)
    for h in range(2):
        for j in range(2):
            put(h, j, 2 * unit, dot(mixed_part(h, j), dattn))
            dmixed[h, pl.ds(pl.multiple_of(own_sub(j) * part, part), part), :] = dot(
                wout_part(h, j), dattn, NT
            ).astype(BF16)
            exact = jnp.concatenate(
                [small[2 * h + j : 2 * h + j + 1, :], bias_down, bias_out, both], 0
            )
            high = exact.astype(BF16).astype(F32)
            for i in range(1, PIECES):
                place_of(h, j, i)[main:, :] = jnp.zeros((8, width), BF16)
            place_of(h, j, 0)[main:, :] = jnp.concatenate([high, exact - high], 0).astype(BF16)
    dkeep_ref[...] = dmixed[1 - same]
    dsend_ref[...] = dmixed[same]


def feed(
    flags, alphas, tok, own_cot, came_cot, keep, recv, up, down, wout, near_up, far_up,
    near_down, far_down, bias, bias_up,
):
    rows, width = tok.shape
    unit = up.shape[1] // 2
    half_width = keep.shape[0]
    shape = jax.ShapeDtypeStruct

    piece = shape((2, PIECES // 2, (2 * unit + half_width // 2) // PIECES + 8, width), BF16)
    outs = (
        shape((rows, width), BF16),
        shape((rows, width), F32),
        shape((half_width, rows), BF16),
        shape((half_width, rows), BF16),
        piece,
        piece,
        piece,
        piece,
    )
    values = (tok, own_cot, came_cot, keep, recv, wout, bias, bias_up)
    later = (up, down, near_up, far_up, near_down, far_down)
    return pl.pallas_call(
        functools.partial(feed_kernel, piece=256),
        out_shape=outs,
        in_specs=[in_smem()] * 2
        + [in_vmem()] * (len(values) + len(later)),
        out_specs=(in_vmem(),) * len(outs),
        scratch_shapes=[
            pltpu.VMEM((2, half_width, rows), BF16),
            pltpu.VMEM((2, half_width, rows), BF16),
            pltpu.VMEM((rows, width), F32),
            pltpu.VMEM((rows, width), F32),
            pltpu.VMEM((rows, width), F32),
            pltpu.VMEM((rows, unit), BF16),
            pltpu.VMEM((rows, unit), BF16),
            pltpu.VMEM((8, unit), F32),
            pltpu.VMEM((rows, width), BF16),
        ],
        compiler_params=pltpu.CompilerParams(vmem_limit_bytes=24 << 20),
        cost_estimate=pl.CostEstimate(
            flops=0, bytes_accessed=0, transcendentals=0
        ),
    )(flags, alphas, *values, *later)


def attend_back_kernel(
    flags, mine_in, other_in, q_t_ref, k_t_ref, k_ref, v_ref, keep_ref, send_ref,
    dkeep_ref, drecv_ref, lse_ref, *refs, block, part_of,
):
    sums_ref = None
    if part_of == 2:
        before_ref, first_ref, sums_all, *refs = refs
        sums_all[0] = before_ref[...]
        sums_ref = sums_all.at[1]
    elif part_of == 0:
        sums_ref, *refs = refs
    grads, mixed, dmixed, probs, dscores, mine_ref, other_ref, done = refs
    if part_of == 2:
        grads[:, :HEAD_DIM, :] = first_ref[...]
    core, longs = flags[0], flags[2]
    half = mine_ref.shape[0]
    total = 2 * half
    copies = [
        pltpu.make_async_copy(mine_in, mine_ref, done.at[0]),
        pltpu.make_async_copy(other_in, other_ref, done.at[1]),
    ]
    if part_of != 1:
        for copy in copies:
            copy.start()
    mixed[core] = keep_ref[...]
    mixed[1 - core] = send_ref[...]
    dmixed[core] = dkeep_ref[...]
    dmixed[1 - core] = drecv_ref[...]
    factor = HEAD_DIM ** (-0.5)
    scale = factor * LOG2E
    part = block // 2

    def one_head(which, _):
        at = pl.ds(pl.multiple_of(which * HEAD_DIM, HEAD_DIM), HEAD_DIM)
        for q0 in range(0, total, block):
            here = slice(q0 % half, q0 % half + block)
            do = dmixed[q0 // half, at, here]
            queries = lower_half(which, q_t_ref[at, q0 : q0 + block])
            upstream = lower_half(which, do)
            lse = lse_ref[which, 0:1, q0 : q0 + block]
            mean = jnp.sum(
                do.astype(F32) * mixed[q0 // half, at, here].astype(F32), 0, keepdims=True
            )
            pieces = [(k0, block, 0) for k0 in range(0, q0, block)]
            pieces += [(q0, part, 0), (q0 + part, part, part)]
            for k0, size, skip in pieces:
                keys, cols = slice(k0, k0 + size), slice(q0 + skip, q0 + block)
                base = lse
                if q0 >= SHORT > k0:
                    base = jnp.where(longs > 0, lse, BIG)
                s = dot(k_ref[0, keys, :], queries[:, skip:])
                dp = dot(v_ref[0, keys, :], upstream[:, skip:])
                p = jnp.exp2(s * scale - base[:, skip:])
                if k0 >= q0:
                    row = lax.broadcasted_iota(jnp.int32, p.shape, 0) + k0
                    col = lax.broadcasted_iota(jnp.int32, p.shape, 1) + (q0 + skip)
                    p = jnp.where(row <= col, p, 0.0)
                probs[keys, cols] = p.astype(BF16)
                dscores[keys, cols] = (p * (dp - mean[:, skip:])).astype(BF16)
                if skip:
                    probs[keys, q0 : q0 + skip] = jnp.zeros((size, skip), BF16)
                    dscores[keys, q0 : q0 + skip] = jnp.zeros((size, skip), BF16)
            end = q0 + block
            grads[0, at, q0:end] = (
                dot(k_t_ref[at, 0:end], dscores[0:end, q0:end]) * factor
            ).astype(BF16)
        for k0 in range(0, total, block):
            keys = slice(k0, k0 + block)
            grads[1, at, keys] = (
                dot(q_t_ref[at, k0:], dscores[keys, k0:], NT) * factor
            ).astype(BF16)
            first = k0 // half
            acc = dot(dmixed[first, at, k0 % half :], probs[keys, k0 : (first + 1) * half], NT)
            if first == 0:
                acc = acc + dot(dmixed[1, at, :], probs[keys, half:], NT)
            grads[2, at, keys] = acc.astype(BF16)
        return 0

    lax.fori_loop((0, 0, 1)[part_of], (2, 1, 2)[part_of], one_head, 0)
    if part_of == 1:
        return
    for copy in copies:
        copy.wait()
    near = pl.ds(pl.multiple_of(core * half, half), half)
    far = pl.ds(pl.multiple_of((1 - core) * half, half), half)
    main = sums_ref.shape[1] - 16
    deep = mine_ref.shape[1]
    for i in range(3):
        value = (
            dot(grads[i, :, near], mine_ref[...]) + dot(grads[i, :, far], other_ref[...])
        ).T.astype(BF16)
        at = 0
        while at < deep:
            piece, row = divmod(i * deep + at, main)
            size = min(main - row, deep - at)
            sums_ref[piece, row : row + size, :] = value[at : at + size]
            at += size
    ones = jnp.ones((8, total), BF16)
    rest = jnp.zeros((14, 2 * HEAD_DIM), F32)
    sums_ref[0, main:, :] = jnp.concatenate(
        [dot(ones, grads[0], NT)[0:1], dot(ones, grads[2], NT)[0:1], rest], 0
    ).astype(BF16)
    for piece in range(1, sums_ref.shape[0]):
        sums_ref[piece, main:, :] = jnp.zeros((16, 2 * HEAD_DIM), BF16)


def attend_back(pair, part_of, before, flags, mine, other, q_t, k_t, k, v, keep, send, dkeep, drecv, lse):
    half, width_all = mine.shape
    total = 2 * half
    shape = jax.ShapeDtypeStruct

    def whole(x):
        return pl.BlockSpec(x.shape, lambda i: (0,) * x.ndim)

    def rows_of(x):
        return pl.BlockSpec((2 * HEAD_DIM, x.shape[1]), lambda i: (pair, 0))

    def pair_of(x):
        return pl.BlockSpec((1,) + x.shape[1:], lambda i: (pair, 0, 0))

    sums = (4, 3 * width_all // 4 + 16, 2 * HEAD_DIM)
    outs = (shape((3, 2 * HEAD_DIM, total), BF16),)
    if part_of == 1:
        outs = (shape((3, HEAD_DIM, total), BF16),)
    else:
        outs = (shape((2,) + sums if part_of else sums, BF16),) + outs
    return pl.pallas_call(
        functools.partial(attend_back_kernel, block=512, part_of=part_of),
        grid=(1,),
        out_shape=outs,
        in_specs=[in_smem(), in_place(), in_place(), rows_of(q_t), rows_of(k_t), pair_of(k),
                  pair_of(v), rows_of(keep), rows_of(send), rows_of(dkeep), rows_of(drecv),
                  pl.BlockSpec((2, 8, total), lambda i: (pair, 0, 0))]
        + [whole(x) for x in before],
        out_specs=tuple(whole(x) for x in outs),
        scratch_shapes=[
            pltpu.VMEM((2, 2 * HEAD_DIM, half), BF16),
            pltpu.VMEM((2, 2 * HEAD_DIM, half), BF16),
            pltpu.VMEM((total, total), BF16),
            pltpu.VMEM((total, total), BF16),
            pltpu.VMEM(mine.shape, BF16),
            pltpu.VMEM(mine.shape, BF16),
            pltpu.SemaphoreType.DMA((2,)),
        ],
        compiler_params=pltpu.CompilerParams(vmem_limit_bytes=24 << 20),
        cost_estimate=pl.CostEstimate(
            flops=0, bytes_accessed=0, transcendentals=0
        ),
    )(flags, mine, other, q_t, k_t, k, v, keep, send, dkeep, drecv, lse, *before)


def inputs_back_kernel(flags, own_pack_ref, first_ref, second_ref, dresid_ref, *refs):
    core = flags[0]
    *grads, own_ref, away_ref, pack_ref = refs
    fill_pack(flags, pack_ref, own_pack_ref, first_ref, second_ref)
    half = own_ref.shape[0]
    width = pack_ref.shape[1] // 2

    def back(which):
        at = pl.ds(pl.multiple_of(which * half, half), half)
        result = []
        for part in range(2):
            total = 0.0
            for i in range(3):
                weights = unpacked(pack_ref, i, width)[part]
                stacked = jnp.concatenate([g[i, :, at] for g in grads], 0)
                total = total + dot(weights, stacked)
            result.append(total.T)
        return jnp.concatenate(result, 1)

    away_ref[...] = back(1 - core).astype(BF16)
    own_ref[...] = dresid_ref[...] + back(core)


def inputs_back(flags, own_pack, first, second, dresid, grads):
    half, width_all = dresid.shape
    shape = jax.ShapeDtypeStruct
    return pl.pallas_call(
        inputs_back_kernel,
        out_shape=(shape((half, width_all), F32), shape((half, width_all), BF16)),
        in_specs=[in_smem()] + [in_vmem()] * (4 + len(grads)),
        out_specs=(in_vmem(),) * 2,
        scratch_shapes=[
            pltpu.VMEM(own_pack.shape, BF16),
        ],
        compiler_params=pltpu.CompilerParams(vmem_limit_bytes=10 << 20),
        cost_estimate=pl.CostEstimate(
            flops=0, bytes_accessed=0, transcendentals=0
        ),
    )(flags, own_pack, first, second, dresid, *grads)


def unpack_heads_kernel(flags, mine_ref, came_ref, grad_ref, bias_ref):
    core, side = flags[0], flags[4]
    main = mine_ref.shape[2] - 16
    for far in range(2):
        source = came_ref if far else mine_ref
        for turn in range(2):
            piece = 2 * (1 - core if far else core) + (1 - side if turn else side)
            at = pl.ds(pl.multiple_of(piece * main, main), main)
            for pair in range(source.shape[1]):
                cols = slice(pair * 128, pair * 128 + 128)
                grad_ref[at, cols] = source[turn, pair, :main, :].astype(F32)

            @pl.when(piece == 0)
            def _():
                for pair in range(source.shape[1]):
                    cols = slice(pair * 128, pair * 128 + 128)
                    bias_ref[:, cols] = source[turn, pair, main:, :].astype(F32)[0:2]


def unpack_heads(flags, mine, came, width):
    shape = jax.ShapeDtypeStruct
    main = mine.shape[2] - 16
    return pl.pallas_call(
        unpack_heads_kernel,
        out_shape=(shape((4 * main, width), F32), shape((2, width), F32)),
        in_specs=[in_smem()] + [in_vmem()] * 2,
        out_specs=(in_vmem(),) * 2,
        compiler_params=pltpu.CompilerParams(vmem_limit_bytes=5 << 20),
    )(flags, mine, came)


def unpack_feed_kernel(
    flags, mine_ref, came_ref, up_ref, down_ref, out_ref, bup_ref, bdown_ref, bout_ref,
    alphas_ref, rows_ref, small_ref, *, unit,
):
    core, side, deep = flags[0], flags[4], flags[5]
    main = mine_ref.shape[3] - 8
    for far in range(2):
        source = came_ref if far else mine_ref
        which = 1 - core if far else core
        for turn in range(2):
            for dip in range(2):
                for order in range(2):
                    piece = (
                        4 * order
                        + 2 * (1 - side if turn else side)
                        + (1 - deep if dip else deep)
                    )
                    at = pl.ds(pl.multiple_of(piece * main, 16), main)
                    rows_ref[which, at, :] = source[turn, dip, order, :main, :]
                    if order == 0:

                        @pl.when(piece == 0)
                        def _():
                            both = source[turn, dip, order, main:, :].astype(F32)
                            small_ref[which] = both[0:4] + both[4:8]

    width = small_ref.shape[2]
    for i in range(2):
        bup_ref[i * unit : (i + 1) * unit] = small_ref[i, 0, :]
    bdown_ref[...] = small_ref[0, 1, :]
    bout_ref[...] = small_ref[0, 2, :]
    last = small_ref[0, 3:4, :]
    lane = lax.broadcasted_iota(jnp.int32, (1, width), 1)
    for i in range(2):
        alphas_ref[i] = jnp.sum(jnp.where(lane == i, last, 0.0))
    for i in range(2):
        up_ref[:, i * unit : (i + 1) * unit] = rows_ref[i, :unit, :].astype(F32)
        down_ref[i * unit : (i + 1) * unit, :] = rows_ref[i, unit : 2 * unit, :].astype(F32)
        part = rows_ref.shape[1] - 2 * unit
        out_ref[i * part : (i + 1) * part, :] = rows_ref[i, 2 * unit :, :].astype(F32)


def unpack_feed(flags, mine, came, unit):
    shape = jax.ShapeDtypeStruct
    main, width = mine.shape[3] - 8, mine.shape[4]
    return pl.pallas_call(
        functools.partial(unpack_feed_kernel, unit=unit),
        out_shape=(
            shape((width, 2 * unit), F32),
            shape((2 * unit, width), F32),
            shape((2 * (PIECES * main - 2 * unit), width), F32),
            shape((2 * unit,), F32),
            shape((width,), F32),
            shape((width,), F32),
            shape((2,), F32),
        ),
        in_specs=[in_smem()] + [in_vmem()] * 2,
        out_specs=(in_vmem(),) * 6 + (in_smem(),),
        scratch_shapes=[
            pltpu.VMEM((2, PIECES * main, width), BF16),
            pltpu.VMEM((2, 4, width), F32),
        ],
        compiler_params=pltpu.CompilerParams(vmem_limit_bytes=10 << 20),
    )(flags, mine, came)


def add_low(values):
    total = values[0].astype(F32)
    for value in values[1:]:
        total = total + value.astype(F32)
    return total.astype(BF16)


def take(value, *picks):
    block, index = [], []
    for axis in range(value.ndim - 2):
        what = picks[axis] if axis < len(picks) else None
        if what is None:
            what = (0, value.shape[axis])
        elif isinstance(what, int):
            what = (what, 1)
        block.append(what[1])
        index.append(what[0])
    return value, tuple(block) + value.shape[-2:], tuple(index) + (0, 0)


def sum_kernel(*refs, plan, n_in):
    ins, outs = refs[:n_in], refs[n_in:]

    def terms(total):
        exact = total[0:4] + total[4:8]
        high = exact.astype(BF16).astype(F32)
        return jnp.concatenate([high, exact - high], 0)

    for out, groups in zip(outs, plan):
        at = 0
        main = out.shape[-2] - 8
        for members, alike in groups:
            lead = 1
            for size in ins[members[0]].shape[:-2]:
                lead *= size
            for i in range(lead):
                total, rows = None, None
                for n, member in enumerate(members):
                    ref = ins[member]
                    index, rest = [], i
                    for size in reversed(ref.shape[:-2]):
                        index.insert(0, rest % size)
                        rest //= size
                    value = ref[tuple(index)].astype(F32)
                    top, low = value[:main], value[main:]
                    total = top if total is None else total + top
                    rows = low if rows is None else rows + low
                    if n + 1 == alike:
                        rows = terms(rows).astype(BF16).astype(F32)
                out[at, :main, :] = total.astype(BF16)
                out[at, main:, :] = terms(rows).astype(BF16)
                at += 1


def sum_pieces(*outs):
    blocks, plan, shapes = [], [], []
    for groups in outs:
        lead, steps = 0, []
        for members, alike in groups:
            steps.append((tuple(range(len(blocks), len(blocks) + len(members))), alike))
            blocks.extend(members)
            count = 1
            for size in members[0][1][:-2]:
                count *= size
            lead += count
        plan.append(tuple(steps))
        shapes.append(jax.ShapeDtypeStruct((lead,) + groups[0][0][0][1][-2:], BF16))
    return pl.pallas_call(
        functools.partial(sum_kernel, plan=tuple(plan), n_in=len(blocks)),
        grid=(1,),
        out_shape=tuple(shapes),
        in_specs=[pl.BlockSpec(block, lambda i, at=at: at) for _, block, at in blocks],
        out_specs=tuple(pl.BlockSpec(x.shape, lambda i: (0, 0, 0)) for x in shapes),
        compiler_params=pltpu.CompilerParams(vmem_limit_bytes=5 << 20),
        cost_estimate=pl.CostEstimate(flops=0, bytes_accessed=0, transcendentals=0),
    )(*(value for value, _, _ in blocks))


def pick(value, side, axis):
    size = value.shape[axis] // 2
    return lax.dynamic_slice_in_dim(value, side * size, size, axis)


def paired_local(
    tokens, long_docs, w_qkv, bias_qv, w_out, bias_out, w_up, bias_up, w_down, bias_down, alphas,
    cotangent, *, n_dp,
):
    devices = 2 * n_dp
    place = lax.axis_index("tp")
    row_index = lax.axis_index("dp")
    core = row_index % 2
    same = (core == place).astype(jnp.int32)
    is_same = core == place

    def swapped(i):
        return (i & ~3) | ((i & 1) << 1) | ((i >> 1) & 1)

    def trade(value):
        pairs = [(i, swapped(i)) for i in range(devices) if i != swapped(i)]
        return lax.ppermute(value, AXES, pairs)

    def cross(value, bit):
        return lax.ppermute(value, AXES, [(i, i ^ bit) for i in range(devices)])

    def collect(value):
        return lax.ppermute(
            value, AXES, [(i, i ^ 1) for i in range(devices) if (i & 1) != (i >> 1) & 1]
        )

    PLACE, CORE, NEXT = 1, 2, 4
    side = (row_index // 2) % 2
    outer = []
    bit = 8
    while bit < devices:
        outer.append((bit, (row_index // (bit // 2)) % 2))
        bit *= 2

    width_all, half_qkv = w_qkv.shape[1:]
    unit = w_up.shape[1] // 2
    part = w_out.shape[0] // 2
    tie = lax.optimization_barrier
    longs = jnp.where(is_same, long_docs, cross(long_docs, CORE))[0]
    flags = jnp.stack([core, place, longs, same, side, outer[0][1]]).astype(jnp.int32)
    small = tie(
        jnp.concatenate(
            [bias_qv.reshape(1, -1), bias_out[None], bias_down[None],
             jnp.zeros((13, width_all), BF16)], 0,
        )
    )
    own_pack = jnp.concatenate(
        [w_qkv[:, : width_all // 2], w_qkv[:, width_all // 2 :]], 2
    ).reshape(-1, 2 * half_qkv)
    small_up = tie(
        jnp.concatenate(
            [lax.dynamic_slice_in_dim(bias_up, core * unit, unit, 0)[None],
             bias_up.reshape(2, unit), jnp.zeros((13, unit), BF16)], 0,
        )
    )
    packed_up = jnp.concatenate(
        [lax.dynamic_slice_in_dim(w_up, core * unit, unit, 1), small_up], 0
    )
    packed_down = jnp.concatenate(
        [
            lax.dynamic_slice_in_dim(w_down, core * unit, unit, 0),
            lax.dynamic_slice_in_dim(w_out, core * part, part, 0),
        ],
        0,
    )
    came, first, came_small = trade(tokens), trade(pick(own_pack, side, 0)), trade(small)
    came, first, came_small, packed_up, packed_down, cotangent_tied, flags = tie(
        (came, first, came_small, packed_up, packed_down, cotangent, flags)
    )
    second = lax.ppermute(
        first, AXES, [(i, i ^ NEXT) for i in range(devices) if (i & 1) != (i >> 1) & 1]
    )
    near_up, near_down = cross(packed_up, PLACE), cross(packed_down, PLACE)
    came_cot = trade(cotangent_tied)
    mine = jnp.where(is_same, tokens, came)
    other = cross(mine, CORE)
    q_t, k_t, k, v, keep, send, lse = attend(
        flags, mine, other, own_pack, first, second, small, came_small
    )
    near_up, near_down, send = tie((near_up, near_down, send))
    far_up, far_down = cross(near_up, CORE), cross(near_down, CORE)
    recv = cross(send, CORE)
    out, dresid, dkeep, dsend, keep_a, keep_b, send_a, send_b = feed(
        flags, alphas, mine, cotangent, came_cot, keep, recv, w_up, w_down, w_out, near_up, far_up,
        near_down, far_down, small, small_up,
    )
    drecv = cross(dsend, CORE)
    back_args = (flags, mine, other, q_t, k_t, k, v, keep, send, dkeep, drecv, lse)

    other_a, other_b = cross(send_a, CORE), cross(send_b, CORE)
    give_a, give_b = sum_pieces(
        [([take(keep_a, 1), take(other_a, 1)], 0)], [([take(keep_b, 1), take(other_b, 1)], 0)]
    )
    back_args, give_a, give_b = tie((back_args, give_a, give_b))
    got_a, got_b = cross(give_a, PLACE), cross(give_b, NEXT)
    sums_0, grads_0 = attend_back(0, 0, (), *back_args)
    stay_a, give_a, give_b = sum_pieces(
        *(
            [
                ([take(keep_a, 0, (i, 2)), take(other_a, 0, (i, 2)), take(got_a, (i, 2))], 2)
            ]
            for i in range(2)
        ),
        [([take(keep_b, 0, (1, 2)), take(other_b, 0, (1, 2)), take(got_b, (1, 2))], 0)],
    )
    back_args, give_a, give_b, sums_0 = tie((back_args, give_a, give_b, sums_0))
    got_a, got_b2 = cross(give_a, NEXT), cross(give_b, PLACE)
    (first_grads,) = attend_back(1, 1, (), *back_args)
    stay, give = sum_pieces(
        *(
            [
                ([take(stay_a, i), take(got_a, i)], 0),
                ([take(keep_b, 0, i), take(other_b, 0, i), take(got_b, i), take(got_b2, i)], 0),
            ]
            for i in range(2)
        )
    )
    back_args, give, first_grads = tie((back_args, give, first_grads))
    low_bit, high_bit = outer[0][0], outer[1][0]
    got = cross(give, low_bit)
    sums, grads_1 = attend_back(1, 2, (sums_0, first_grads), *back_args)
    halves = [sum_pieces([([take(stay, i), take(got, i)], 0)])[0] for i in range(2)]
    grads_0, halves, sums = tie((grads_0, halves, sums))
    got_half = cross(halves[0], high_bit)
    got_sums = collect(sums)
    own, away = inputs_back(flags, own_pack, first, second, dresid, (grads_0, grads_1))
    got_half, got_sums, own, away = tie((got_half, got_sums, own, away))

    stay_q, give_q = (
        add_low([pick(p, i, 1) for p in (sums, got_sums)]) for i in (core, 1 - core)
    )
    heads = jnp.where(is_same, stay_q, cross(give_q, CORE))
    grad_tokens = (own + cross(away, CORE).astype(F32)).astype(BF16)
    half, give_q, out = tie((halves[1], pick(heads, 1 - side, 1), out))
    got_other = cross(half, high_bit)
    got_q = cross(give_q, NEXT)
    out_came = trade(out)
    tokens_came = trade(grad_tokens)
    heads = add_low([pick(heads, side, 1), got_q])[:, 0]
    (value,) = sum_pieces(
        [([take(halves[0]), take(got_half)], 0), ([take(half), take(got_other)], 0)]
    )
    value, heads = tie((value, heads))
    along, beside = cross(value, low_bit), cross(value, NEXT)
    heads = add_low([heads, cross(heads, low_bit)])
    along, beside, heads = tie((along, beside, heads))
    corner = cross(along, NEXT)
    heads = add_low([heads, cross(heads, high_bit)])
    corner, heads, tokens_came, out_came = tie((corner, heads, tokens_came, out_came))
    value = jnp.stack([jnp.stack([value, along]), jnp.stack([beside, corner])])
    value, heads = tie((value, heads))
    heads_next = cross(heads, NEXT)
    value_came = cross(value, CORE)
    out = jnp.where(is_same, out, out_came)
    grad_tokens = jnp.where(is_same, grad_tokens, tokens_came)
    grad_up, grad_down, grad_out, grad_bias_up, grad_bias_down, grad_bias_out, grad_alphas = (
        unpack_feed(flags, value, value_came, unit)
    )
    heads_next, grad_up, out, grad_tokens = tie((heads_next, grad_up, out, grad_tokens))
    heads = jnp.stack([heads, heads_next])
    grad_w_qkv, grad_bias_qv = unpack_heads(flags, heads, cross(heads, CORE), half_qkv)
    return (
        out, grad_tokens, grad_w_qkv.reshape(3, width_all, half_qkv), grad_bias_qv, grad_out,
        grad_bias_out, grad_up, grad_bias_up, grad_down, grad_bias_down, grad_alphas,
    )


def doc_numbers(total, longs):
    places = jnp.arange(total, dtype=jnp.int32)
    border = 2 * SHORT * longs
    return jnp.where(places < border, places // (2 * SHORT), longs + (places - border) // SHORT)


def contract_rows(left, right):
    return lax.dot_general(
        left, right, (((0,), (0,)), ((), ())), preferred_element_type=jnp.float32
    )


def contract_cols(left, right):
    return lax.dot_general(
        left, right, (((1,), (1,)), ((), ())), preferred_element_type=jnp.float32
    )


def gelu_grad(pre_act, upstream):
    _, pull = jax.vjp(jax.nn.gelu, pre_act)
    return pull(upstream)[0]


def local(
    tokens,
    long_docs,
    w_qkv,
    bias_qv,
    w_out,
    bias_out,
    w_up,
    bias_up,
    w_down,
    bias_down,
    alphas,
    cotangent,
):
    gathered = lax.all_gather(tokens, "tp", axis=0, tiled=True)
    total = gathered.shape[0]
    local_width = w_qkv.shape[2]
    local_heads = local_width // HEAD_DIM
    block = min(512, SHORT)
    window = 2 * SHORT // block
    span = window * block
    blocks_count = total // block
    docs = doc_numbers(total, long_docs[0])
    alpha_attn = alphas[0]
    alpha_ffn = alphas[1]
    scale_value = HEAD_DIM ** (-0.5)
    projected = jnp.einsum("td,cdf->ctf", gathered, w_qkv, preferred_element_type=jnp.float32)
    bias_float = bias_qv.astype(jnp.float32)
    query_all = (
        (projected[0] + bias_float[0]).astype(jnp.bfloat16).reshape(total, local_heads, HEAD_DIM)
    )
    key_all = projected[1].astype(jnp.bfloat16).reshape(total, local_heads, HEAD_DIM)
    value_all = (
        (projected[2] + bias_float[1]).astype(jnp.bfloat16).reshape(total, local_heads, HEAD_DIM)
    )

    def block_pieces(index):
        query_start = index * block
        key_start = jnp.maximum(index - window + 1, 0) * block
        query_rows = lax.dynamic_slice_in_dim(query_all, query_start, block, 0)
        query_docs = lax.dynamic_slice_in_dim(docs, query_start, block, 0)
        query_place = query_start + jnp.arange(block, dtype=jnp.int32)
        key_place = key_start + jnp.arange(span, dtype=jnp.int32)
        allowed = (docs[None, :] == query_docs[:, None]) & (
            key_place[None, :] <= query_place[:, None]
        )
        logits = (
            jnp.einsum("qhe,khe->hqk", query_rows, key_all, preferred_element_type=jnp.float32)
            * scale_value
        )
        logits = jnp.where(allowed[None], logits, -1e30)
        return (query_start, key_start, query_rows, key_all, value_all, logits)

    def forward_block(index):
        _, _, _, _, value_rows, logits = block_pieces(index)
        peak = jnp.max(logits, axis=-1, keepdims=True)
        expo = jnp.exp(logits - peak)
        summed = jnp.sum(expo, axis=-1, keepdims=True)
        probs = (expo / summed).astype(jnp.bfloat16)
        mixed_block = jnp.einsum(
            "hqk,khe->qhe", probs, value_rows, preferred_element_type=jnp.float32
        )
        return (mixed_block.astype(jnp.bfloat16), (peak + jnp.log(summed))[..., 0])

    mixed_blocks, log_totals = lax.map(forward_block, jnp.arange(blocks_count, dtype=jnp.int32))
    mixed = mixed_blocks.reshape(total, local_width)
    attn_full = lax.psum_scatter(
        jnp.dot(mixed, w_out, preferred_element_type=jnp.float32),
        "tp",
        scatter_dimension=0,
        tiled=True,
    ) + bias_out.astype(jnp.float32)
    resid = tokens.astype(jnp.float32) + alpha_attn * attn_full
    resid_low = resid.astype(jnp.bfloat16)
    cot_float = cotangent.astype(jnp.float32)
    ffn_grad_low = (alpha_ffn * cot_float).astype(jnp.bfloat16)
    resid_all = lax.all_gather(resid_low, "tp", axis=0, tiled=True)
    pre_act = jnp.dot(resid_all, w_up, preferred_element_type=jnp.float32) + bias_up.astype(
        jnp.float32
    )
    act_low = jax.nn.gelu(pre_act).astype(jnp.bfloat16)
    ffn_out = lax.psum_scatter(
        jnp.dot(act_low, w_down, preferred_element_type=jnp.float32),
        "tp",
        scatter_dimension=0,
        tiled=True,
    )
    ffn_grad_all = lax.all_gather(ffn_grad_low, "tp", axis=0, tiled=True)
    grad_w_down = contract_rows(act_low, ffn_grad_all)
    grad_pre = gelu_grad(pre_act, contract_cols(ffn_grad_all, w_down)).astype(jnp.bfloat16)
    grad_w_up = contract_rows(resid_all, grad_pre)
    grad_bias_up = jnp.sum(grad_pre.astype(jnp.float32), axis=0)
    grad_resid_ffn = lax.psum_scatter(
        contract_cols(grad_pre, w_up), "tp", scatter_dimension=0, tiled=True
    )
    ffn_full = ffn_out + bias_down.astype(jnp.float32)
    out = (resid + alpha_ffn * ffn_full).astype(jnp.bfloat16)
    grad_alpha_ffn = jnp.sum(cot_float * ffn_full)
    grad_bias_down = alpha_ffn * jnp.sum(cot_float, axis=0)
    grad_resid = cot_float + grad_resid_ffn
    grad_alpha_attn = jnp.sum(grad_resid * attn_full)
    grad_bias_out = alpha_attn * jnp.sum(grad_resid, axis=0)
    attn_grad_low = (alpha_attn * grad_resid).astype(jnp.bfloat16)
    attn_grad_all = lax.all_gather(attn_grad_low, "tp", axis=0, tiled=True)
    grad_w_out = contract_rows(mixed, attn_grad_all)
    grad_mixed = (
        contract_cols(attn_grad_all, w_out)
        .astype(jnp.bfloat16)
        .reshape(total, local_heads, HEAD_DIM)
    )

    def backward_block(carry, index):
        grad_keys, grad_values = carry
        query_start, key_start, query_rows, key_rows, value_rows, logits = block_pieces(index)
        block_totals = lax.dynamic_index_in_dim(log_totals, index, 0, keepdims=False)
        probs = jnp.exp(logits - block_totals[:, :, None])
        upstream = lax.dynamic_slice_in_dim(grad_mixed, query_start, block, 0)
        grad_probs = jnp.einsum(
            "qhe,khe->hqk", upstream, value_rows, preferred_element_type=jnp.float32
        )
        row_terms = jnp.sum(probs * grad_probs, axis=-1, keepdims=True)
        grad_logits = (probs * (grad_probs - row_terms)).astype(jnp.bfloat16)
        grad_query_block = (
            jnp.einsum("hqk,khe->qhe", grad_logits, key_rows, preferred_element_type=jnp.float32)
            * scale_value
        )
        key_part = (
            jnp.einsum("hqk,qhe->khe", grad_logits, query_rows, preferred_element_type=jnp.float32)
            * scale_value
        )
        value_part = jnp.einsum(
            "hqk,qhe->khe", probs.astype(jnp.bfloat16), upstream, preferred_element_type=jnp.float32
        )
        grad_keys = grad_keys + key_part
        grad_values = grad_values + value_part
        return ((grad_keys, grad_values), grad_query_block)

    zero_grads = jnp.zeros((total, local_heads, HEAD_DIM), jnp.float32)
    (grad_keys, grad_values), grad_query_blocks = lax.scan(
        backward_block, (zero_grads, zero_grads), jnp.arange(blocks_count, dtype=jnp.int32)
    )
    grad_proj = jnp.stack(
        [
            grad_query_blocks.reshape(total, local_width),
            grad_keys.reshape(total, local_width),
            grad_values.reshape(total, local_width),
        ]
    ).astype(jnp.bfloat16)
    grad_w_qkv = jnp.einsum("td,ctf->cdf", gathered, grad_proj, preferred_element_type=jnp.float32)
    grad_bias_qv = jnp.stack(
        [
            jnp.sum(grad_proj[0].astype(jnp.float32), axis=0),
            jnp.sum(grad_proj[2].astype(jnp.float32), axis=0),
        ]
    )
    grad_in_attn = lax.psum_scatter(
        jnp.einsum("ctf,cdf->td", grad_proj, w_qkv, preferred_element_type=jnp.float32),
        "tp",
        scatter_dimension=0,
        tiled=True,
    )
    grad_tokens = (grad_resid + grad_in_attn).astype(jnp.bfloat16)
    summed = lax.psum(
        (grad_w_qkv, grad_bias_qv, grad_w_out, grad_w_up, grad_bias_up, grad_w_down), "dp"
    )
    small = lax.psum(
        (grad_bias_out, grad_bias_down, jnp.stack([grad_alpha_attn, grad_alpha_ffn])), ("dp", "tp")
    )
    return (
        out,
        grad_tokens,
        summed[0],
        summed[1],
        summed[2],
        small[0],
        summed[3],
        summed[4],
        summed[5],
        small[1],
        small[2],
    )


def solution(mesh):
    step = local
    if mesh.shape["tp"] == 2 and mesh.shape["dp"] == 16:
        step = functools.partial(paired_local, n_dp=mesh.shape["dp"])
    return jax.shard_map(
        step,
        mesh=mesh,
        in_specs=(
            P(("dp", "tp"), None),
            P("dp"),
            P(None, None, "tp"),
            P(None, "tp"),
            P("tp", None),
            P(),
            P(None, "tp"),
            P("tp"),
            P("tp", None),
            P(),
            P(),
            P(("dp", "tp"), None),
        ),
        out_specs=(
            P(("dp", "tp"), None),
            P(("dp", "tp"), None),
            P(None, None, "tp"),
            P(None, "tp"),
            P("tp", None),
            P(),
            P(None, "tp"),
            P("tp"),
            P("tp", None),
            P(),
            P(),
        ),
        check_vma=False,
    )
```

```python
import functools

import jax
import jax.numpy as jnp
from jax import lax
from jax.experimental import pallas as pl
from jax.experimental.pallas import tpu as pltpu
from jax.sharding import PartitionSpec as P

HEAD_DIM = 64
SHORT = 1024
LOG2E = 1.4426950408889634
F32 = jnp.float32
BF16 = jnp.bfloat16
NT = (((1,), (1,)), ((), ()))
TN = (((0,), (0,)), ((), ()))
AXES = ("dp", "tp")
BIG = 1e30
PIECES = 8


def dot(left, right, dims=None):
    if dims is None:
        return jnp.dot(left, right, preferred_element_type=F32)
    return lax.dot_general(left, right, dims, preferred_element_type=F32)


def in_vmem():
    return pl.BlockSpec(memory_space=pltpu.VMEM)


def in_smem():
    return pl.BlockSpec(memory_space=pltpu.SMEM)


def in_place():
    return pl.BlockSpec(memory_space=pl.ANY)


def fill_pack(flags, pack_ref, own_ref, first_ref, second_ref):
    same, side = flags[3] > 0, flags[4] == 0
    size = first_ref.shape[0]
    first, second = first_ref[...], second_ref[...]
    pack_ref[:size] = jnp.where(same, own_ref[:size], jnp.where(side, first, second))
    pack_ref[size:] = jnp.where(same, own_ref[size:], jnp.where(side, second, first))


def lower_half(which, rows):
    zeros = jnp.zeros_like(rows)
    return jnp.where(
        which == 0, jnp.concatenate([rows, zeros], 0), jnp.concatenate([zeros, rows], 0)
    )


def unpacked(pack_ref, which, width):
    rows = pack_ref.shape[1] // 2
    at = slice(which * rows, which * rows + rows)
    return pack_ref[at, :width], pack_ref[at, width : 2 * width]


def attend_kernel(
    flags, mine_ref, other_ref, own_pack_ref, first_ref, second_ref, bias_ref, came_bias_ref,
    q_t_out, k_t_out, k_out, v_out, keep_ref, send_ref, lse_ref,
    v_t, mixed, scores, pack_ref, q_t_ref, k_t_ref, k_ref, v_ref, done, *, block,
):
    core, longs = flags[0], flags[2]
    fill_pack(flags, pack_ref, own_pack_ref, first_ref, second_ref)
    half = mine_ref.shape[0]
    total = 2 * half
    width = pack_ref.shape[1] // 2
    deep = pack_ref.shape[1] // 2
    pairs = width // 128
    heads = width // HEAD_DIM
    turned = [jnp.concatenate([p.T for p in unpacked(pack_ref, i, width)], 1) for i in range(3)]
    bias = jnp.where(flags[3] > 0, bias_ref[...], came_bias_ref[...]).astype(F32)[0:8]
    column = bias.T[:, 0:1]

    def project(rows_ref, which):
        at = pl.ds(pl.multiple_of(which * half, half), half)
        rows = rows_ref[...]
        q_t_ref[:, at] = (dot(turned[0], rows, NT) + column[:width]).astype(BF16)
        k_t_ref[:, at] = dot(turned[1], rows, NT).astype(BF16)
        v_t[:, at] = (dot(turned[2], rows, NT) + column[width:]).astype(BF16)
        for i, target in ((1, k_ref), (2, v_ref)):
            upper, lower = unpacked(pack_ref, i, width)
            for pair in range(pairs):
                cols = slice(pair * 128, pair * 128 + 128)
                part = dot(rows[:, :deep], upper[:, cols]) + dot(rows[:, deep:], lower[:, cols])
                if i == 2:
                    part = part + bias[0:1, width + pair * 128 : width + pair * 128 + 128]
                target[pair, at, :] = part.astype(BF16)

    project(mine_ref, core)
    project(other_ref, 1 - core)
    copies = [
        pltpu.make_async_copy(source, target, done.at[i])
        for i, (source, target) in enumerate(
            ((q_t_ref, q_t_out), (k_t_ref, k_t_out), (k_ref, k_out), (v_ref, v_out))
        )
    ]
    for copy in copies:
        copy.start()
    row = lax.broadcasted_iota(jnp.int32, (block, block), 0)
    col = lax.broadcasted_iota(jnp.int32, (block, block), 1)
    scale = HEAD_DIM ** (-0.5) * LOG2E

    def one_head(head, _):
        at = pl.ds(pl.multiple_of(head * HEAD_DIM, HEAD_DIM), HEAD_DIM)
        pair, which = head // 2, head % 2
        for q0 in range(0, total, block):
            queries = lower_half(which, q_t_ref[at, q0 : q0 + block])
            peak = jnp.full((8, block), -BIG, F32)
            for k0 in range(0, q0 + block, block):
                s = dot(k_ref[pair, k0 : k0 + block, :], queries)
                if k0 == q0:
                    s = jnp.where(row <= col, s, -BIG)
                scores[k0 : k0 + block, :] = s
                top = jnp.max(s.reshape(block // 8, 8, block), 0)
                if q0 >= SHORT > k0:
                    top = jnp.where(longs > 0, top, -BIG)
                peak = jnp.maximum(peak, top)
            peak = jnp.max(peak, 0, keepdims=True) * scale
            acc = jnp.zeros((HEAD_DIM, block), F32)
            norm = jnp.zeros((8, block), F32)
            for k0 in range(0, q0 + block, block):
                base = peak
                if q0 >= SHORT > k0:
                    base = jnp.where(longs > 0, peak, BIG)
                e = jnp.exp2(scores[k0 : k0 + block, :] * scale - base)
                norm = norm + jnp.sum(e.reshape(block // 8, 8, block), 0)
                acc = acc + dot(v_t[at, k0 : k0 + block], e.astype(BF16))
            norm = jnp.sum(norm, 0, keepdims=True)
            mixed[q0 // half, at, q0 % half : q0 % half + block] = (acc / norm).astype(BF16)
            lse_ref[head, :, q0 : q0 + block] = jnp.broadcast_to(
                peak + jnp.log2(norm), (8, block)
            )
        return 0

    lax.fori_loop(0, heads, one_head, 0)
    keep_ref[...] = mixed[core]
    send_ref[...] = mixed[1 - core]
    for copy in copies:
        copy.wait()


def attend(flags, mine, other, own_pack, first, second, bias, came_bias):
    half = mine.shape[0]
    total, width = 2 * half, own_pack.shape[1] // 2
    shape = jax.ShapeDtypeStruct
    block = 512
    return pl.pallas_call(
        functools.partial(attend_kernel, block=block),
        out_shape=(
            shape((width, total), BF16),
            shape((width, total), BF16),
            shape((width // 128, total, 128), BF16),
            shape((width // 128, total, 128), BF16),
            shape((width, half), BF16),
            shape((width, half), BF16),
            shape((width // HEAD_DIM, 8, total), F32),
        ),
        in_specs=[in_smem()] + [in_vmem()] * 7,
        out_specs=(in_place(),) * 4 + (in_vmem(),) * 3,
        scratch_shapes=[
            pltpu.VMEM((width, total), BF16),
            pltpu.VMEM((2, width, half), BF16),
            pltpu.VMEM((total, block), F32),
            pltpu.VMEM(own_pack.shape, BF16),
            pltpu.VMEM((width, total), BF16),
            pltpu.VMEM((width, total), BF16),
            pltpu.VMEM((width // 128, total, 128), BF16),
            pltpu.VMEM((width // 128, total, 128), BF16),
            pltpu.SemaphoreType.DMA((4,)),
        ],
        compiler_params=pltpu.CompilerParams(vmem_limit_bytes=16 << 20),
        cost_estimate=pl.CostEstimate(
            flops=0, bytes_accessed=0, transcendentals=0
        ),
    )(flags, mine, other, own_pack, first, second, bias, came_bias)


def feed_kernel(
    flags, alphas, tok_ref, own_cot_ref, came_cot_ref, keep_ref, recv_ref, wout_ref, bias_ref,
    bup_ref, up_ref, down_ref, near_up, far_up, near_down, far_down,
    out_ref, dresid_ref, dkeep_ref, dsend_ref, gkeep_a_ref, gkeep_b_ref, gsend_a_ref, gsend_b_ref,
    mixed, dmixed, attn, resid, ffn, act, dpre, small, cot_ref,
    *, piece,
):
    core, same = flags[0], flags[3]
    rows, width = tok_ref.shape
    side, deep = flags[4], flags[5]
    main = gkeep_a_ref.shape[2] - 8
    unit = up_ref.shape[1] // 2
    part = wout_ref.shape[0] // 2
    a_attn, a_ffn = alphas[0], alphas[1]
    cot_ref[...] = jnp.where(same > 0, own_cot_ref[...], came_cot_ref[...])
    biases = bias_ref[...].astype(F32)
    own_bup = bup_ref[...].astype(F32)
    mixed[1 - same] = keep_ref[...]
    mixed[same] = recv_ref[...]

    def own_sub(j):
        return core if j == 0 else 1 - core

    def place_of(h, j, piece_at):
        y = 1 - side if (piece_at // 2) % 2 else side
        z = 1 - deep if piece_at % 2 else deep
        if piece_at < PIECES // 2:
            return (gkeep_a_ref, gsend_a_ref)[j].at[h, 2 * y + z]
        return (gkeep_b_ref, gsend_b_ref)[j].at[y, 2 * h + z]

    def put(h, j, start, value):
        value = value.astype(BF16)
        at = 0
        while at < value.shape[0]:
            piece_at, row = divmod(start + at, main)
            size = min(main - row, value.shape[0] - at)
            place_of(h, j, piece_at)[row : row + size, :] = value[at : at + size]
            at += size

    def wout_part(h, j):
        if h == 0:
            return wout_ref[pl.ds(pl.multiple_of(own_sub(j) * part, part), part), :]
        return (near_down, far_down)[j][unit : unit + part, :]

    def mixed_part(h, j):
        return mixed[h, pl.ds(pl.multiple_of(own_sub(j) * part, part), part), :]

    total = dot(mixed_part(0, 0), wout_part(0, 0), TN)
    for h, j in ((0, 1), (1, 0), (1, 1)):
        total = total + dot(mixed_part(h, j), wout_part(h, j), TN)
    attn[...] = total + biases[1:2]
    resid[...] = tok_ref[...].astype(F32) + a_attn * attn[...]
    low = resid[...].astype(BF16)
    low_t = low.T
    dffn = (cot_ref[...].astype(F32) * a_ffn).astype(BF16)
    dffn_t = dffn.T
    dresid_ref[...] = cot_ref[...].astype(F32)
    ffn[...] = jnp.broadcast_to(biases[2:3], ffn.shape)
    for h in range(2):
        for j in range(2):
            sub = pl.ds(pl.multiple_of(own_sub(j) * unit, unit), unit)
            if h == 0:
                up, down = up_ref[:, sub], down_ref[sub, :]
            else:
                source = (near_up, far_up)[j]
                up, down = source[:unit, :], (near_down, far_down)[j][:unit, :]
            if h == 0:
                bias = jnp.where(own_sub(j) == 0, own_bup[1:2], own_bup[2:3])
            else:
                bias = source[unit : unit + 16, :].astype(F32)[0:1]
            bias_grad = jnp.zeros((8, unit), F32)
            for r0 in range(0, rows, piece):
                at = slice(r0, r0 + piece)
                u = dot(low[at], up) + bias
                square = u * u
                t = jnp.tanh(u * (0.7978845608028654 + 0.035677408136300125 * square))
                s = 0.5 + 0.5 * t
                slope = s + (0.5 * u) * (1.0 - t * t) * (
                    0.7978845608028654 + 0.10703222440890037 * square
                )
                act[at, :] = (u * s).astype(BF16)
                d = dot(dffn[at], down, NT) * slope
                d_low = d.astype(BF16)
                dpre[at, :] = d_low
                bias_grad = bias_grad + jnp.sum(
                    d_low.astype(F32).reshape(piece // 8, 8, unit), 0
                )
                ffn[at, :] += dot(act[at, :], down)
                dresid_ref[at, :] += dot(d_low, up, NT)
            put(h, j, 0, dot(low_t, dpre[...]))
            put(h, j, unit, dot(dffn_t, act[...]).T)
            small[2 * h + j, :] = jnp.sum(bias_grad, 0)
    g = cot_ref[...].astype(F32)
    out_ref[...] = (resid[...] + a_ffn * ffn[...]).astype(BF16)
    dresid = dresid_ref[...]
    bias_down = a_ffn * jnp.sum(g, 0, keepdims=True)
    bias_out = a_attn * jnp.sum(dresid, 0, keepdims=True)
    sums = [
        jnp.sum(jnp.sum(v, 0, keepdims=True), 1, keepdims=True)
        for v in (dresid * attn[...], g * ffn[...])
    ]
    lane = lax.broadcasted_iota(jnp.int32, (1, width), 1)
    both = jnp.where(lane == 0, sums[0], jnp.where(lane == 1, sums[1], 0.0))
    dattn = (a_attn * dresid).astype(BF16)
    for h in range(2):
        for j in range(2):
            put(h, j, 2 * unit, dot(mixed_part(h, j), dattn))
            dmixed[h, pl.ds(pl.multiple_of(own_sub(j) * part, part), part), :] = dot(
                wout_part(h, j), dattn, NT
            ).astype(BF16)
            exact = jnp.concatenate(
                [small[2 * h + j : 2 * h + j + 1, :], bias_down, bias_out, both], 0
            )
            high = exact.astype(BF16).astype(F32)
            for i in range(1, PIECES):
                place_of(h, j, i)[main:, :] = jnp.zeros((8, width), BF16)
            place_of(h, j, 0)[main:, :] = jnp.concatenate([high, exact - high], 0).astype(BF16)
    dkeep_ref[...] = dmixed[1 - same]
    dsend_ref[...] = dmixed[same]


def feed(
    flags, alphas, tok, own_cot, came_cot, keep, recv, up, down, wout, near_up, far_up,
    near_down, far_down, bias, bias_up,
):
    rows, width = tok.shape
    unit = up.shape[1] // 2
    half_width = keep.shape[0]
    shape = jax.ShapeDtypeStruct

    piece = shape((2, PIECES // 2, (2 * unit + half_width // 2) // PIECES + 8, width), BF16)
    outs = (
        shape((rows, width), BF16),
        shape((rows, width), F32),
        shape((half_width, rows), BF16),
        shape((half_width, rows), BF16),
        piece,
        piece,
        piece,
        piece,
    )
    values = (tok, own_cot, came_cot, keep, recv, wout, bias, bias_up)
    later = (up, down, near_up, far_up, near_down, far_down)
    return pl.pallas_call(
        functools.partial(feed_kernel, piece=256),
        out_shape=outs,
        in_specs=[in_smem()] * 2
        + [in_vmem()] * (len(values) + len(later)),
        out_specs=(in_vmem(),) * len(outs),
        scratch_shapes=[
            pltpu.VMEM((2, half_width, rows), BF16),
            pltpu.VMEM((2, half_width, rows), BF16),
            pltpu.VMEM((rows, width), F32),
            pltpu.VMEM((rows, width), F32),
            pltpu.VMEM((rows, width), F32),
            pltpu.VMEM((rows, unit), BF16),
            pltpu.VMEM((rows, unit), BF16),
            pltpu.VMEM((8, unit), F32),
            pltpu.VMEM((rows, width), BF16),
        ],
        compiler_params=pltpu.CompilerParams(vmem_limit_bytes=24 << 20),
        cost_estimate=pl.CostEstimate(
            flops=0, bytes_accessed=0, transcendentals=0
        ),
    )(flags, alphas, *values, *later)


def attend_back_kernel(
    flags, mine_in, other_in, q_t_ref, k_t_ref, k_ref, v_ref, keep_ref, send_ref,
    dkeep_ref, drecv_ref, lse_ref, *refs, block, part_of,
):
    sums_ref = None
    if part_of == 2:
        before_ref, first_ref, sums_all, *refs = refs
        sums_all[0] = before_ref[...]
        sums_ref = sums_all.at[1]
    elif part_of == 0:
        sums_ref, *refs = refs
    grads, mixed, dmixed, probs, dscores, mine_ref, other_ref, done = refs
    if part_of == 2:
        grads[:, :HEAD_DIM, :] = first_ref[...]
    core, longs = flags[0], flags[2]
    half = mine_ref.shape[0]
    total = 2 * half
    copies = [
        pltpu.make_async_copy(mine_in, mine_ref, done.at[0]),
        pltpu.make_async_copy(other_in, other_ref, done.at[1]),
    ]
    if part_of != 1:
        for copy in copies:
            copy.start()
    mixed[core] = keep_ref[...]
    mixed[1 - core] = send_ref[...]
    dmixed[core] = dkeep_ref[...]
    dmixed[1 - core] = drecv_ref[...]
    factor = HEAD_DIM ** (-0.5)
    scale = factor * LOG2E
    part = block // 2

    def one_head(which, _):
        at = pl.ds(pl.multiple_of(which * HEAD_DIM, HEAD_DIM), HEAD_DIM)
        for q0 in range(0, total, block):
            here = slice(q0 % half, q0 % half + block)
            do = dmixed[q0 // half, at, here]
            queries = lower_half(which, q_t_ref[at, q0 : q0 + block])
            upstream = lower_half(which, do)
            lse = lse_ref[which, 0:1, q0 : q0 + block]
            mean = jnp.sum(
                do.astype(F32) * mixed[q0 // half, at, here].astype(F32), 0, keepdims=True
            )
            pieces = [(k0, block, 0) for k0 in range(0, q0, block)]
            pieces += [(q0, part, 0), (q0 + part, part, part)]
            for k0, size, skip in pieces:
                keys, cols = slice(k0, k0 + size), slice(q0 + skip, q0 + block)
                base = lse
                if q0 >= SHORT > k0:
                    base = jnp.where(longs > 0, lse, BIG)
                s = dot(k_ref[0, keys, :], queries[:, skip:])
                dp = dot(v_ref[0, keys, :], upstream[:, skip:])
                p = jnp.exp2(s * scale - base[:, skip:])
                if k0 >= q0:
                    row = lax.broadcasted_iota(jnp.int32, p.shape, 0) + k0
                    col = lax.broadcasted_iota(jnp.int32, p.shape, 1) + (q0 + skip)
                    p = jnp.where(row <= col, p, 0.0)
                probs[keys, cols] = p.astype(BF16)
                dscores[keys, cols] = (p * (dp - mean[:, skip:])).astype(BF16)
                if skip:
                    probs[keys, q0 : q0 + skip] = jnp.zeros((size, skip), BF16)
                    dscores[keys, q0 : q0 + skip] = jnp.zeros((size, skip), BF16)
            end = q0 + block
            grads[0, at, q0:end] = (
                dot(k_t_ref[at, 0:end], dscores[0:end, q0:end]) * factor
            ).astype(BF16)
        for k0 in range(0, total, block):
            keys = slice(k0, k0 + block)
            grads[1, at, keys] = (
                dot(q_t_ref[at, k0:], dscores[keys, k0:], NT) * factor
            ).astype(BF16)
            first = k0 // half
            acc = dot(dmixed[first, at, k0 % half :], probs[keys, k0 : (first + 1) * half], NT)
            if first == 0:
                acc = acc + dot(dmixed[1, at, :], probs[keys, half:], NT)
            grads[2, at, keys] = acc.astype(BF16)
        return 0

    lax.fori_loop((0, 0, 1)[part_of], (2, 1, 2)[part_of], one_head, 0)
    if part_of == 1:
        return
    for copy in copies:
        copy.wait()
    near = pl.ds(pl.multiple_of(core * half, half), half)
    far = pl.ds(pl.multiple_of((1 - core) * half, half), half)
    main = sums_ref.shape[1] - 16
    deep = mine_ref.shape[1]
    for i in range(3):
        value = (
            dot(grads[i, :, near], mine_ref[...]) + dot(grads[i, :, far], other_ref[...])
        ).T.astype(BF16)
        at = 0
        while at < deep:
            piece, row = divmod(i * deep + at, main)
            size = min(main - row, deep - at)
            sums_ref[piece, row : row + size, :] = value[at : at + size]
            at += size
    ones = jnp.ones((8, total), BF16)
    rest = jnp.zeros((14, 2 * HEAD_DIM), F32)
    sums_ref[0, main:, :] = jnp.concatenate(
        [dot(ones, grads[0], NT)[0:1], dot(ones, grads[2], NT)[0:1], rest], 0
    ).astype(BF16)
    for piece in range(1, sums_ref.shape[0]):
        sums_ref[piece, main:, :] = jnp.zeros((16, 2 * HEAD_DIM), BF16)


def attend_back(pair, part_of, before, flags, mine, other, q_t, k_t, k, v, keep, send, dkeep, drecv, lse):
    half, width_all = mine.shape
    total = 2 * half
    shape = jax.ShapeDtypeStruct

    def whole(x):
        return pl.BlockSpec(x.shape, lambda i: (0,) * x.ndim)

    def rows_of(x):
        return pl.BlockSpec((2 * HEAD_DIM, x.shape[1]), lambda i: (pair, 0))

    def pair_of(x):
        return pl.BlockSpec((1,) + x.shape[1:], lambda i: (pair, 0, 0))

    sums = (4, 3 * width_all // 4 + 16, 2 * HEAD_DIM)
    outs = (shape((3, 2 * HEAD_DIM, total), BF16),)
    if part_of == 1:
        outs = (shape((3, HEAD_DIM, total), BF16),)
    else:
        outs = (shape((2,) + sums if part_of else sums, BF16),) + outs
    return pl.pallas_call(
        functools.partial(attend_back_kernel, block=512, part_of=part_of),
        grid=(1,),
        out_shape=outs,
        in_specs=[in_smem(), in_place(), in_place(), rows_of(q_t), rows_of(k_t), pair_of(k),
                  pair_of(v), rows_of(keep), rows_of(send), rows_of(dkeep), rows_of(drecv),
                  pl.BlockSpec((2, 8, total), lambda i: (pair, 0, 0))]
        + [whole(x) for x in before],
        out_specs=tuple(whole(x) for x in outs),
        scratch_shapes=[
            pltpu.VMEM((2, 2 * HEAD_DIM, half), BF16),
            pltpu.VMEM((2, 2 * HEAD_DIM, half), BF16),
            pltpu.VMEM((total, total), BF16),
            pltpu.VMEM((total, total), BF16),
            pltpu.VMEM(mine.shape, BF16),
            pltpu.VMEM(mine.shape, BF16),
            pltpu.SemaphoreType.DMA((2,)),
        ],
        compiler_params=pltpu.CompilerParams(vmem_limit_bytes=24 << 20),
        cost_estimate=pl.CostEstimate(
            flops=0, bytes_accessed=0, transcendentals=0
        ),
    )(flags, mine, other, q_t, k_t, k, v, keep, send, dkeep, drecv, lse, *before)


def inputs_back_kernel(flags, own_pack_ref, first_ref, second_ref, dresid_ref, *refs):
    core = flags[0]
    *grads, own_ref, away_ref, pack_ref = refs
    fill_pack(flags, pack_ref, own_pack_ref, first_ref, second_ref)
    half = own_ref.shape[0]
    width = pack_ref.shape[1] // 2

    def back(which):
        at = pl.ds(pl.multiple_of(which * half, half), half)
        result = []
        for part in range(2):
            total = 0.0
            for i in range(3):
                weights = unpacked(pack_ref, i, width)[part]
                stacked = jnp.concatenate([g[i, :, at] for g in grads], 0)
                total = total + dot(weights, stacked)
            result.append(total.T)
        return jnp.concatenate(result, 1)

    away_ref[...] = back(1 - core).astype(BF16)
    own_ref[...] = dresid_ref[...] + back(core)


def inputs_back(flags, own_pack, first, second, dresid, grads):
    half, width_all = dresid.shape
    shape = jax.ShapeDtypeStruct
    return pl.pallas_call(
        inputs_back_kernel,
        out_shape=(shape((half, width_all), F32), shape((half, width_all), BF16)),
        in_specs=[in_smem()] + [in_vmem()] * (4 + len(grads)),
        out_specs=(in_vmem(),) * 2,
        scratch_shapes=[
            pltpu.VMEM(own_pack.shape, BF16),
        ],
        compiler_params=pltpu.CompilerParams(vmem_limit_bytes=10 << 20),
        cost_estimate=pl.CostEstimate(
            flops=0, bytes_accessed=0, transcendentals=0
        ),
    )(flags, own_pack, first, second, dresid, *grads)


def unpack_heads_kernel(flags, mine_ref, came_ref, grad_ref, bias_ref):
    core, side = flags[0], flags[4]
    main = mine_ref.shape[2] - 16
    for far in range(2):
        source = came_ref if far else mine_ref
        for turn in range(2):
            piece = 2 * (1 - core if far else core) + (1 - side if turn else side)
            at = pl.ds(pl.multiple_of(piece * main, main), main)
            for pair in range(source.shape[1]):
                cols = slice(pair * 128, pair * 128 + 128)
                grad_ref[at, cols] = source[turn, pair, :main, :].astype(F32)

            @pl.when(piece == 0)
            def _():
                for pair in range(source.shape[1]):
                    cols = slice(pair * 128, pair * 128 + 128)
                    bias_ref[:, cols] = source[turn, pair, main:, :].astype(F32)[0:2]


def unpack_heads(flags, mine, came, width):
    shape = jax.ShapeDtypeStruct
    main = mine.shape[2] - 16
    return pl.pallas_call(
        unpack_heads_kernel,
        out_shape=(shape((4 * main, width), F32), shape((2, width), F32)),
        in_specs=[in_smem()] + [in_vmem()] * 2,
        out_specs=(in_vmem(),) * 2,
        compiler_params=pltpu.CompilerParams(vmem_limit_bytes=5 << 20),
    )(flags, mine, came)


def unpack_feed_kernel(
    flags, mine_ref, came_ref, up_ref, down_ref, out_ref, bup_ref, bdown_ref, bout_ref,
    alphas_ref, rows_ref, small_ref, *, unit,
):
    core, side, deep = flags[0], flags[4], flags[5]
    main = mine_ref.shape[3] - 8
    for far in range(2):
        source = came_ref if far else mine_ref
        which = 1 - core if far else core
        for turn in range(2):
            for dip in range(2):
                for order in range(2):
                    piece = (
                        4 * order
                        + 2 * (1 - side if turn else side)
                        + (1 - deep if dip else deep)
                    )
                    at = pl.ds(pl.multiple_of(piece * main, 16), main)
                    rows_ref[which, at, :] = source[turn, dip, order, :main, :]
                    if order == 0:

                        @pl.when(piece == 0)
                        def _():
                            both = source[turn, dip, order, main:, :].astype(F32)
                            small_ref[which] = both[0:4] + both[4:8]

    width = small_ref.shape[2]
    for i in range(2):
        bup_ref[i * unit : (i + 1) * unit] = small_ref[i, 0, :]
    bdown_ref[...] = small_ref[0, 1, :]
    bout_ref[...] = small_ref[0, 2, :]
    last = small_ref[0, 3:4, :]
    lane = lax.broadcasted_iota(jnp.int32, (1, width), 1)
    for i in range(2):
        alphas_ref[i] = jnp.sum(jnp.where(lane == i, last, 0.0))
    for i in range(2):
        up_ref[:, i * unit : (i + 1) * unit] = rows_ref[i, :unit, :].astype(F32)
        down_ref[i * unit : (i + 1) * unit, :] = rows_ref[i, unit : 2 * unit, :].astype(F32)
        part = rows_ref.shape[1] - 2 * unit
        out_ref[i * part : (i + 1) * part, :] = rows_ref[i, 2 * unit :, :].astype(F32)


def unpack_feed(flags, mine, came, unit):
    shape = jax.ShapeDtypeStruct
    main, width = mine.shape[3] - 8, mine.shape[4]
    return pl.pallas_call(
        functools.partial(unpack_feed_kernel, unit=unit),
        out_shape=(
            shape((width, 2 * unit), F32),
            shape((2 * unit, width), F32),
            shape((2 * (PIECES * main - 2 * unit), width), F32),
            shape((2 * unit,), F32),
            shape((width,), F32),
            shape((width,), F32),
            shape((2,), F32),
        ),
        in_specs=[in_smem()] + [in_vmem()] * 2,
        out_specs=(in_vmem(),) * 6 + (in_smem(),),
        scratch_shapes=[
            pltpu.VMEM((2, PIECES * main, width), BF16),
            pltpu.VMEM((2, 4, width), F32),
        ],
        compiler_params=pltpu.CompilerParams(vmem_limit_bytes=10 << 20),
    )(flags, mine, came)


def add_low(values):
    total = values[0].astype(F32)
    for value in values[1:]:
        total = total + value.astype(F32)
    return total.astype(BF16)


def take(value, *picks):
    block, index = [], []
    for axis in range(value.ndim - 2):
        what = picks[axis] if axis < len(picks) else None
        if what is None:
            what = (0, value.shape[axis])
        elif isinstance(what, int):
            what = (what, 1)
        block.append(what[1])
        index.append(what[0])
    return value, tuple(block) + value.shape[-2:], tuple(index) + (0, 0)


def sum_kernel(*refs, plan, n_in):
    ins, outs = refs[:n_in], refs[n_in:]

    def terms(total):
        exact = total[0:4] + total[4:8]
        high = exact.astype(BF16).astype(F32)
        return jnp.concatenate([high, exact - high], 0)

    for out, groups in zip(outs, plan):
        at = 0
        main = out.shape[-2] - 8
        for members, alike in groups:
            lead = 1
            for size in ins[members[0]].shape[:-2]:
                lead *= size
            for i in range(lead):
                total, rows = None, None
                for n, member in enumerate(members):
                    ref = ins[member]
                    index, rest = [], i
                    for size in reversed(ref.shape[:-2]):
                        index.insert(0, rest % size)
                        rest //= size
                    value = ref[tuple(index)].astype(F32)
                    top, low = value[:main], value[main:]
                    total = top if total is None else total + top
                    rows = low if rows is None else rows + low
                    if n + 1 == alike:
                        rows = terms(rows).astype(BF16).astype(F32)
                out[at, :main, :] = total.astype(BF16)
                out[at, main:, :] = terms(rows).astype(BF16)
                at += 1


def sum_pieces(*outs):
    blocks, plan, shapes = [], [], []
    for groups in outs:
        lead, steps = 0, []
        for members, alike in groups:
            steps.append((tuple(range(len(blocks), len(blocks) + len(members))), alike))
            blocks.extend(members)
            count = 1
            for size in members[0][1][:-2]:
                count *= size
            lead += count
        plan.append(tuple(steps))
        shapes.append(jax.ShapeDtypeStruct((lead,) + groups[0][0][0][1][-2:], BF16))
    return pl.pallas_call(
        functools.partial(sum_kernel, plan=tuple(plan), n_in=len(blocks)),
        grid=(1,),
        out_shape=tuple(shapes),
        in_specs=[pl.BlockSpec(block, lambda i, at=at: at) for _, block, at in blocks],
        out_specs=tuple(pl.BlockSpec(x.shape, lambda i: (0, 0, 0)) for x in shapes),
        compiler_params=pltpu.CompilerParams(vmem_limit_bytes=5 << 20),
        cost_estimate=pl.CostEstimate(flops=0, bytes_accessed=0, transcendentals=0),
    )(*(value for value, _, _ in blocks))


def pick(value, side, axis):
    size = value.shape[axis] // 2
    return lax.dynamic_slice_in_dim(value, side * size, size, axis)


def paired_local(
    tokens, long_docs, w_qkv, bias_qv, w_out, bias_out, w_up, bias_up, w_down, bias_down, alphas,
    cotangent, *, n_dp,
):
    devices = 2 * n_dp
    place = lax.axis_index("tp")
    row_index = lax.axis_index("dp")
    core = row_index % 2
    same = (core == place).astype(jnp.int32)
    is_same = core == place

    def swapped(i):
        return (i & ~3) | ((i & 1) << 1) | ((i >> 1) & 1)

    def trade(value):
        pairs = [(i, swapped(i)) for i in range(devices) if i != swapped(i)]
        return lax.ppermute(value, AXES, pairs)

    def cross(value, bit):
        return lax.ppermute(value, AXES, [(i, i ^ bit) for i in range(devices)])

    def collect(value):
        return lax.ppermute(
            value, AXES, [(i, i ^ 1) for i in range(devices) if (i & 1) != (i >> 1) & 1]
        )

    PLACE, CORE, NEXT = 1, 2, 4
    side = (row_index // 2) % 2
    outer = []
    bit = 8
    while bit < devices:
        outer.append((bit, (row_index // (bit // 2)) % 2))
        bit *= 2

    width_all, half_qkv = w_qkv.shape[1:]
    unit = w_up.shape[1] // 2
    part = w_out.shape[0] // 2
    tie = lax.optimization_barrier
    longs = jnp.where(is_same, long_docs, cross(long_docs, CORE))[0]
    flags = jnp.stack([core, place, longs, same, side, outer[0][1]]).astype(jnp.int32)
    small = tie(
        jnp.concatenate(
            [bias_qv.reshape(1, -1), bias_out[None], bias_down[None],
             jnp.zeros((13, width_all), BF16)], 0,
        )
    )
    own_pack = jnp.concatenate(
        [w_qkv[:, : width_all // 2], w_qkv[:, width_all // 2 :]], 2
    ).reshape(-1, 2 * half_qkv)
    small_up = tie(
        jnp.concatenate(
            [lax.dynamic_slice_in_dim(bias_up, core * unit, unit, 0)[None],
             bias_up.reshape(2, unit), jnp.zeros((13, unit), BF16)], 0,
        )
    )
    packed_up = jnp.concatenate(
        [lax.dynamic_slice_in_dim(w_up, core * unit, unit, 1), small_up], 0
    )
    packed_down = jnp.concatenate(
        [
            lax.dynamic_slice_in_dim(w_down, core * unit, unit, 0),
            lax.dynamic_slice_in_dim(w_out, core * part, part, 0),
        ],
        0,
    )
    came, first, came_small = trade(tokens), trade(pick(own_pack, side, 0)), trade(small)
    came, first, came_small, packed_up, packed_down, cotangent_tied, flags = tie(
        (came, first, came_small, packed_up, packed_down, cotangent, flags)
    )
    second = lax.ppermute(
        first, AXES, [(i, i ^ NEXT) for i in range(devices) if (i & 1) != (i >> 1) & 1]
    )
    near_up, near_down = cross(packed_up, PLACE), cross(packed_down, PLACE)
    came_cot = trade(cotangent_tied)
    mine = jnp.where(is_same, tokens, came)
    other = cross(mine, CORE)
    q_t, k_t, k, v, keep, send, lse = attend(
        flags, mine, other, own_pack, first, second, small, came_small
    )
    near_up, near_down, send = tie((near_up, near_down, send))
    far_up, far_down = cross(near_up, CORE), cross(near_down, CORE)
    recv = cross(send, CORE)
    out, dresid, dkeep, dsend, keep_a, keep_b, send_a, send_b = feed(
        flags, alphas, mine, cotangent, came_cot, keep, recv, w_up, w_down, w_out, near_up, far_up,
        near_down, far_down, small, small_up,
    )
    drecv = cross(dsend, CORE)
    back_args = (flags, mine, other, q_t, k_t, k, v, keep, send, dkeep, drecv, lse)

    other_a, other_b = cross(send_a, CORE), cross(send_b, CORE)
    give_a, give_b = sum_pieces(
        [([take(keep_a, 1), take(other_a, 1)], 0)], [([take(keep_b, 1), take(other_b, 1)], 0)]
    )
    back_args, give_a, give_b = tie((back_args, give_a, give_b))
    got_a, got_b = cross(give_a, PLACE), cross(give_b, NEXT)
    sums_0, grads_0 = attend_back(0, 0, (), *back_args)
    stay_a, give_a, give_b = sum_pieces(
        *(
            [
                ([take(keep_a, 0, (i, 2)), take(other_a, 0, (i, 2)), take(got_a, (i, 2))], 2)
            ]
            for i in range(2)
        ),
        [([take(keep_b, 0, (1, 2)), take(other_b, 0, (1, 2)), take(got_b, (1, 2))], 0)],
    )
    back_args, give_a, give_b, sums_0 = tie((back_args, give_a, give_b, sums_0))
    got_a, got_b2 = cross(give_a, NEXT), cross(give_b, PLACE)
    (first_grads,) = attend_back(1, 1, (), *back_args)
    stay, give = sum_pieces(
        *(
            [
                ([take(stay_a, i), take(got_a, i)], 0),
                ([take(keep_b, 0, i), take(other_b, 0, i), take(got_b, i), take(got_b2, i)], 0),
            ]
            for i in range(2)
        )
    )
    back_args, give, first_grads = tie((back_args, give, first_grads))
    low_bit, high_bit = outer[0][0], outer[1][0]
    got = cross(give, low_bit)
    sums, grads_1 = attend_back(1, 2, (sums_0, first_grads), *back_args)
    halves = [sum_pieces([([take(stay, i), take(got, i)], 0)])[0] for i in range(2)]
    grads_0, halves, sums = tie((grads_0, halves, sums))
    got_half = cross(halves[0], high_bit)
    got_sums = collect(sums)
    own, away = inputs_back(flags, own_pack, first, second, dresid, (grads_0, grads_1))
    got_half, got_sums, own, away = tie((got_half, got_sums, own, away))

    stay_q, give_q = (
        add_low([pick(p, i, 1) for p in (sums, got_sums)]) for i in (core, 1 - core)
    )
    heads = jnp.where(is_same, stay_q, cross(give_q, CORE))
    grad_tokens = (own + cross(away, CORE).astype(F32)).astype(BF16)
    half, give_q, out, grad_tokens = tie(
        (halves[1], pick(heads, 1 - side, 1), out, grad_tokens)
    )
    got_other = cross(half, high_bit)
    got_q = cross(give_q, NEXT)
    out_came = trade(out)
    tokens_came = trade(grad_tokens)
    heads = add_low([pick(heads, side, 1), got_q])[:, 0]
    (value,) = sum_pieces(
        [([take(halves[0]), take(got_half)], 0), ([take(half), take(got_other)], 0)]
    )
    value, heads = tie((value, heads))
    along, beside = cross(value, low_bit), cross(value, NEXT)
    heads = add_low([heads, cross(heads, low_bit)])
    along, beside, heads = tie((along, beside, heads))
    corner = cross(along, NEXT)
    heads = add_low([heads, cross(heads, high_bit)])
    corner, heads, tokens_came, out_came = tie((corner, heads, tokens_came, out_came))
    value = jnp.stack([jnp.stack([value, along]), jnp.stack([beside, corner])])
    value, heads = tie((value, heads))
    heads_next = cross(heads, NEXT)
    value_came = cross(value, CORE)
    out = jnp.where(is_same, out, out_came)
    grad_tokens = jnp.where(is_same, grad_tokens, tokens_came)
    grad_up, grad_down, grad_out, grad_bias_up, grad_bias_down, grad_bias_out, grad_alphas = (
        unpack_feed(flags, value, value_came, unit)
    )
    heads_next, grad_up, out, grad_tokens = tie((heads_next, grad_up, out, grad_tokens))
    heads = jnp.stack([heads, heads_next])
    grad_w_qkv, grad_bias_qv = unpack_heads(flags, heads, cross(heads, CORE), half_qkv)
    return (
        out, grad_tokens, grad_w_qkv.reshape(3, width_all, half_qkv), grad_bias_qv, grad_out,
        grad_bias_out, grad_up, grad_bias_up, grad_down, grad_bias_down, grad_alphas,
    )


def doc_numbers(total, longs):
    places = jnp.arange(total, dtype=jnp.int32)
    border = 2 * SHORT * longs
    return jnp.where(places < border, places // (2 * SHORT), longs + (places - border) // SHORT)


def contract_rows(left, right):
    return lax.dot_general(
        left, right, (((0,), (0,)), ((), ())), preferred_element_type=jnp.float32
    )


def contract_cols(left, right):
    return lax.dot_general(
        left, right, (((1,), (1,)), ((), ())), preferred_element_type=jnp.float32
    )


def gelu_grad(pre_act, upstream):
    _, pull = jax.vjp(jax.nn.gelu, pre_act)
    return pull(upstream)[0]


def local(
    tokens,
    long_docs,
    w_qkv,
    bias_qv,
    w_out,
    bias_out,
    w_up,
    bias_up,
    w_down,
    bias_down,
    alphas,
    cotangent,
):
    gathered = lax.all_gather(tokens, "tp", axis=0, tiled=True)
    total = gathered.shape[0]
    local_width = w_qkv.shape[2]
    local_heads = local_width // HEAD_DIM
    block = min(512, SHORT)
    window = 2 * SHORT // block
    span = window * block
    blocks_count = total // block
    docs = doc_numbers(total, long_docs[0])
    alpha_attn = alphas[0]
    alpha_ffn = alphas[1]
    scale_value = HEAD_DIM ** (-0.5)
    projected = jnp.einsum("td,cdf->ctf", gathered, w_qkv, preferred_element_type=jnp.float32)
    bias_float = bias_qv.astype(jnp.float32)
    query_all = (
        (projected[0] + bias_float[0]).astype(jnp.bfloat16).reshape(total, local_heads, HEAD_DIM)
    )
    key_all = projected[1].astype(jnp.bfloat16).reshape(total, local_heads, HEAD_DIM)
    value_all = (
        (projected[2] + bias_float[1]).astype(jnp.bfloat16).reshape(total, local_heads, HEAD_DIM)
    )

    def block_pieces(index):
        query_start = index * block
        key_start = jnp.maximum(index - window + 1, 0) * block
        query_rows = lax.dynamic_slice_in_dim(query_all, query_start, block, 0)
        query_docs = lax.dynamic_slice_in_dim(docs, query_start, block, 0)
        query_place = query_start + jnp.arange(block, dtype=jnp.int32)
        key_place = key_start + jnp.arange(span, dtype=jnp.int32)
        allowed = (docs[None, :] == query_docs[:, None]) & (
            key_place[None, :] <= query_place[:, None]
        )
        logits = (
            jnp.einsum("qhe,khe->hqk", query_rows, key_all, preferred_element_type=jnp.float32)
            * scale_value
        )
        logits = jnp.where(allowed[None], logits, -1e30)
        return (query_start, key_start, query_rows, key_all, value_all, logits)

    def forward_block(index):
        _, _, _, _, value_rows, logits = block_pieces(index)
        peak = jnp.max(logits, axis=-1, keepdims=True)
        expo = jnp.exp(logits - peak)
        summed = jnp.sum(expo, axis=-1, keepdims=True)
        probs = (expo / summed).astype(jnp.bfloat16)
        mixed_block = jnp.einsum(
            "hqk,khe->qhe", probs, value_rows, preferred_element_type=jnp.float32
        )
        return (mixed_block.astype(jnp.bfloat16), (peak + jnp.log(summed))[..., 0])

    mixed_blocks, log_totals = lax.map(forward_block, jnp.arange(blocks_count, dtype=jnp.int32))
    mixed = mixed_blocks.reshape(total, local_width)
    attn_full = lax.psum_scatter(
        jnp.dot(mixed, w_out, preferred_element_type=jnp.float32),
        "tp",
        scatter_dimension=0,
        tiled=True,
    ) + bias_out.astype(jnp.float32)
    resid = tokens.astype(jnp.float32) + alpha_attn * attn_full
    resid_low = resid.astype(jnp.bfloat16)
    cot_float = cotangent.astype(jnp.float32)
    ffn_grad_low = (alpha_ffn * cot_float).astype(jnp.bfloat16)
    resid_all = lax.all_gather(resid_low, "tp", axis=0, tiled=True)
    pre_act = jnp.dot(resid_all, w_up, preferred_element_type=jnp.float32) + bias_up.astype(
        jnp.float32
    )
    act_low = jax.nn.gelu(pre_act).astype(jnp.bfloat16)
    ffn_out = lax.psum_scatter(
        jnp.dot(act_low, w_down, preferred_element_type=jnp.float32),
        "tp",
        scatter_dimension=0,
        tiled=True,
    )
    ffn_grad_all = lax.all_gather(ffn_grad_low, "tp", axis=0, tiled=True)
    grad_w_down = contract_rows(act_low, ffn_grad_all)
    grad_pre = gelu_grad(pre_act, contract_cols(ffn_grad_all, w_down)).astype(jnp.bfloat16)
    grad_w_up = contract_rows(resid_all, grad_pre)
    grad_bias_up = jnp.sum(grad_pre.astype(jnp.float32), axis=0)
    grad_resid_ffn = lax.psum_scatter(
        contract_cols(grad_pre, w_up), "tp", scatter_dimension=0, tiled=True
    )
    ffn_full = ffn_out + bias_down.astype(jnp.float32)
    out = (resid + alpha_ffn * ffn_full).astype(jnp.bfloat16)
    grad_alpha_ffn = jnp.sum(cot_float * ffn_full)
    grad_bias_down = alpha_ffn * jnp.sum(cot_float, axis=0)
    grad_resid = cot_float + grad_resid_ffn
    grad_alpha_attn = jnp.sum(grad_resid * attn_full)
    grad_bias_out = alpha_attn * jnp.sum(grad_resid, axis=0)
    attn_grad_low = (alpha_attn * grad_resid).astype(jnp.bfloat16)
    attn_grad_all = lax.all_gather(attn_grad_low, "tp", axis=0, tiled=True)
    grad_w_out = contract_rows(mixed, attn_grad_all)
    grad_mixed = (
        contract_cols(attn_grad_all, w_out)
        .astype(jnp.bfloat16)
        .reshape(total, local_heads, HEAD_DIM)
    )

    def backward_block(carry, index):
        grad_keys, grad_values = carry
        query_start, key_start, query_rows, key_rows, value_rows, logits = block_pieces(index)
        block_totals = lax.dynamic_index_in_dim(log_totals, index, 0, keepdims=False)
        probs = jnp.exp(logits - block_totals[:, :, None])
        upstream = lax.dynamic_slice_in_dim(grad_mixed, query_start, block, 0)
        grad_probs = jnp.einsum(
            "qhe,khe->hqk", upstream, value_rows, preferred_element_type=jnp.float32
        )
        row_terms = jnp.sum(probs * grad_probs, axis=-1, keepdims=True)
        grad_logits = (probs * (grad_probs - row_terms)).astype(jnp.bfloat16)
        grad_query_block = (
            jnp.einsum("hqk,khe->qhe", grad_logits, key_rows, preferred_element_type=jnp.float32)
            * scale_value
        )
        key_part = (
            jnp.einsum("hqk,qhe->khe", grad_logits, query_rows, preferred_element_type=jnp.float32)
            * scale_value
        )
        value_part = jnp.einsum(
            "hqk,qhe->khe", probs.astype(jnp.bfloat16), upstream, preferred_element_type=jnp.float32
        )
        grad_keys = grad_keys + key_part
        grad_values = grad_values + value_part
        return ((grad_keys, grad_values), grad_query_block)

    zero_grads = jnp.zeros((total, local_heads, HEAD_DIM), jnp.float32)
    (grad_keys, grad_values), grad_query_blocks = lax.scan(
        backward_block, (zero_grads, zero_grads), jnp.arange(blocks_count, dtype=jnp.int32)
    )
    grad_proj = jnp.stack(
        [
            grad_query_blocks.reshape(total, local_width),
            grad_keys.reshape(total, local_width),
            grad_values.reshape(total, local_width),
        ]
    ).astype(jnp.bfloat16)
    grad_w_qkv = jnp.einsum("td,ctf->cdf", gathered, grad_proj, preferred_element_type=jnp.float32)
    grad_bias_qv = jnp.stack(
        [
            jnp.sum(grad_proj[0].astype(jnp.float32), axis=0),
            jnp.sum(grad_proj[2].astype(jnp.float32), axis=0),
        ]
    )
    grad_in_attn = lax.psum_scatter(
        jnp.einsum("ctf,cdf->td", grad_proj, w_qkv, preferred_element_type=jnp.float32),
        "tp",
        scatter_dimension=0,
        tiled=True,
    )
    grad_tokens = (grad_resid + grad_in_attn).astype(jnp.bfloat16)
    summed = lax.psum(
        (grad_w_qkv, grad_bias_qv, grad_w_out, grad_w_up, grad_bias_up, grad_w_down), "dp"
    )
    small = lax.psum(
        (grad_bias_out, grad_bias_down, jnp.stack([grad_alpha_attn, grad_alpha_ffn])), ("dp", "tp")
    )
    return (
        out,
        grad_tokens,
        summed[0],
        summed[1],
        summed[2],
        small[0],
        summed[3],
        summed[4],
        summed[5],
        small[1],
        small[2],
    )


def solution(mesh):
    step = local
    if mesh.shape["tp"] == 2 and mesh.shape["dp"] == 16:
        step = functools.partial(paired_local, n_dp=mesh.shape["dp"])
    return jax.shard_map(
        step,
        mesh=mesh,
        in_specs=(
            P(("dp", "tp"), None),
            P("dp"),
            P(None, None, "tp"),
            P(None, "tp"),
            P("tp", None),
            P(),
            P(None, "tp"),
            P("tp"),
            P("tp", None),
            P(),
            P(),
            P(("dp", "tp"), None),
        ),
        out_specs=(
            P(("dp", "tp"), None),
            P(("dp", "tp"), None),
            P(None, None, "tp"),
            P(None, "tp"),
            P("tp", None),
            P(),
            P(None, "tp"),
            P("tp"),
            P("tp", None),
            P(),
            P(),
        ),
        check_vma=False,
    )
```
